32 devices in a mesh: groups: 2 (over y), seq: 4 (over x, core), chan: 4 (over z).
Axes of the slice: x: 2, y: 2, z: 4, core: 2. Of those that a mesh axis runs over, the one named last changes fastest.
Arguments:
- gate_input: bfloat16 [1024, 4096], P(('groups', 'seq'), 'chan'), parts along dimension 0, may hold values from -6 to 6
- value_input: bfloat16 [1024, 4096], P(('groups', 'seq'), 'chan'), parts along dimension 0, may hold values from -6 to 6
- short_filter: float32 [4096, 128], P('chan'), may hold values from -0.5 to 0.5
- long_filter: bfloat16 [512, 4096], P('seq', 'chan'), may hold values from -0.375 to 0.375
- query_weight: bfloat16 [32, 128, 128], P('chan'), may hold values from -0.5 to 0.5
- key_matrix: bfloat16 [1024, 4096], P(('groups', 'seq'), 'chan'), parts along dimension 0, may hold values from -200 to 200
- value_matrix: bfloat16 [1024, 4096], P(('groups', 'seq'), 'chan'), parts along dimension 0, may hold values from -6 to 6
Outputs:
- attended: bfloat16 [1024, 4096], P(('groups', 'seq'), 'chan'), parts along dimension 0
The draws below stay inside these ranges and needn't reach their ends.
There are 2 independent parts, one for each index of `groups`. The reference program is written for one: setup_inputs(seed, part) draws one part's arguments, and reference() takes and returns one part's arrays. A program takes and returns all parts, laid end to end along the dimension named above; an argument that names none is the same for every part. Nothing has to cross between parts.
All inputs are finite; a program needn't handle non-finite values.
Results may differ from the reference program's by a relative error of at most 0.011.
Values may be sent and summed in bfloat16 or wider, within the bound.
No kernel may reach another device: no remote copies, remote signals or barrier semaphores. Data moves between devices by JAX's collectives and lax.ppermute only.
A program may use at most 64 MiB of HBM per device.

```python
import math
import jax
import jax.numpy as jnp
from jax import lax

HEADS = 32
HEAD_DIM = 128
TAPS = 128
DW = 4096
L = 512


def draw_key_matrix(key, part):
    base = jax.random.normal(jax.random.fold_in(key, 11), (L, DW), jnp.float32)
    return jnp.clip(base, -200.0, 200.0).astype(jnp.bfloat16)


def levels(rng, shape, cuts, smallest, largest):
    factor_of, own = 1.0, jax.random.fold_in(rng, 6)
    for position, shards_of in cuts:
        draws = jnp.exp(jax.random.uniform(jax.random.fold_in(own, position), (shards_of,), jnp.float32, smallest / len(cuts), largest / len(cuts)))
        factor_of = factor_of * jnp.repeat(draws, shape[position] // shards_of).reshape([-1 if axis == position else 1 for axis in range(len(shape))])
    return factor_of


def normal_values(rng, extent, deviation, bound, cuts=(), held_as=jnp.bfloat16):
    array = jax.random.normal(rng, extent, jnp.float32) * deviation
    if len(cuts) > 0:
        array = levels(rng, extent, cuts, -0.22, 0.18) * array
    return jnp.clip(array, min=-bound, max=bound).astype(held_as)


def setup_inputs(seed: int = 0, part: int = 0) -> dict:
    seeds = jax.random.split(jax.random.key(seed), 8)
    part_splits = jax.random.split(jax.random.fold_in(seeds[7], part), 8)
    gate_input = normal_values(part_splits[0], (L, DW), 1.0, 6.0, ((0, 4), (1, 4)))
    value_input = normal_values(part_splits[1], (L, DW), 1.0, 6.0, ((0, 4), (1, 4)))
    short_filter = normal_values(seeds[2], (DW, TAPS), TAPS ** -0.5, 0.5, ((0, 4),), jnp.float32)
    long_filter = normal_values(seeds[3], (L, DW), (L // 2) ** -0.5, 0.375, ((0, 4), (1, 4)))
    query_weight = normal_values(seeds[4], (HEADS, HEAD_DIM, HEAD_DIM), HEAD_DIM ** -0.5, 0.5, ((0, 4),))
    key_matrix = draw_key_matrix(jax.random.fold_in(jax.random.fold_in(seeds[7], part), 71), part)
    value_matrix = normal_values(part_splits[6], (L, DW), 1.0, 6.0, ((0, 4), (1, 4)))
    return dict(gate_input=gate_input, value_input=value_input, short_filter=short_filter, long_filter=long_filter, query_weight=query_weight, key_matrix=key_matrix, value_matrix=value_matrix)


def reference(gate_input, value_input, short_filter, long_filter, query_weight, key_matrix, value_matrix):
    width_block = math.gcd(DW, 256)
    block_count = DW // width_block
    gate_blocks = gate_input.reshape(L, block_count, width_block).transpose(1, 0, 2)
    value_blocks = value_input.reshape(L, block_count, width_block).transpose(1, 0, 2)
    filter_blocks = short_filter.reshape(block_count, width_block, TAPS)
    long_blocks = long_filter.reshape(L, block_count, width_block).transpose(1, 0, 2)

    def one_block(quad):
        gate_part, value_part, taps_part, long_part = quad
        padded = jnp.pad(gate_part.astype(jnp.float32), ((TAPS - 1, 0), (0, 0)))
        kernel = taps_part.astype(jnp.float32)[:, ::-1].T[:, None, :]
        smoothed = lax.conv_general_dilated(padded[None], kernel, (1,), 'VALID', dimension_numbers=('NHC', 'HIO', 'NHC'), feature_group_count=width_block, precision=lax.Precision.HIGHEST)[0]
        mixed_input = (smoothed * value_part.astype(jnp.float32)).astype(jnp.bfloat16)
        spec = jnp.fft.rfft(mixed_input.astype(jnp.float32), n=2 * L, axis=0) * jnp.fft.rfft(long_part.astype(jnp.float32), n=2 * L, axis=0)
        return jnp.fft.irfft(spec, n=2 * L, axis=0)[:L].astype(jnp.bfloat16)
    conv_blocks = lax.map(one_block, (gate_blocks, value_blocks, filter_blocks, long_blocks))
    conv_out = conv_blocks.transpose(1, 0, 2).reshape(L, DW)
    conv_heads = conv_out.reshape(L, HEADS, HEAD_DIM).astype(jnp.float32)
    queries = jnp.einsum('thd,hde->the', conv_heads, query_weight.astype(jnp.float32)).astype(jnp.bfloat16)
    query_heads = queries.transpose(1, 0, 2)
    key_heads = key_matrix.reshape(L, HEADS, HEAD_DIM).transpose(1, 0, 2)
    value_heads = value_matrix.reshape(L, HEADS, HEAD_DIM).transpose(1, 0, 2)
    block_rows = math.gcd(L, 1024)

    def one_head(triple):
        head_query, head_key, head_value = triple

        def one_rows(block_pair):
            block_query, block_first = block_pair
            scores = jnp.dot(block_query, head_key.T, preferred_element_type=jnp.float32) / math.sqrt(HEAD_DIM)
            query_pos = block_first + lax.iota(jnp.int32, block_rows)
            key_pos = lax.iota(jnp.int32, L)
            allowed = key_pos[None, :] <= query_pos[:, None]
            row_peak = lax.optimization_barrier(jnp.max(jnp.where(allowed, scores, -1e+30), axis=1, keepdims=True))
            weights = jnp.where(allowed, jnp.exp(scores - row_peak), 0.0)
            weight_sum = lax.optimization_barrier(jnp.sum(weights, axis=1, keepdims=True))
            product = jnp.dot(weights.astype(jnp.bfloat16), head_value, preferred_element_type=jnp.float32)
            return (product / weight_sum).astype(jnp.bfloat16)
        block_firsts = lax.iota(jnp.int32, L // block_rows) * block_rows
        blocks = head_query.reshape(L // block_rows, block_rows, HEAD_DIM)
        return lax.map(one_rows, (blocks, block_firsts)).reshape(L, HEAD_DIM)
    result = lax.map(one_head, (query_heads, key_heads, value_heads))
    return result.transpose(1, 0, 2).reshape(L, DW)
```

```python
import functools
import math

import jax
import jax.numpy as jnp
import ml_dtypes
import numpy as np
from jax import lax
from jax.experimental import pallas as pl
from jax.experimental.pallas import tpu as pltpu
from jax.sharding import PartitionSpec as P

HEAD_DIM = 128
TAPS = 128
RADIX = 128


HIGHEST = lax.Precision.HIGHEST


def shifted(value, axis, steps):
    count = lax.axis_size(axis)
    initial, last = (max(0, -steps), min(count, count - steps))
    return lax.ppermute(value, axis, [(source, source + steps) for source in range(initial, last)])


def unit_table(height, breadth, modulus, orient):
    product = (
        lax.broadcasted_iota(jnp.int32, (height, breadth), 0)
        * lax.broadcasted_iota(jnp.int32, (height, breadth), 1)
        % modulus
    )
    angles = 2.0 * math.pi / modulus * product.astype(jnp.float32)
    return (jnp.cos(angles), orient * jnp.sin(angles))


def block_table(factor, orient):
    inner_re, inner_im = unit_table(factor, factor, factor, orient)
    upper = jnp.concatenate([inner_re, inner_im], axis=1)
    lower = jnp.concatenate([-inner_im, inner_re], axis=1)
    return jnp.concatenate([upper, lower], axis=0)


def spectrum(signal, factor):
    channels, length = signal.shape
    full_length = 2 * length
    column_count = full_length // factor
    folded = signal.reshape(channels, column_count // 2, factor)
    outer_re, outer_im = unit_table(column_count, column_count // 2, column_count, -1.0)
    outer_both = jnp.concatenate([outer_re, outer_im], axis=0)
    first = jnp.einsum("kn,cnm->ckm", outer_both, folded, precision=HIGHEST)
    first_re = first[:, :column_count]
    first_im = first[:, column_count:]
    twist_re, twist_im = unit_table(column_count, factor, full_length, -1.0)
    mid_re = first_re * twist_re - first_im * twist_im
    mid_im = first_re * twist_im + first_im * twist_re
    joined = jnp.concatenate([mid_re, mid_im], axis=2)
    return jnp.einsum("ckn,nm->ckm", joined, block_table(factor, -1.0), precision=HIGHEST)


def inverse(spec_both, factor, length):
    channels = spec_both.shape[0]
    full_length = 2 * length
    column_count = full_length // factor
    mid = jnp.einsum("ckm,mn->ckn", spec_both, block_table(factor, 1.0), precision=HIGHEST)
    mid_re = mid[:, :, :factor]
    mid_im = mid[:, :, factor:]
    twist_re, twist_im = unit_table(column_count, factor, full_length, 1.0)
    turn_re = mid_re * twist_re - mid_im * twist_im
    turn_im = mid_re * twist_im + mid_im * twist_re
    outer_re, outer_im = unit_table(column_count // 2, column_count, column_count, 1.0)
    outer_both = jnp.concatenate([outer_re, -outer_im], axis=1)
    turned = jnp.concatenate([turn_re, turn_im], axis=1)
    result = jnp.einsum("nk,ckm->cnm", outer_both, turned, precision=HIGHEST)
    return result.reshape(channels, length) / full_length


def general_shards(
    gate_input, value_input, short_filter, long_filter, query_weight, key_matrix, value_matrix
):
    seq_rows, local_width = gate_input.shape
    last_rows = gate_input[seq_rows - (TAPS - 1) :]
    earlier = shifted(last_rows, "seq", 1)
    padded = jnp.concatenate([earlier, gate_input], axis=0).astype(jnp.float32)
    kernel = short_filter[:, ::-1].T[:, None, :]
    smoothed = lax.conv_general_dilated(
        padded[None],
        kernel,
        (1,),
        "VALID",
        dimension_numbers=("NHC", "HIO", "NHC"),
        feature_group_count=local_width,
        precision=HIGHEST,
    )[0]
    mixed_input = (smoothed * value_input.astype(jnp.float32)).astype(jnp.bfloat16)
    signal, kernel_line = (
        lax.all_to_all(mixed_input.T, "seq", split_axis=0, concat_axis=1, tiled=True),
        lax.all_to_all(long_filter.T, "seq", split_axis=0, concat_axis=1, tiled=True),
    )
    length = signal.shape[1]
    signal_both = spectrum(signal.astype(jnp.float32), RADIX)
    kernel_both = spectrum(kernel_line.astype(jnp.float32), RADIX)
    signal_re = signal_both[:, :, :RADIX]
    signal_im = signal_both[:, :, RADIX:]
    kernel_re = kernel_both[:, :, :RADIX]
    kernel_im = kernel_both[:, :, RADIX:]
    joint = jnp.concatenate(
        [
            signal_re * kernel_re - signal_im * kernel_im,
            signal_re * kernel_im + signal_im * kernel_re,
        ],
        axis=2,
    )
    conv_line = inverse(joint, RADIX, length).astype(jnp.bfloat16)
    my_index = lax.axis_index("seq")
    group_firsts = [my_index * seq_rows]
    conv_columns = lax.all_to_all(conv_line, "seq", split_axis=1, concat_axis=0, tiled=True)
    heads_here = local_width // HEAD_DIM
    conv_heads = conv_columns.reshape(heads_here, HEAD_DIM, seq_rows)
    query_heads = jnp.einsum(
        "hds,hde->hse", conv_heads, query_weight, preferred_element_type=jnp.float32
    ).astype(jnp.bfloat16)
    group_count = len(group_firsts)
    query_groups = [query_heads]
    key_heads = key_matrix.reshape(seq_rows, heads_here, HEAD_DIM).transpose(1, 0, 2)
    value_heads = value_matrix.reshape(seq_rows, heads_here, HEAD_DIM).transpose(1, 0, 2)
    score_scale = 1.0 / math.sqrt(HEAD_DIM)

    def attend_group(running, group_query, group_first, key_block, value_block, first_row):
        block_rows = key_block.shape[1]

        def compute(current):
            peak_value, weight_sum, weighted = current
            scores = (
                jnp.einsum(
                    "hqd,hkd->hqk", group_query, key_block, preferred_element_type=jnp.float32
                )
                * score_scale
            )
            key_pos = first_row + lax.iota(jnp.int32, block_rows)
            query_pos = group_first + lax.iota(jnp.int32, seq_rows)
            allowed = (key_pos[None, :] <= query_pos[:, None])[None]
            scores = jnp.where(allowed, scores, -1e30)
            new_peak = jnp.maximum(peak_value, jnp.max(scores, axis=2))
            weights = jnp.where(allowed, jnp.exp(scores - new_peak[:, :, None]), 0.0)
            rescale = jnp.exp(peak_value - new_peak)
            weight_sum = weight_sum * rescale + jnp.sum(weights, axis=2)
            weighted = weighted * rescale[:, :, None] + jnp.einsum(
                "hqk,hkd->hqd",
                weights.astype(jnp.bfloat16),
                value_block,
                preferred_element_type=jnp.float32,
            )
            return (new_peak, weight_sum, weighted)

        live = first_row <= group_first + seq_rows - 1
        return lax.cond(live, compute, lambda current: current, running)

    def attend(states, key_block, value_block, first_row):
        return tuple(
            (
                attend_group(
                    states[g], query_groups[g], group_firsts[g], key_block, value_block, first_row
                )
                for g in range(group_count)
            )
        )

    one_state = (
        jnp.full((heads_here, seq_rows), -1e30, jnp.float32),
        jnp.zeros((heads_here, seq_rows), jnp.float32),
        jnp.zeros((heads_here, seq_rows, HEAD_DIM), jnp.float32),
    )
    initial = tuple((one_state for g in range(group_count)))
    running = initial
    key_piece = lax.all_gather(key_heads, "seq", axis=1, tiled=True)
    value_piece = lax.all_gather(value_heads, "seq", axis=1, tiled=True)
    piece_rows = key_piece.shape[1]
    block_rows = 512
    block_count = piece_rows // block_rows
    key_blocks = key_piece.reshape(heads_here, block_count, block_rows, HEAD_DIM).transpose(
        1, 0, 2, 3
    )
    value_blocks = value_piece.reshape(heads_here, block_count, block_rows, HEAD_DIM).transpose(
        1, 0, 2, 3
    )

    def advance(current, element):
        key_block, value_block, position = element
        return (attend(current, key_block, value_block, position * block_rows), None)

    running, _ = lax.scan(
        advance, running, (key_blocks, value_blocks, lax.iota(jnp.int32, block_count))
    )
    outputs = [state[2] / state[1][:, :, None] for state in running]
    result = outputs[0]
    attended_rows = result.transpose(1, 0, 2).reshape(seq_rows, local_width).astype(jnp.bfloat16)
    return attended_rows


def block_tables(block):
    angle = np.pi / block * (np.arange(block) + 0.5)
    window = angle[:, None] * (np.arange(2 * block) - block)[None]
    ahead = np.concatenate([np.cos(window), -np.sin(window)], axis=0)
    inner = np.arange(block)[:, None] * angle[None]
    back = np.concatenate([np.cos(inner), -np.sin(inner)], axis=1) / block

    def pair(table):
        high = table.astype(ml_dtypes.bfloat16)
        rest = (table - high.astype(np.float64)).astype(ml_dtypes.bfloat16)
        return np.concatenate([high, rest], axis=0)

    return pair(ahead), pair(back)


def two_parts(value):
    high = value.astype(jnp.bfloat16)
    return high, (value - high.astype(jnp.float32)).astype(jnp.bfloat16)


def mxu(left, right):
    return jnp.dot(left, right, preferred_element_type=jnp.float32)


def folded_sum(stacked):
    half = stacked.shape[0] // 2
    return stacked[:half] + stacked[half:]


def to_block(back, spec_re, spec_im, block):
    re_high, re_rest = two_parts(spec_re)
    im_high, im_rest = two_parts(spec_im)
    main = mxu(back[:, :block], re_high) + mxu(back[:, block:], im_high)
    small = mxu(back[:block, :block], re_rest) + mxu(back[:block, block:], im_rest)
    return folded_sum(main) + small


def conv_kernel(
    place_ref, gate_ref, value_ref, filter_ref, *rest, count, block, head_dim
):
    arrived = rest[: count - 1]
    taps_ref, weight_ref, ahead_ref, back_ref, query_ref = rest[count - 1 : count + 4]
    gate_all, value_all, filter_all = rest[count + 4 :]
    here = place_ref[0]
    gate_all[0] = jnp.zeros_like(gate_ref)
    filter_all[0] = jnp.zeros_like(filter_ref)
    gate_all[here + 1] = gate_ref[...]
    value_all[here] = value_ref[...]
    filter_all[here + 1] = filter_ref[...]
    for step, piece in enumerate(arrived, 1):
        source = here ^ step
        gate_all[source + 1] = piece[0]
        value_all[source] = piece[1]
        filter_all[source + 1] = piece[2]
    ahead = ahead_ref[...]
    first = ahead[:, block:]
    back = back_ref[...]
    turned = (((1,), (1,)), ((), ()))
    taps_high, taps_rest = two_parts(taps_ref[...])
    taps_spec = folded_sum(
        lax.dot_general(first, taps_high, turned, preferred_element_type=jnp.float32)
    ) + lax.dot_general(
        first[: 2 * block], taps_rest, turned, preferred_element_type=jnp.float32
    )
    taps_re, taps_im = taps_spec[:block], taps_spec[block:]
    lines = []
    kernels = []
    heads = weight_ref.shape[0]
    for b in range(count):
        window = jnp.concatenate([gate_all[b], gate_all[b + 1]], axis=0)
        gate_spec = folded_sum(mxu(ahead, window))
        gate_re, gate_im = gate_spec[:block], gate_spec[block:]
        smoothed = to_block(
            back,
            gate_re * taps_re - gate_im * taps_im,
            gate_re * taps_im + gate_im * taps_re,
            block,
        )
        mixed = (smoothed * value_all[b].astype(jnp.float32)).astype(jnp.bfloat16)
        lines.append(folded_sum(mxu(first, mixed)))
        kernels.append(
            folded_sum(
                mxu(ahead, jnp.concatenate([filter_all[b], filter_all[b + 1]], axis=0))
            )
        )
    for b in range(count):
        total_re, total_im = 0.0, 0.0
        for j in range(b + 1):
            line, kernel = lines[j], kernels[b - j]
            line_re, line_im = line[:block], line[block:]
            kernel_re, kernel_im = kernel[:block], kernel[block:]
            total_re = total_re + (line_re * kernel_re - line_im * kernel_im)
            total_im = total_im + (line_re * kernel_im + line_im * kernel_re)
        conv_out = to_block(back, total_re, total_im, block).astype(jnp.bfloat16)
        for h in range(heads):
            columns = slice(h * head_dim, (h + 1) * head_dim)
            query_ref[b, :, columns] = mxu(conv_out[:, columns], weight_ref[h]).astype(
                jnp.bfloat16
            )


def attend_kernel(place_ref, query_ref, key_ref, value_ref, *rest, count, block, head_dim):
    arrived = rest[: count - 1]
    outs = rest[count - 1 : 2 * count - 1]
    key_all, value_all, out_all = rest[2 * count - 1 :]
    here = place_ref[0]
    key_all[here] = key_ref[...]
    value_all[here] = value_ref[...]
    for step, piece in enumerate(arrived, 1):
        key_all[here ^ step] = piece[0]
        value_all[here ^ step] = piece[1]
    width = query_ref.shape[2]
    turned = (((1,), (1,)), ((), ()))
    scale = 1.0 / math.sqrt(head_dim)
    row = lax.broadcasted_iota(jnp.int32, (block, block), 0)
    column = lax.broadcasted_iota(jnp.int32, (block, block), 1)
    allowed = column <= row
    for h in range(width // head_dim):
        columns = slice(h * head_dim, (h + 1) * head_dim)
        for b in range(count):
            query = query_ref[b, :, columns]
            scores = []
            for j in range(b + 1):
                part = (
                    lax.dot_general(
                        query,
                        key_all[j, :, columns],
                        turned,
                        preferred_element_type=jnp.float32,
                    )
                    * scale
                )
                scores.append(jnp.where(allowed, part, -1e30) if j == b else part)
            peak = functools.reduce(jnp.maximum, scores)
            peak = jnp.max(peak, axis=1, keepdims=True)
            weights = [jnp.exp(part - peak) for part in scores]
            weights[b] = jnp.where(allowed, weights[b], 0.0)
            weight_sum = jnp.sum(functools.reduce(jnp.add, weights), axis=1, keepdims=True)
            total = functools.reduce(
                jnp.add,
                [
                    mxu(weights[j].astype(jnp.bfloat16), value_all[j, :, columns])
                    for j in range(b + 1)
                ],
            )
            out_all[b, :, columns] = (total / weight_sum).astype(jnp.bfloat16)
    for step, out in enumerate(outs):
        out[...] = out_all[here ^ step]


def join_kernel(place_ref, *rest):
    pieces, out_ref = rest[:-1], rest[-1]
    here = place_ref[0]
    width = pieces[0].shape[1]
    for step, piece in enumerate(pieces):
        start = pl.multiple_of((here ^ step) * width, width)
        out_ref[:, pl.ds(start, width)] = piece[...]


WHOLE = pl.BlockSpec(memory_space=pltpu.VMEM)


def head_shards(
    gate_input, value_input, short_filter, long_filter, query_weight, key_matrix, value_matrix
):
    count = lax.axis_size("seq")
    block, local_width = gate_input.shape
    width = local_width // count
    heads = width // HEAD_DIM
    here = lax.axis_index("seq")
    place = here.astype(jnp.int32).reshape(1)

    def columns_of(value, owner):
        return lax.dynamic_slice_in_dim(value, owner * width, width, axis=1)

    def swap(value, step):
        return lax.ppermute(value, "seq", [(i, i ^ step) for i in range(count)])

    def swap_columns(arrays):
        return [
            swap(jnp.stack([columns_of(a, here ^ step) for a in arrays]), step)
            for step in range(1, count)
        ]

    arrived = swap_columns([gate_input, value_input, long_filter])
    arrived_later = swap_columns([key_matrix, value_matrix])
    ahead, back = block_tables(block)
    mine = pl.BlockSpec((block, width), lambda i, p: (0, p[0]))
    scratch = lambda n: pltpu.VMEM((n, block, width), jnp.bfloat16)
    params = pltpu.CompilerParams(vmem_limit_bytes=32 * 1024 * 1024)
    queries = pl.pallas_call(
        functools.partial(conv_kernel, count=count, block=block, head_dim=HEAD_DIM),
        out_shape=jax.ShapeDtypeStruct((count, block, width), jnp.bfloat16),
        grid_spec=pltpu.PrefetchScalarGridSpec(
            num_scalar_prefetch=1,
            grid=(1,),
            in_specs=[mine] * 3
            + [WHOLE] * (count - 1)
            + [
                pl.BlockSpec((width, TAPS), lambda i, p: (p[0], 0)),
                pl.BlockSpec((heads, HEAD_DIM, HEAD_DIM), lambda i, p: (p[0], 0, 0)),
            ]
            + [WHOLE] * 2,
            out_specs=WHOLE,
            scratch_shapes=[scratch(count + 1), scratch(count), scratch(count + 1)],
        ),
        compiler_params=params,
    )(
        place, gate_input, value_input, long_filter, *arrived, short_filter, query_weight,
        jnp.asarray(ahead), jnp.asarray(back),
    )
    pieces = pl.pallas_call(
        functools.partial(attend_kernel, count=count, block=block, head_dim=HEAD_DIM),
        out_shape=[jax.ShapeDtypeStruct((block, width), jnp.bfloat16)] * count,
        grid_spec=pltpu.PrefetchScalarGridSpec(
            num_scalar_prefetch=1,
            grid=(1,),
            in_specs=[WHOLE] + [mine] * 2 + [WHOLE] * (count - 1),
            out_specs=[WHOLE] * count,
            scratch_shapes=[scratch(count)] * 3,
        ),
        compiler_params=params,
    )(place, queries, key_matrix, value_matrix, *arrived_later)
    pieces = [pieces[0]] + [swap(pieces[step], step) for step in range(1, count)]
    return pl.pallas_call(
        join_kernel,
        out_shape=jax.ShapeDtypeStruct((block, local_width), jnp.bfloat16),
        in_specs=[pl.BlockSpec(memory_space=pltpu.SMEM)] + [WHOLE] * count,
        out_specs=WHOLE,
        compiler_params=params,
    )(place, *pieces)


def shards(*arrays):
    count = lax.axis_size("seq")
    block, local_width = arrays[0].shape
    even = local_width % (count * HEAD_DIM) == 0
    if even and count & (count - 1) == 0 and block == TAPS:
        return head_shards(*arrays)
    return general_shards(*arrays)


def solution(mesh):
    in_specs = (
        P(("groups", "seq"), "chan"),
        P(("groups", "seq"), "chan"),
        P("chan", None),
        P("seq", "chan"),
        P("chan", None, None),
        P(("groups", "seq"), "chan"),
        P(("groups", "seq"), "chan"),
    )
    out_specs = P(("groups", "seq"), "chan")
    return jax.shard_map(shards, mesh=mesh, in_specs=in_specs, out_specs=out_specs, check_vma=False)
```

```python
import functools
import math

import jax
import jax.numpy as jnp
import ml_dtypes
import numpy as np
from jax import lax
from jax.experimental import pallas as pl
from jax.experimental.pallas import tpu as pltpu
from jax.sharding import PartitionSpec as P

HEAD_DIM = 128
TAPS = 128
RADIX = 128


HIGHEST = lax.Precision.HIGHEST


def shifted(value, axis, steps):
    count = lax.axis_size(axis)
    initial, last = (max(0, -steps), min(count, count - steps))
    return lax.ppermute(value, axis, [(source, source + steps) for source in range(initial, last)])


def unit_table(height, breadth, modulus, orient):
    product = (
        lax.broadcasted_iota(jnp.int32, (height, breadth), 0)
        * lax.broadcasted_iota(jnp.int32, (height, breadth), 1)
        % modulus
    )
    angles = 2.0 * math.pi / modulus * product.astype(jnp.float32)
    return (jnp.cos(angles), orient * jnp.sin(angles))


def block_table(factor, orient):
    inner_re, inner_im = unit_table(factor, factor, factor, orient)
    upper = jnp.concatenate([inner_re, inner_im], axis=1)
    lower = jnp.concatenate([-inner_im, inner_re], axis=1)
    return jnp.concatenate([upper, lower], axis=0)


def spectrum(signal, factor):
    channels, length = signal.shape
    full_length = 2 * length
    column_count = full_length // factor
    folded = signal.reshape(channels, column_count // 2, factor)
    outer_re, outer_im = unit_table(column_count, column_count // 2, column_count, -1.0)
    outer_both = jnp.concatenate([outer_re, outer_im], axis=0)
    first = jnp.einsum("kn,cnm->ckm", outer_both, folded, precision=HIGHEST)
    first_re = first[:, :column_count]
    first_im = first[:, column_count:]
    twist_re, twist_im = unit_table(column_count, factor, full_length, -1.0)
    mid_re = first_re * twist_re - first_im * twist_im
    mid_im = first_re * twist_im + first_im * twist_re
    joined = jnp.concatenate([mid_re, mid_im], axis=2)
    return jnp.einsum("ckn,nm->ckm", joined, block_table(factor, -1.0), precision=HIGHEST)


def inverse(spec_both, factor, length):
    channels = spec_both.shape[0]
    full_length = 2 * length
    column_count = full_length // factor
    mid = jnp.einsum("ckm,mn->ckn", spec_both, block_table(factor, 1.0), precision=HIGHEST)
    mid_re = mid[:, :, :factor]
    mid_im = mid[:, :, factor:]
    twist_re, twist_im = unit_table(column_count, factor, full_length, 1.0)
    turn_re = mid_re * twist_re - mid_im * twist_im
    turn_im = mid_re * twist_im + mid_im * twist_re
    outer_re, outer_im = unit_table(column_count // 2, column_count, column_count, 1.0)
    outer_both = jnp.concatenate([outer_re, -outer_im], axis=1)
    turned = jnp.concatenate([turn_re, turn_im], axis=1)
    result = jnp.einsum("nk,ckm->cnm", outer_both, turned, precision=HIGHEST)
    return result.reshape(channels, length) / full_length


def general_shards(
    gate_input, value_input, short_filter, long_filter, query_weight, key_matrix, value_matrix
):
    seq_rows, local_width = gate_input.shape
    last_rows = gate_input[seq_rows - (TAPS - 1) :]
    earlier = shifted(last_rows, "seq", 1)
    padded = jnp.concatenate([earlier, gate_input], axis=0).astype(jnp.float32)
    kernel = short_filter[:, ::-1].T[:, None, :]
    smoothed = lax.conv_general_dilated(
        padded[None],
        kernel,
        (1,),
        "VALID",
        dimension_numbers=("NHC", "HIO", "NHC"),
        feature_group_count=local_width,
        precision=HIGHEST,
    )[0]
    mixed_input = (smoothed * value_input.astype(jnp.float32)).astype(jnp.bfloat16)
    signal, kernel_line = (
        lax.all_to_all(mixed_input.T, "seq", split_axis=0, concat_axis=1, tiled=True),
        lax.all_to_all(long_filter.T, "seq", split_axis=0, concat_axis=1, tiled=True),
    )
    length = signal.shape[1]
    signal_both = spectrum(signal.astype(jnp.float32), RADIX)
    kernel_both = spectrum(kernel_line.astype(jnp.float32), RADIX)
    signal_re = signal_both[:, :, :RADIX]
    signal_im = signal_both[:, :, RADIX:]
    kernel_re = kernel_both[:, :, :RADIX]
    kernel_im = kernel_both[:, :, RADIX:]
    joint = jnp.concatenate(
        [
            signal_re * kernel_re - signal_im * kernel_im,
            signal_re * kernel_im + signal_im * kernel_re,
        ],
        axis=2,
    )
    conv_line = inverse(joint, RADIX, length).astype(jnp.bfloat16)
    my_index = lax.axis_index("seq")
    group_firsts = [my_index * seq_rows]
    conv_columns = lax.all_to_all(conv_line, "seq", split_axis=1, concat_axis=0, tiled=True)
    heads_here = local_width // HEAD_DIM
    conv_heads = conv_columns.reshape(heads_here, HEAD_DIM, seq_rows)
    query_heads = jnp.einsum(
        "hds,hde->hse", conv_heads, query_weight, preferred_element_type=jnp.float32
    ).astype(jnp.bfloat16)
    group_count = len(group_firsts)
    query_groups = [query_heads]
    key_heads = key_matrix.reshape(seq_rows, heads_here, HEAD_DIM).transpose(1, 0, 2)
    value_heads = value_matrix.reshape(seq_rows, heads_here, HEAD_DIM).transpose(1, 0, 2)
    score_scale = 1.0 / math.sqrt(HEAD_DIM)

    def attend_group(running, group_query, group_first, key_block, value_block, first_row):
        block_rows = key_block.shape[1]

        def compute(current):
            peak_value, weight_sum, weighted = current
            scores = (
                jnp.einsum(
                    "hqd,hkd->hqk", group_query, key_block, preferred_element_type=jnp.float32
                )
                * score_scale
            )
            key_pos = first_row + lax.iota(jnp.int32, block_rows)
            query_pos = group_first + lax.iota(jnp.int32, seq_rows)
            allowed = (key_pos[None, :] <= query_pos[:, None])[None]
            scores = jnp.where(allowed, scores, -1e30)
            new_peak = jnp.maximum(peak_value, jnp.max(scores, axis=2))
            weights = jnp.where(allowed, jnp.exp(scores - new_peak[:, :, None]), 0.0)
            rescale = jnp.exp(peak_value - new_peak)
            weight_sum = weight_sum * rescale + jnp.sum(weights, axis=2)
            weighted = weighted * rescale[:, :, None] + jnp.einsum(
                "hqk,hkd->hqd",
                weights.astype(jnp.bfloat16),
                value_block,
                preferred_element_type=jnp.float32,
            )
            return (new_peak, weight_sum, weighted)

        live = first_row <= group_first + seq_rows - 1
        return lax.cond(live, compute, lambda current: current, running)

    def attend(states, key_block, value_block, first_row):
        return tuple(
            (
                attend_group(
                    states[g], query_groups[g], group_firsts[g], key_block, value_block, first_row
                )
                for g in range(group_count)
            )
        )

    one_state = (
        jnp.full((heads_here, seq_rows), -1e30, jnp.float32),
        jnp.zeros((heads_here, seq_rows), jnp.float32),
        jnp.zeros((heads_here, seq_rows, HEAD_DIM), jnp.float32),
    )
    initial = tuple((one_state for g in range(group_count)))
    running = initial
    key_piece = lax.all_gather(key_heads, "seq", axis=1, tiled=True)
    value_piece = lax.all_gather(value_heads, "seq", axis=1, tiled=True)
    piece_rows = key_piece.shape[1]
    block_rows = 512
    block_count = piece_rows // block_rows
    key_blocks = key_piece.reshape(heads_here, block_count, block_rows, HEAD_DIM).transpose(
        1, 0, 2, 3
    )
    value_blocks = value_piece.reshape(heads_here, block_count, block_rows, HEAD_DIM).transpose(
        1, 0, 2, 3
    )

    def advance(current, element):
        key_block, value_block, position = element
        return (attend(current, key_block, value_block, position * block_rows), None)

    running, _ = lax.scan(
        advance, running, (key_blocks, value_blocks, lax.iota(jnp.int32, block_count))
    )
    outputs = [state[2] / state[1][:, :, None] for state in running]
    result = outputs[0]
    attended_rows = result.transpose(1, 0, 2).reshape(seq_rows, local_width).astype(jnp.bfloat16)
    return attended_rows


def block_tables(block):
    angle = np.pi / block * (np.arange(block) + 0.5)
    window = angle[:, None] * (np.arange(2 * block) - block)[None]
    ahead = np.concatenate([np.cos(window), -np.sin(window)], axis=0)
    inner = np.arange(block)[:, None] * angle[None]
    back = np.concatenate([np.cos(inner), -np.sin(inner)], axis=1) / block

    def pair(table):
        high = table.astype(ml_dtypes.bfloat16)
        rest = (table - high.astype(np.float64)).astype(ml_dtypes.bfloat16)
        return np.concatenate([high, rest], axis=0)

    return pair(ahead), pair(back)


def two_parts(value):
    high = value.astype(jnp.bfloat16)
    return high, (value - high.astype(jnp.float32)).astype(jnp.bfloat16)


def mxu(left, right):
    return jnp.dot(left, right, preferred_element_type=jnp.float32)


def folded_sum(stacked):
    half = stacked.shape[0] // 2
    return stacked[:half] + stacked[half:]


def to_block(back, spec_re, spec_im, block):
    re_high, re_rest = two_parts(spec_re)
    im_high, im_rest = two_parts(spec_im)
    main = mxu(back[:, :block], re_high) + mxu(back[:, block:], im_high)
    small = mxu(back[:block, :block], re_rest) + mxu(back[:block, block:], im_rest)
    return folded_sum(main) + small


def pack_kernel(place_ref, *rest, steps, width):
    sources, outs, sem = rest[: -len(steps) - 1], rest[-len(steps) - 1 : -1], rest[-1]
    here = place_ref[0]
    copies = []
    for (step, first, last), out in zip(steps, outs):
        columns = pl.ds(pl.multiple_of((here ^ step) * width, width), width)
        for n, source in enumerate(sources[first:last]):
            rows = source.shape[0]
            copies.append(
                pltpu.make_async_copy(
                    source.at[:, columns], out.at[n * rows : (n + 1) * rows], sem.at[len(copies)]
                )
            )
    for copy in copies:
        copy.start()
    for copy in copies:
        copy.wait()


def conv_kernel(
    place_ref, own_ref, near_ref, *rest, count, block, head_dim
):
    arrived = rest[: count - 2]
    taps_ref, weight_ref, ahead_ref, back_ref, query_ref = rest[count - 2 : count + 3]
    gate_all, value_all, filter_all = rest[count + 3 :]
    here = place_ref[0]
    gate_all[0] = jnp.zeros(gate_all.shape[1:], gate_all.dtype)
    filter_all[0] = jnp.zeros(filter_all.shape[1:], filter_all.dtype)
    for step, piece in enumerate((own_ref, near_ref, *arrived)):
        source = here ^ step
        gate_all[source + 1] = piece[:block]
        value_all[source] = piece[block : 2 * block]
        filter_all[source + 1] = piece[2 * block : 3 * block]
    ahead = ahead_ref[...]
    first = ahead[:, block:]
    back = back_ref[...]
    turned = (((1,), (1,)), ((), ()))
    taps_high, taps_rest = two_parts(taps_ref[...])
    taps_spec = folded_sum(
        lax.dot_general(first, taps_high, turned, preferred_element_type=jnp.float32)
    ) + lax.dot_general(
        first[: 2 * block], taps_rest, turned, preferred_element_type=jnp.float32
    )
    taps_re, taps_im = taps_spec[:block], taps_spec[block:]
    lines = []
    kernels = []
    heads = weight_ref.shape[0]
    for b in range(count):
        window = jnp.concatenate([gate_all[b], gate_all[b + 1]], axis=0)
        gate_spec = folded_sum(mxu(ahead, window))
        gate_re, gate_im = gate_spec[:block], gate_spec[block:]
        smoothed = to_block(
            back,
            gate_re * taps_re - gate_im * taps_im,
            gate_re * taps_im + gate_im * taps_re,
            block,
        )
        mixed = (smoothed * value_all[b].astype(jnp.float32)).astype(jnp.bfloat16)
        lines.append(folded_sum(mxu(first, mixed)))
        kernels.append(
            folded_sum(
                mxu(ahead, jnp.concatenate([filter_all[b], filter_all[b + 1]], axis=0))
            )
        )
    for b in range(count):
        total_re, total_im = 0.0, 0.0
        for j in range(b + 1):
            line, kernel = lines[j], kernels[b - j]
            line_re, line_im = line[:block], line[block:]
            kernel_re, kernel_im = kernel[:block], kernel[block:]
            total_re = total_re + (line_re * kernel_re - line_im * kernel_im)
            total_im = total_im + (line_re * kernel_im + line_im * kernel_re)
        conv_out = to_block(back, total_re, total_im, block).astype(jnp.bfloat16)
        for h in range(heads):
            columns = slice(h * head_dim, (h + 1) * head_dim)
            query_ref[b, :, columns] = mxu(conv_out[:, columns], weight_ref[h]).astype(
                jnp.bfloat16
            )


def weigh_kernel(place_ref, query_ref, own_ref, near_ref, *rest, count, block, head_dim):
    arrived = rest[: count - 2]
    weight_ref, part_ref, key_all = rest[count - 2 :]
    here = place_ref[0]
    for step, piece in enumerate((own_ref, near_ref)):
        key_all[here ^ step] = piece[3 * block : 4 * block]
    for step, piece in enumerate(arrived, 2):
        key_all[here ^ step] = piece[...]
    width = query_ref.shape[2]
    turned = (((1,), (1,)), ((), ()))
    scale = 1.0 / math.sqrt(head_dim)
    row = lax.broadcasted_iota(jnp.int32, (block, block), 0)
    column = lax.broadcasted_iota(jnp.int32, (block, block), 1)
    allowed = column <= row
    for h in range(width // head_dim):
        columns = slice(h * head_dim, (h + 1) * head_dim)
        for b in range(count):
            query = query_ref[b, :, columns]
            scores = []
            for j in range(b + 1):
                part = (
                    lax.dot_general(
                        query,
                        key_all[j, :, columns],
                        turned,
                        preferred_element_type=jnp.float32,
                    )
                    * scale
                )
                scores.append(jnp.where(allowed, part, -1e30) if j == b else part)
            peak = functools.reduce(jnp.maximum, scores)
            peak = jnp.max(peak, axis=1, keepdims=True)
            weights = [jnp.exp(part - peak) for part in scores]
            weights[b] = jnp.where(allowed, weights[b], 0.0)
            weight_sum = jnp.sum(functools.reduce(jnp.add, weights), axis=1, keepdims=True)
            part_ref[h, b] = jnp.broadcast_to(1.0 / weight_sum, (block, head_dim))
            for j in range(b + 1):
                weight_ref[h, b, :, j * block : (j + 1) * block] = weights[j].astype(
                    jnp.bfloat16
                )


def sum_kernel(
    place_ref, weight_ref, part_ref, own_ref, near_ref, *rest, count, block, head_dim
):
    arrived = rest[: count - 2]
    outs = rest[count - 2 : 2 * count - 2]
    value_all, out_all = rest[2 * count - 2 :]
    here = place_ref[0]

    def rows_of(b):
        return pl.ds(pl.multiple_of(b * block, block), block)

    for step, piece in enumerate((own_ref, near_ref)):
        value_all[rows_of(here ^ step)] = piece[4 * block : 5 * block]
    for step, piece in enumerate(arrived, 2):
        value_all[rows_of(here ^ step)] = piece[...]
    for h in range(value_all.shape[1] // head_dim):
        columns = slice(h * head_dim, (h + 1) * head_dim)
        for b in range(count):
            seen = (b + 1) * block
            total = mxu(weight_ref[h, b, :, :seen], value_all[:seen, columns])
            out_all[b, :, columns] = (total * part_ref[h, b]).astype(jnp.bfloat16)
    for step, out in enumerate(outs):
        out[...] = out_all[here ^ step]


def join_kernel(place_ref, *rest):
    pieces, out_ref = rest[:-1], rest[-1]
    here = place_ref[0]
    width = pieces[0].shape[1]
    for step, piece in enumerate(pieces):
        start = pl.multiple_of((here ^ step) * width, width)
        out_ref[:, pl.ds(start, width)] = piece[...]


WHOLE = pl.BlockSpec(memory_space=pltpu.VMEM)


def head_shards(
    gate_input, value_input, short_filter, long_filter, query_weight, key_matrix, value_matrix
):
    count = lax.axis_size("seq")
    block, local_width = gate_input.shape
    width = local_width // count
    heads = width // HEAD_DIM
    here = lax.axis_index("seq")
    place = here.astype(jnp.int32).reshape(1)

    def swap(value, step):
        return lax.ppermute(value, "seq", [(i, i ^ step) for i in range(count)])

    def packed(arrays, steps, after=()):
        return pl.pallas_call(
            functools.partial(pack_kernel, steps=steps, width=width),
            out_shape=[
                pltpu.VMEM(((last - first) * block, width), jnp.bfloat16)
                for _, first, last in steps
            ],
            in_specs=[pl.BlockSpec(memory_space=pltpu.SMEM)]
            + [pl.BlockSpec(memory_space=pl.ANY)] * (len(arrays) + len(after)),
            out_specs=[WHOLE] * len(steps),
            scratch_shapes=[
                pltpu.SemaphoreType.DMA((sum(last - first for _, first, last in steps),))
            ],
            compiler_params=params,
        )(place, *[pltpu.with_memory_space_constraint(a, pltpu.HBM) for a in arrays], *after)

    ahead, back = block_tables(block)
    scratch = lambda n: pltpu.VMEM((n, block, width), jnp.bfloat16)
    params = pltpu.CompilerParams(vmem_limit_bytes=32 * 1024 * 1024)
    far = range(2, count)
    streams = [gate_input, value_input, long_filter]
    *first, own, near, k2, k3, v2, v3 = packed(
        streams + [key_matrix, value_matrix],
        [(step, 0, 3) for step in far]
        + [(0, 0, 5), (1, 0, 5)]
        + [(step, 3, 4) for step in far]
        + [(step, 4, 5) for step in far],
    )
    later = [k2, k3, v2, v3]
    arrived = [swap(piece, step) for step, piece in zip(far, first)]
    near = swap(near, 1)
    near, *later = lax.optimization_barrier((near, *later))
    later = [swap(piece, step) for step, piece in zip([*far, *far], later)]
    arrived_keys, arrived_values = later[: len(far)], later[len(far) :]
    queries = pl.pallas_call(
        functools.partial(conv_kernel, count=count, block=block, head_dim=HEAD_DIM),
        out_shape=jax.ShapeDtypeStruct((count, block, width), jnp.bfloat16),
        grid_spec=pltpu.PrefetchScalarGridSpec(
            num_scalar_prefetch=1,
            grid=(1,),
            in_specs=[WHOLE] * count
            + [
                pl.BlockSpec((width, TAPS), lambda i, p: (p[0], 0)),
                pl.BlockSpec((heads, HEAD_DIM, HEAD_DIM), lambda i, p: (p[0], 0, 0)),
            ]
            + [WHOLE] * 2,
            out_specs=WHOLE,
            scratch_shapes=[scratch(count + 1), scratch(count), scratch(count + 1)],
        ),
        compiler_params=params,
    )(place, own, near, *arrived, short_filter, query_weight, jnp.asarray(ahead), jnp.asarray(back))
    weights, parts = pl.pallas_call(
        functools.partial(weigh_kernel, count=count, block=block, head_dim=HEAD_DIM),
        out_shape=[
            jax.ShapeDtypeStruct((heads, count, block, count * block), jnp.bfloat16),
            jax.ShapeDtypeStruct((heads, count, block, HEAD_DIM), jnp.float32),
        ],
        grid_spec=pltpu.PrefetchScalarGridSpec(
            num_scalar_prefetch=1,
            grid=(1,),
            in_specs=[WHOLE] * (count + 1),
            out_specs=[WHOLE] * 2,
            scratch_shapes=[scratch(count)],
        ),
        compiler_params=params,
    )(place, queries, own, near, *arrived_keys)
    pieces = pl.pallas_call(
        functools.partial(sum_kernel, count=count, block=block, head_dim=HEAD_DIM),
        out_shape=[jax.ShapeDtypeStruct((block, width), jnp.bfloat16)] * count,
        grid_spec=pltpu.PrefetchScalarGridSpec(
            num_scalar_prefetch=1,
            grid=(1,),
            in_specs=[WHOLE] * (count + 2),
            out_specs=[WHOLE] * count,
            scratch_shapes=[
                pltpu.VMEM((count * block, width), jnp.bfloat16),
                scratch(count),
            ],
        ),
        compiler_params=params,
    )(place, weights, parts, own, near, *arrived_values)
    swapped = {step: swap(pieces[step], step) for step in [*far, 1]}
    pieces = [pieces[0]] + [swapped[step] for step in range(1, count)]
    return pl.pallas_call(
        join_kernel,
        out_shape=jax.ShapeDtypeStruct((block, local_width), jnp.bfloat16),
        in_specs=[pl.BlockSpec(memory_space=pltpu.SMEM)] + [WHOLE] * count,
        out_specs=WHOLE,
        compiler_params=params,
    )(place, *pieces)


def shards(*arrays):
    count = lax.axis_size("seq")
    block, local_width = arrays[0].shape
    even = local_width % (count * HEAD_DIM) == 0
    if even and count > 1 and count & (count - 1) == 0 and block == TAPS:
        return head_shards(*arrays)
    return general_shards(*arrays)


def solution(mesh):
    in_specs = (
        P(("groups", "seq"), "chan"),
        P(("groups", "seq"), "chan"),
        P("chan", None),
        P("seq", "chan"),
        P("chan", None, None),
        P(("groups", "seq"), "chan"),
        P(("groups", "seq"), "chan"),
    )
    out_specs = P(("groups", "seq"), "chan")
    return jax.shard_map(shards, mesh=mesh, in_specs=in_specs, out_specs=out_specs, check_vma=False)
```

```python
import functools
import math

import jax
import jax.numpy as jnp
import ml_dtypes
import numpy as np
from jax import lax
from jax.experimental import pallas as pl
from jax.experimental.pallas import tpu as pltpu
from jax.sharding import PartitionSpec as P

HEAD_DIM = 128
TAPS = 128
RADIX = 128


HIGHEST = lax.Precision.HIGHEST


def shifted(value, axis, steps):
    count = lax.axis_size(axis)
    initial, last = (max(0, -steps), min(count, count - steps))
    return lax.ppermute(value, axis, [(source, source + steps) for source in range(initial, last)])


def unit_table(height, breadth, modulus, orient):
    product = (
        lax.broadcasted_iota(jnp.int32, (height, breadth), 0)
        * lax.broadcasted_iota(jnp.int32, (height, breadth), 1)
        % modulus
    )
    angles = 2.0 * math.pi / modulus * product.astype(jnp.float32)
    return (jnp.cos(angles), orient * jnp.sin(angles))


def block_table(factor, orient):
    inner_re, inner_im = unit_table(factor, factor, factor, orient)
    upper = jnp.concatenate([inner_re, inner_im], axis=1)
    lower = jnp.concatenate([-inner_im, inner_re], axis=1)
    return jnp.concatenate([upper, lower], axis=0)


def spectrum(signal, factor):
    channels, length = signal.shape
    full_length = 2 * length
    column_count = full_length // factor
    folded = signal.reshape(channels, column_count // 2, factor)
    outer_re, outer_im = unit_table(column_count, column_count // 2, column_count, -1.0)
    outer_both = jnp.concatenate([outer_re, outer_im], axis=0)
    first = jnp.einsum("kn,cnm->ckm", outer_both, folded, precision=HIGHEST)
    first_re = first[:, :column_count]
    first_im = first[:, column_count:]
    twist_re, twist_im = unit_table(column_count, factor, full_length, -1.0)
    mid_re = first_re * twist_re - first_im * twist_im
    mid_im = first_re * twist_im + first_im * twist_re
    joined = jnp.concatenate([mid_re, mid_im], axis=2)
    return jnp.einsum("ckn,nm->ckm", joined, block_table(factor, -1.0), precision=HIGHEST)


def inverse(spec_both, factor, length):
    channels = spec_both.shape[0]
    full_length = 2 * length
    column_count = full_length // factor
    mid = jnp.einsum("ckm,mn->ckn", spec_both, block_table(factor, 1.0), precision=HIGHEST)
    mid_re = mid[:, :, :factor]
    mid_im = mid[:, :, factor:]
    twist_re, twist_im = unit_table(column_count, factor, full_length, 1.0)
    turn_re = mid_re * twist_re - mid_im * twist_im
    turn_im = mid_re * twist_im + mid_im * twist_re
    outer_re, outer_im = unit_table(column_count // 2, column_count, column_count, 1.0)
    outer_both = jnp.concatenate([outer_re, -outer_im], axis=1)
    turned = jnp.concatenate([turn_re, turn_im], axis=1)
    result = jnp.einsum("nk,ckm->cnm", outer_both, turned, precision=HIGHEST)
    return result.reshape(channels, length) / full_length


def general_shards(
    gate_input, value_input, short_filter, long_filter, query_weight, key_matrix, value_matrix
):
    seq_rows, local_width = gate_input.shape
    last_rows = gate_input[seq_rows - (TAPS - 1) :]
    earlier = shifted(last_rows, "seq", 1)
    padded = jnp.concatenate([earlier, gate_input], axis=0).astype(jnp.float32)
    kernel = short_filter[:, ::-1].T[:, None, :]
    smoothed = lax.conv_general_dilated(
        padded[None],
        kernel,
        (1,),
        "VALID",
        dimension_numbers=("NHC", "HIO", "NHC"),
        feature_group_count=local_width,
        precision=HIGHEST,
    )[0]
    mixed_input = (smoothed * value_input.astype(jnp.float32)).astype(jnp.bfloat16)
    signal, kernel_line = (
        lax.all_to_all(mixed_input.T, "seq", split_axis=0, concat_axis=1, tiled=True),
        lax.all_to_all(long_filter.T, "seq", split_axis=0, concat_axis=1, tiled=True),
    )
    length = signal.shape[1]
    signal_both = spectrum(signal.astype(jnp.float32), RADIX)
    kernel_both = spectrum(kernel_line.astype(jnp.float32), RADIX)
    signal_re = signal_both[:, :, :RADIX]
    signal_im = signal_both[:, :, RADIX:]
    kernel_re = kernel_both[:, :, :RADIX]
    kernel_im = kernel_both[:, :, RADIX:]
    joint = jnp.concatenate(
        [
            signal_re * kernel_re - signal_im * kernel_im,
            signal_re * kernel_im + signal_im * kernel_re,
        ],
        axis=2,
    )
    conv_line = inverse(joint, RADIX, length).astype(jnp.bfloat16)
    my_index = lax.axis_index("seq")
    group_firsts = [my_index * seq_rows]
    conv_columns = lax.all_to_all(conv_line, "seq", split_axis=1, concat_axis=0, tiled=True)
    heads_here = local_width // HEAD_DIM
    conv_heads = conv_columns.reshape(heads_here, HEAD_DIM, seq_rows)
    query_heads = jnp.einsum(
        "hds,hde->hse", conv_heads, query_weight, preferred_element_type=jnp.float32
    ).astype(jnp.bfloat16)
    group_count = len(group_firsts)
    query_groups = [query_heads]
    key_heads = key_matrix.reshape(seq_rows, heads_here, HEAD_DIM).transpose(1, 0, 2)
    value_heads = value_matrix.reshape(seq_rows, heads_here, HEAD_DIM).transpose(1, 0, 2)
    score_scale = 1.0 / math.sqrt(HEAD_DIM)

    def attend_group(running, group_query, group_first, key_block, value_block, first_row):
        block_rows = key_block.shape[1]

        def compute(current):
            peak_value, weight_sum, weighted = current
            scores = (
                jnp.einsum(
                    "hqd,hkd->hqk", group_query, key_block, preferred_element_type=jnp.float32
                )
                * score_scale
            )
            key_pos = first_row + lax.iota(jnp.int32, block_rows)
            query_pos = group_first + lax.iota(jnp.int32, seq_rows)
            allowed = (key_pos[None, :] <= query_pos[:, None])[None]
            scores = jnp.where(allowed, scores, -1e30)
            new_peak = jnp.maximum(peak_value, jnp.max(scores, axis=2))
            weights = jnp.where(allowed, jnp.exp(scores - new_peak[:, :, None]), 0.0)
            rescale = jnp.exp(peak_value - new_peak)
            weight_sum = weight_sum * rescale + jnp.sum(weights, axis=2)
            weighted = weighted * rescale[:, :, None] + jnp.einsum(
                "hqk,hkd->hqd",
                weights.astype(jnp.bfloat16),
                value_block,
                preferred_element_type=jnp.float32,
            )
            return (new_peak, weight_sum, weighted)

        live = first_row <= group_first + seq_rows - 1
        return lax.cond(live, compute, lambda current: current, running)

    def attend(states, key_block, value_block, first_row):
        return tuple(
            (
                attend_group(
                    states[g], query_groups[g], group_firsts[g], key_block, value_block, first_row
                )
                for g in range(group_count)
            )
        )

    one_state = (
        jnp.full((heads_here, seq_rows), -1e30, jnp.float32),
        jnp.zeros((heads_here, seq_rows), jnp.float32),
        jnp.zeros((heads_here, seq_rows, HEAD_DIM), jnp.float32),
    )
    initial = tuple((one_state for g in range(group_count)))
    running = initial
    key_piece = lax.all_gather(key_heads, "seq", axis=1, tiled=True)
    value_piece = lax.all_gather(value_heads, "seq", axis=1, tiled=True)
    piece_rows = key_piece.shape[1]
    block_rows = 512
    block_count = piece_rows // block_rows
    key_blocks = key_piece.reshape(heads_here, block_count, block_rows, HEAD_DIM).transpose(
        1, 0, 2, 3
    )
    value_blocks = value_piece.reshape(heads_here, block_count, block_rows, HEAD_DIM).transpose(
        1, 0, 2, 3
    )

    def advance(current, element):
        key_block, value_block, position = element
        return (attend(current, key_block, value_block, position * block_rows), None)

    running, _ = lax.scan(
        advance, running, (key_blocks, value_blocks, lax.iota(jnp.int32, block_count))
    )
    outputs = [state[2] / state[1][:, :, None] for state in running]
    result = outputs[0]
    attended_rows = result.transpose(1, 0, 2).reshape(seq_rows, local_width).astype(jnp.bfloat16)
    return attended_rows


def block_tables(block):
    angle = np.pi / block * (np.arange(block) + 0.5)
    window = angle[:, None] * (np.arange(2 * block) - block)[None]
    ahead = np.concatenate([np.cos(window), -np.sin(window)], axis=0)
    inner = np.arange(block)[:, None] * angle[None]
    back = np.concatenate([np.cos(inner), -np.sin(inner)], axis=1) / block

    def pair(table):
        high = table.astype(ml_dtypes.bfloat16)
        rest = (table - high.astype(np.float64)).astype(ml_dtypes.bfloat16)
        return np.concatenate([high, rest], axis=0)

    return pair(ahead), pair(back)


def two_parts(value):
    high = value.astype(jnp.bfloat16)
    return high, (value - high.astype(jnp.float32)).astype(jnp.bfloat16)


def mxu(left, right):
    return jnp.dot(left, right, preferred_element_type=jnp.float32)


def folded_sum(stacked):
    half = stacked.shape[0] // 2
    return stacked[:half] + stacked[half:]


def wide_mxu(table, value):
    half = table.shape[0] // 2
    wide = jnp.concatenate([table[:half], table[half:]], axis=1)
    return mxu(wide, jnp.concatenate([value, value], axis=0))


def to_block(back, spec_re, spec_im, block):
    high, rest = two_parts(jnp.concatenate([spec_re, spec_im], axis=0))
    return folded_sum(mxu(back, high)) + mxu(back[:block], rest)


def pack_kernel(place_ref, *rest, parts, width):
    outs, sem = rest[-len(parts) - 1 : -1], rest[-1]
    here = place_ref[0]
    copies = []
    for (step, first, last), out in zip(parts, outs):
        columns = pl.ds(pl.multiple_of((here ^ step) * width, width), width)
        for n, source in enumerate(rest[first:last]):
            rows = source.shape[0]
            copies.append(
                pltpu.make_async_copy(
                    source.at[:, columns], out.at[n * rows : (n + 1) * rows], sem.at[len(copies)]
                )
            )
    for copy in copies:
        copy.start()
    for copy in copies:
        copy.wait()


def conv_kernel(
    place_ref, own_ref, near_ref, *rest, count, block, head_dim
):
    arrived = rest[: count - 2]
    taps_ref, weight_ref, ahead_ref, back_ref, query_ref = rest[count - 2 : count + 3]
    gate_all, value_all, filter_all = rest[count + 3 :]
    here = place_ref[0]
    gate_all[0] = jnp.zeros(gate_all.shape[1:], gate_all.dtype)
    filter_all[0] = jnp.zeros(filter_all.shape[1:], filter_all.dtype)
    for step, piece in enumerate((own_ref, near_ref, *arrived)):
        source = here ^ step
        gate_all[source + 1] = piece[:block]
        value_all[source] = piece[block : 2 * block]
        filter_all[source + 1] = piece[2 * block : 3 * block]
    ahead = ahead_ref[...]
    first = ahead[:, block:]
    back = back_ref[...]
    turned = (((1,), (1,)), ((), ()))
    width = own_ref.shape[1]
    heads = width // head_dim
    taps = taps_ref[pl.ds(pl.multiple_of(here * width, width), width)]
    taps_high, taps_rest = two_parts(taps)
    taps_spec = folded_sum(
        lax.dot_general(first, taps_high, turned, preferred_element_type=jnp.float32)
    ) + lax.dot_general(
        first[: 2 * block], taps_rest, turned, preferred_element_type=jnp.float32
    )
    taps_re, taps_im = taps_spec[:block], taps_spec[block:]
    lines = []
    kernels = []
    for b in range(count):
        window = jnp.concatenate([gate_all[b], gate_all[b + 1]], axis=0)
        gate_spec = wide_mxu(ahead, window)
        gate_re, gate_im = gate_spec[:block], gate_spec[block:]
        smoothed = to_block(
            back,
            gate_re * taps_re - gate_im * taps_im,
            gate_re * taps_im + gate_im * taps_re,
            block,
        )
        mixed = (smoothed * value_all[b].astype(jnp.float32)).astype(jnp.bfloat16)
        lines.append(wide_mxu(first, mixed))
        kernels.append(
            wide_mxu(ahead, jnp.concatenate([filter_all[b], filter_all[b + 1]], axis=0))
        )
    for b in range(count):
        total_re, total_im = 0.0, 0.0
        for j in range(b + 1):
            line, kernel = lines[j], kernels[b - j]
            line_re, line_im = line[:block], line[block:]
            kernel_re, kernel_im = kernel[:block], kernel[block:]
            total_re = total_re + (line_re * kernel_re - line_im * kernel_im)
            total_im = total_im + (line_re * kernel_im + line_im * kernel_re)
        conv_out = to_block(back, total_re, total_im, block).astype(jnp.bfloat16)
        for h in range(heads):
            columns = slice(h * head_dim, (h + 1) * head_dim)
            query_ref[b, :, columns] = mxu(conv_out[:, columns], weight_ref[here * heads + h]).astype(
                jnp.bfloat16
            )


def weigh_kernel(place_ref, query_ref, own_ref, near_ref, *rest, count, block, head_dim):
    arrived = rest[: count - 2]
    weight_ref, part_ref, key_all = rest[count - 2 :]
    here = place_ref[0]
    for step, piece in enumerate((own_ref, near_ref, *arrived)):
        key_all[here ^ step] = piece[:block]
    width = query_ref.shape[2]
    turned = (((1,), (1,)), ((), ()))
    scale = 1.0 / math.sqrt(head_dim)
    row = lax.broadcasted_iota(jnp.int32, (block, block), 0)
    column = lax.broadcasted_iota(jnp.int32, (block, block), 1)
    allowed = column <= row
    for h in range(width // head_dim):
        columns = slice(h * head_dim, (h + 1) * head_dim)
        for b in range(count):
            query = query_ref[b, :, columns]
            scores = []
            for j in range(b + 1):
                part = (
                    lax.dot_general(
                        query,
                        key_all[j, :, columns],
                        turned,
                        preferred_element_type=jnp.float32,
                    )
                    * scale
                )
                scores.append(jnp.where(allowed, part, -1e30) if j == b else part)
            peak = functools.reduce(jnp.maximum, scores)
            peak = jnp.max(peak, axis=1, keepdims=True)
            weights = [jnp.exp(part - peak) for part in scores]
            weights[b] = jnp.where(allowed, weights[b], 0.0)
            weight_sum = jnp.sum(functools.reduce(jnp.add, weights), axis=1, keepdims=True)
            part_ref[h, b] = jnp.broadcast_to(1.0 / weight_sum, (block, head_dim))
            for j in range(b + 1):
                weight_ref[h, b, :, j * block : (j + 1) * block] = weights[j].astype(
                    jnp.bfloat16
                )


def sum_kernel(
    place_ref, weight_ref, part_ref, own_ref, near_ref, *rest, count, block, head_dim
):
    arrived = rest[: count - 2]
    outs = rest[count - 2 : 2 * count - 2]
    value_all, out_all = rest[2 * count - 2 :]
    here = place_ref[0]

    def rows_of(b):
        return pl.ds(pl.multiple_of(b * block, block), block)

    for step, piece in enumerate((own_ref, near_ref, *arrived)):
        value_all[rows_of(here ^ step)] = piece[-block:]
    for h in range(value_all.shape[1] // head_dim):
        columns = slice(h * head_dim, (h + 1) * head_dim)
        for b in range(count):
            seen = (b + 1) * block
            total = mxu(weight_ref[h, b, :, :seen], value_all[:seen, columns])
            out_all[b, :, columns] = (total * part_ref[h, b]).astype(jnp.bfloat16)
    for step, out in enumerate(outs):
        out[...] = out_all[here ^ step]


def join_kernel(place_ref, *rest):
    pieces, out_ref = rest[:-1], rest[-1]
    here = place_ref[0]
    width = pieces[0].shape[1]
    for step, piece in enumerate(pieces):
        start = pl.multiple_of((here ^ step) * width, width)
        out_ref[:, pl.ds(start, width)] = piece[...]


WHOLE = pl.BlockSpec(memory_space=pltpu.VMEM)


def head_shards(
    gate_input, value_input, short_filter, long_filter, query_weight, key_matrix, value_matrix
):
    count = lax.axis_size("seq")
    block, local_width = gate_input.shape
    width = local_width // count
    heads = width // HEAD_DIM
    here = lax.axis_index("seq")
    place = here.astype(jnp.int32).reshape(1)

    def swap(value, step):
        return lax.ppermute(value, "seq", [(i, i ^ step) for i in range(count)])

    def packed(arrays, parts, after=()):
        return pl.pallas_call(
            functools.partial(pack_kernel, parts=parts, width=width),
            out_shape=[
                pltpu.VMEM(((last - first) * block, width), jnp.bfloat16)
                for _, first, last in parts
            ],
            in_specs=[pl.BlockSpec(memory_space=pltpu.SMEM)]
            + [pl.BlockSpec(memory_space=pl.ANY)] * (len(arrays) + len(after)),
            out_specs=[WHOLE] * len(parts),
            scratch_shapes=[
                pltpu.SemaphoreType.DMA((sum(last - first for _, first, last in parts),))
            ],
            compiler_params=params,
        )(place, *[pltpu.with_memory_space_constraint(a, pltpu.HBM) for a in arrays], *after)

    ahead, back = block_tables(block)
    scratch = lambda n: pltpu.VMEM((n, block, width), jnp.bfloat16)
    params = pltpu.CompilerParams(vmem_limit_bytes=32 * 1024 * 1024)
    far = range(2, count)
    streams = [gate_input, value_input, long_filter]
    first, near = packed(streams, [(far[0], 0, 3), (1, 0, 3)])
    near = swap(near, 1)
    own, *others = packed(
        [*streams, key_matrix, value_matrix],
        [(0, 0, 3)]
        + [(step, 0, 3) for step in far[1:]]
        + [(0, 3, 5), (1, 3, 5)]
        + [(step, n, n + 1) for n in (3, 4) for step in far],
        after=[near],
    )
    arrived = [swap(piece, step) for step, piece in zip(far, [first, *others])]
    own_later, near_later, *later = others[len(far) - 1 :]
    near_later = swap(near_later, 1)
    near_later, *later = lax.optimization_barrier((near_later, *later))
    later = [swap(piece, step) for step, piece in zip([*far, *far], later)]
    arrived_keys, arrived_values = later[: len(far)], later[len(far) :]
    queries = pl.pallas_call(
        functools.partial(conv_kernel, count=count, block=block, head_dim=HEAD_DIM),
        out_shape=jax.ShapeDtypeStruct((count, block, width), jnp.bfloat16),
        grid_spec=pltpu.PrefetchScalarGridSpec(
            num_scalar_prefetch=1,
            grid=(1,),
            in_specs=[WHOLE] * count
            + [WHOLE] * 4,
            out_specs=WHOLE,
            scratch_shapes=[scratch(count + 1), scratch(count), scratch(count + 1)],
        ),
        compiler_params=params,
    )(place, own, near, *arrived, short_filter, query_weight, jnp.asarray(ahead), jnp.asarray(back))
    weights, parts = pl.pallas_call(
        functools.partial(weigh_kernel, count=count, block=block, head_dim=HEAD_DIM),
        out_shape=[
            jax.ShapeDtypeStruct((heads, count, block, count * block), jnp.bfloat16),
            jax.ShapeDtypeStruct((heads, count, block, HEAD_DIM), jnp.float32),
        ],
        grid_spec=pltpu.PrefetchScalarGridSpec(
            num_scalar_prefetch=1,
            grid=(1,),
            in_specs=[WHOLE] * (count + 1),
            out_specs=[WHOLE] * 2,
            scratch_shapes=[scratch(count)],
        ),
        compiler_params=params,
    )(place, queries, own_later, near_later, *arrived_keys)
    pieces = pl.pallas_call(
        functools.partial(sum_kernel, count=count, block=block, head_dim=HEAD_DIM),
        out_shape=[jax.ShapeDtypeStruct((block, width), jnp.bfloat16)] * count,
        grid_spec=pltpu.PrefetchScalarGridSpec(
            num_scalar_prefetch=1,
            grid=(1,),
            in_specs=[WHOLE] * (count + 2),
            out_specs=[WHOLE] * count,
            scratch_shapes=[
                pltpu.VMEM((count * block, width), jnp.bfloat16),
                scratch(count),
            ],
        ),
        compiler_params=params,
    )(place, weights, parts, own_later, near_later, *arrived_values)
    swapped = {step: swap(pieces[step], step) for step in [*far, 1]}
    pieces = [pieces[0]] + [swapped[step] for step in range(1, count)]
    return pl.pallas_call(
        join_kernel,
        out_shape=jax.ShapeDtypeStruct((block, local_width), jnp.bfloat16),
        in_specs=[pl.BlockSpec(memory_space=pltpu.SMEM)] + [WHOLE] * count,
        out_specs=WHOLE,
        compiler_params=params,
    )(place, *pieces)


def shards(*arrays):
    count = lax.axis_size("seq")
    block, local_width = arrays[0].shape
    even = local_width % (count * HEAD_DIM) == 0
    if even and count > 1 and count & (count - 1) == 0 and block == TAPS:
        return head_shards(*arrays)
    return general_shards(*arrays)


def solution(mesh):
    in_specs = (
        P(("groups", "seq"), "chan"),
        P(("groups", "seq"), "chan"),
        P("chan", None),
        P("seq", "chan"),
        P("chan", None, None),
        P(("groups", "seq"), "chan"),
        P(("groups", "seq"), "chan"),
    )
    out_specs = P(("groups", "seq"), "chan")
    return jax.shard_map(shards, mesh=mesh, in_specs=in_specs, out_specs=out_specs, check_vma=False)
```

```python
import functools
import math

import jax
import jax.numpy as jnp
import ml_dtypes
import numpy as np
from jax import lax
from jax.experimental import pallas as pl
from jax.experimental.pallas import tpu as pltpu
from jax.sharding import PartitionSpec as P

HEAD_DIM = 128
TAPS = 128
RADIX = 128


HIGHEST = lax.Precision.HIGHEST


def shifted(value, axis, steps):
    count = lax.axis_size(axis)
    initial, last = (max(0, -steps), min(count, count - steps))
    return lax.ppermute(value, axis, [(source, source + steps) for source in range(initial, last)])


def unit_table(height, breadth, modulus, orient):
    product = (
        lax.broadcasted_iota(jnp.int32, (height, breadth), 0)
        * lax.broadcasted_iota(jnp.int32, (height, breadth), 1)
        % modulus
    )
    angles = 2.0 * math.pi / modulus * product.astype(jnp.float32)
    return (jnp.cos(angles), orient * jnp.sin(angles))


def block_table(factor, orient):
    inner_re, inner_im = unit_table(factor, factor, factor, orient)
    upper = jnp.concatenate([inner_re, inner_im], axis=1)
    lower = jnp.concatenate([-inner_im, inner_re], axis=1)
    return jnp.concatenate([upper, lower], axis=0)


def spectrum(signal, factor):
    channels, length = signal.shape
    full_length = 2 * length
    column_count = full_length // factor
    folded = signal.reshape(channels, column_count // 2, factor)
    outer_re, outer_im = unit_table(column_count, column_count // 2, column_count, -1.0)
    outer_both = jnp.concatenate([outer_re, outer_im], axis=0)
    first = jnp.einsum("kn,cnm->ckm", outer_both, folded, precision=HIGHEST)
    first_re = first[:, :column_count]
    first_im = first[:, column_count:]
    twist_re, twist_im = unit_table(column_count, factor, full_length, -1.0)
    mid_re = first_re * twist_re - first_im * twist_im
    mid_im = first_re * twist_im + first_im * twist_re
    joined = jnp.concatenate([mid_re, mid_im], axis=2)
    return jnp.einsum("ckn,nm->ckm", joined, block_table(factor, -1.0), precision=HIGHEST)


def inverse(spec_both, factor, length):
    channels = spec_both.shape[0]
    full_length = 2 * length
    column_count = full_length // factor
    mid = jnp.einsum("ckm,mn->ckn", spec_both, block_table(factor, 1.0), precision=HIGHEST)
    mid_re = mid[:, :, :factor]
    mid_im = mid[:, :, factor:]
    twist_re, twist_im = unit_table(column_count, factor, full_length, 1.0)
    turn_re = mid_re * twist_re - mid_im * twist_im
    turn_im = mid_re * twist_im + mid_im * twist_re
    outer_re, outer_im = unit_table(column_count // 2, column_count, column_count, 1.0)
    outer_both = jnp.concatenate([outer_re, -outer_im], axis=1)
    turned = jnp.concatenate([turn_re, turn_im], axis=1)
    result = jnp.einsum("nk,ckm->cnm", outer_both, turned, precision=HIGHEST)
    return result.reshape(channels, length) / full_length


def general_shards(
    gate_input, value_input, short_filter, long_filter, query_weight, key_matrix, value_matrix
):
    seq_rows, local_width = gate_input.shape
    last_rows = gate_input[seq_rows - (TAPS - 1) :]
    earlier = shifted(last_rows, "seq", 1)
    padded = jnp.concatenate([earlier, gate_input], axis=0).astype(jnp.float32)
    kernel = short_filter[:, ::-1].T[:, None, :]
    smoothed = lax.conv_general_dilated(
        padded[None],
        kernel,
        (1,),
        "VALID",
        dimension_numbers=("NHC", "HIO", "NHC"),
        feature_group_count=local_width,
        precision=HIGHEST,
    )[0]
    mixed_input = (smoothed * value_input.astype(jnp.float32)).astype(jnp.bfloat16)
    signal, kernel_line = (
        lax.all_to_all(mixed_input.T, "seq", split_axis=0, concat_axis=1, tiled=True),
        lax.all_to_all(long_filter.T, "seq", split_axis=0, concat_axis=1, tiled=True),
    )
    length = signal.shape[1]
    signal_both = spectrum(signal.astype(jnp.float32), RADIX)
    kernel_both = spectrum(kernel_line.astype(jnp.float32), RADIX)
    signal_re = signal_both[:, :, :RADIX]
    signal_im = signal_both[:, :, RADIX:]
    kernel_re = kernel_both[:, :, :RADIX]
    kernel_im = kernel_both[:, :, RADIX:]
    joint = jnp.concatenate(
        [
            signal_re * kernel_re - signal_im * kernel_im,
            signal_re * kernel_im + signal_im * kernel_re,
        ],
        axis=2,
    )
    conv_line = inverse(joint, RADIX, length).astype(jnp.bfloat16)
    my_index = lax.axis_index("seq")
    group_firsts = [my_index * seq_rows]
    conv_columns = lax.all_to_all(conv_line, "seq", split_axis=1, concat_axis=0, tiled=True)
    heads_here = local_width // HEAD_DIM
    conv_heads = conv_columns.reshape(heads_here, HEAD_DIM, seq_rows)
    query_heads = jnp.einsum(
        "hds,hde->hse", conv_heads, query_weight, preferred_element_type=jnp.float32
    ).astype(jnp.bfloat16)
    group_count = len(group_firsts)
    query_groups = [query_heads]
    key_heads = key_matrix.reshape(seq_rows, heads_here, HEAD_DIM).transpose(1, 0, 2)
    value_heads = value_matrix.reshape(seq_rows, heads_here, HEAD_DIM).transpose(1, 0, 2)
    score_scale = 1.0 / math.sqrt(HEAD_DIM)

    def attend_group(running, group_query, group_first, key_block, value_block, first_row):
        block_rows = key_block.shape[1]

        def compute(current):
            peak_value, weight_sum, weighted = current
            scores = (
                jnp.einsum(
                    "hqd,hkd->hqk", group_query, key_block, preferred_element_type=jnp.float32
                )
                * score_scale
            )
            key_pos = first_row + lax.iota(jnp.int32, block_rows)
            query_pos = group_first + lax.iota(jnp.int32, seq_rows)
            allowed = (key_pos[None, :] <= query_pos[:, None])[None]
            scores = jnp.where(allowed, scores, -1e30)
            new_peak = jnp.maximum(peak_value, jnp.max(scores, axis=2))
            weights = jnp.where(allowed, jnp.exp(scores - new_peak[:, :, None]), 0.0)
            rescale = jnp.exp(peak_value - new_peak)
            weight_sum = weight_sum * rescale + jnp.sum(weights, axis=2)
            weighted = weighted * rescale[:, :, None] + jnp.einsum(
                "hqk,hkd->hqd",
                weights.astype(jnp.bfloat16),
                value_block,
                preferred_element_type=jnp.float32,
            )
            return (new_peak, weight_sum, weighted)

        live = first_row <= group_first + seq_rows - 1
        return lax.cond(live, compute, lambda current: current, running)

    def attend(states, key_block, value_block, first_row):
        return tuple(
            (
                attend_group(
                    states[g], query_groups[g], group_firsts[g], key_block, value_block, first_row
                )
                for g in range(group_count)
            )
        )

    one_state = (
        jnp.full((heads_here, seq_rows), -1e30, jnp.float32),
        jnp.zeros((heads_here, seq_rows), jnp.float32),
        jnp.zeros((heads_here, seq_rows, HEAD_DIM), jnp.float32),
    )
    initial = tuple((one_state for g in range(group_count)))
    running = initial
    key_piece = lax.all_gather(key_heads, "seq", axis=1, tiled=True)
    value_piece = lax.all_gather(value_heads, "seq", axis=1, tiled=True)
    piece_rows = key_piece.shape[1]
    block_rows = 512
    block_count = piece_rows // block_rows
    key_blocks = key_piece.reshape(heads_here, block_count, block_rows, HEAD_DIM).transpose(
        1, 0, 2, 3
    )
    value_blocks = value_piece.reshape(heads_here, block_count, block_rows, HEAD_DIM).transpose(
        1, 0, 2, 3
    )

    def advance(current, element):
        key_block, value_block, position = element
        return (attend(current, key_block, value_block, position * block_rows), None)

    running, _ = lax.scan(
        advance, running, (key_blocks, value_blocks, lax.iota(jnp.int32, block_count))
    )
    outputs = [state[2] / state[1][:, :, None] for state in running]
    result = outputs[0]
    attended_rows = result.transpose(1, 0, 2).reshape(seq_rows, local_width).astype(jnp.bfloat16)
    return attended_rows


def block_tables(block):
    angle = np.pi / block * (np.arange(block) + 0.5)
    window = angle[:, None] * (np.arange(2 * block) - block)[None]
    ahead = np.concatenate([np.cos(window), -np.sin(window)], axis=0)
    inner = np.arange(block)[:, None] * angle[None]
    back = np.concatenate([np.cos(inner), -np.sin(inner)], axis=1) / block

    def pair(table):
        high = table.astype(ml_dtypes.bfloat16)
        rest = (table - high.astype(np.float64)).astype(ml_dtypes.bfloat16)
        return np.concatenate([high, rest], axis=0)

    return pair(ahead), pair(back)


def two_parts(value):
    high = value.astype(jnp.bfloat16)
    return high, (value - high.astype(jnp.float32)).astype(jnp.bfloat16)


def mxu(left, right):
    return jnp.dot(left, right, preferred_element_type=jnp.float32)


def folded_sum(stacked):
    half = stacked.shape[0] // 2
    return stacked[:half] + stacked[half:]


def wide_mxu(table, value):
    half = table.shape[0] // 2
    wide = jnp.concatenate([table[:half], table[half:]], axis=1)
    return mxu(wide, jnp.concatenate([value, value], axis=0))


def to_block(back, spec_re, spec_im, block):
    high, rest = two_parts(jnp.concatenate([spec_re, spec_im], axis=0))
    return folded_sum(mxu(back, high)) + mxu(back[:block], rest)


def pack_kernel(*rest, parts, width):
    outs, sem = rest[-len(parts) - 1 : -1], rest[-1]
    here, group = lax.axis_index("seq"), lax.axis_index("groups")
    copies = []
    for (step, columns, shared, arrays), out in zip(parts, outs):
        start = (here ^ step) * width
        if shared:
            start = start + group * columns
        chosen = pl.ds(pl.multiple_of(start, HEAD_DIM), columns)
        for n, source in enumerate(rest[i] for i in arrays):
            rows = source.shape[0]
            copies.append(
                pltpu.make_async_copy(
                    source.at[:, chosen], out.at[n * rows : (n + 1) * rows], sem.at[len(copies)]
                )
            )
    for copy in copies:
        copy.start()
    for copy in copies:
        copy.wait()


def own_columns(ref, here, width):
    return ref[:, pl.ds(pl.multiple_of(here * width, width), width)]


def smooth_kernel(gate_ref, value_ref, near_ref, *rest, count, block):
    arrived = rest[: count - 2]
    taps_ref, ahead_ref, back_ref, mixed_ref, gate_all, value_all = rest[count - 2 :]
    here = lax.axis_index("seq")
    gate_all[0] = jnp.zeros(gate_all.shape[1:], gate_all.dtype)
    width = near_ref.shape[1]
    gate_all[here + 1] = own_columns(gate_ref, here, width)
    value_all[here] = own_columns(value_ref, here, width)
    for step, piece in enumerate((near_ref, *arrived), 1):
        gate_all[(here ^ step) + 1] = piece[:block]
        value_all[here ^ step] = piece[block : 2 * block]
    ahead = ahead_ref[...]
    back = back_ref[...]
    first = ahead[:, block:]
    turned = (((1,), (1,)), ((), ()))
    taps = taps_ref[pl.ds(pl.multiple_of(here * width, width), width)]
    taps_high, taps_rest = two_parts(taps)
    taps_spec = folded_sum(
        lax.dot_general(first, taps_high, turned, preferred_element_type=jnp.float32)
    ) + lax.dot_general(
        first[: 2 * block], taps_rest, turned, preferred_element_type=jnp.float32
    )
    taps_re, taps_im = taps_spec[:block], taps_spec[block:]
    for b in range(count):
        window = jnp.concatenate([gate_all[b], gate_all[b + 1]], axis=0)
        gate_spec = wide_mxu(ahead, window)
        gate_re, gate_im = gate_spec[:block], gate_spec[block:]
        smoothed = to_block(
            back,
            gate_re * taps_re - gate_im * taps_im,
            gate_re * taps_im + gate_im * taps_re,
            block,
        )
        mixed_ref[b] = (smoothed * value_all[b].astype(jnp.float32)).astype(jnp.bfloat16)


def conv_kernel(mixed_ref, own_ref, near_ref, *rest, count, groups, block, head_dim):
    far = count - 2
    shares = rest[:groups]
    weight_ref, ahead_ref, back_ref, query_ref, filter_all = rest[groups:]
    here = lax.axis_index("seq")
    group = lax.axis_index("groups") if groups > 1 else 0
    filter_all[0] = jnp.zeros(filter_all.shape[1:], filter_all.dtype)
    filter_all[here + 1] = own_columns(own_ref, here, near_ref.shape[1])
    filter_all[(here ^ 1) + 1] = near_ref[2 * block : 3 * block]
    for shift, share in enumerate(shares):
        columns = share.shape[1]
        start = lax.rem(group + groups - shift, groups) * columns
        chosen = pl.ds(pl.multiple_of(start, head_dim), columns)
        for n in range(far):
            filter_all[(here ^ (n + 2)) + 1, :, chosen] = share[n * block : (n + 1) * block]
    ahead = ahead_ref[...]
    back = back_ref[...]
    first = ahead[:, block:]
    heads = mixed_ref.shape[2] // head_dim
    lines = []
    kernels = []
    for b in range(count):
        lines.append(wide_mxu(first, mixed_ref[b]))
        kernels.append(
            wide_mxu(ahead, jnp.concatenate([filter_all[b], filter_all[b + 1]], axis=0))
        )
    for b in range(count):
        total_re, total_im = 0.0, 0.0
        for j in range(b + 1):
            line, kernel = lines[j], kernels[b - j]
            line_re, line_im = line[:block], line[block:]
            kernel_re, kernel_im = kernel[:block], kernel[block:]
            total_re = total_re + (line_re * kernel_re - line_im * kernel_im)
            total_im = total_im + (line_re * kernel_im + line_im * kernel_re)
        conv_out = to_block(back, total_re, total_im, block).astype(jnp.bfloat16)
        for h in range(heads):
            columns = slice(h * head_dim, (h + 1) * head_dim)
            query_ref[b, :, columns] = mxu(
                conv_out[:, columns], weight_ref[here * heads + h]
            ).astype(jnp.bfloat16)


def weigh_kernel(query_ref, own_ref, near_ref, *rest, count, block, head_dim):
    arrived = rest[: count - 2]
    weight_ref, part_ref, key_all = rest[count - 2 :]
    here = lax.axis_index("seq")
    key_all[here] = own_columns(own_ref, here, near_ref.shape[1])
    for step, piece in enumerate((near_ref, *arrived), 1):
        first = max(piece.shape[0] - 2 * block, 0)
        key_all[here ^ step] = piece[first : first + block]
    width = query_ref.shape[2]
    turned = (((1,), (1,)), ((), ()))
    scale = 1.0 / math.sqrt(head_dim)
    row = lax.broadcasted_iota(jnp.int32, (block, block), 0)
    column = lax.broadcasted_iota(jnp.int32, (block, block), 1)
    allowed = column <= row
    for h in range(width // head_dim):
        columns = slice(h * head_dim, (h + 1) * head_dim)
        for b in range(count):
            query = query_ref[b, :, columns]
            scores = []
            for j in range(b + 1):
                part = (
                    lax.dot_general(
                        query,
                        key_all[j, :, columns],
                        turned,
                        preferred_element_type=jnp.float32,
                    )
                    * scale
                )
                scores.append(jnp.where(allowed, part, -1e30) if j == b else part)
            peak = functools.reduce(jnp.maximum, scores)
            peak = jnp.max(peak, axis=1, keepdims=True)
            weights = [jnp.exp(part - peak) for part in scores]
            weights[b] = jnp.where(allowed, weights[b], 0.0)
            weight_sum = jnp.sum(functools.reduce(jnp.add, weights), axis=1, keepdims=True)
            part_ref[h, b] = jnp.broadcast_to(1.0 / weight_sum, (block, head_dim))
            for j in range(b + 1):
                weight_ref[h, b, :, j * block : (j + 1) * block] = weights[j].astype(
                    jnp.bfloat16
                )


def sum_kernel(
    weight_ref, part_ref, own_ref, near_ref, *rest, count, block, head_dim
):
    arrived = rest[: count - 2]
    outs = rest[count - 2 : 2 * count - 2]
    value_all, out_all = rest[2 * count - 2 :]
    here = lax.axis_index("seq")

    def rows_of(b):
        return pl.ds(pl.multiple_of(b * block, block), block)

    value_all[rows_of(here)] = own_columns(own_ref, here, near_ref.shape[1])
    for step, piece in enumerate((near_ref, *arrived), 1):
        value_all[rows_of(here ^ step)] = piece[-block:]
    for h in range(value_all.shape[1] // head_dim):
        columns = slice(h * head_dim, (h + 1) * head_dim)
        for b in range(count):
            seen = (b + 1) * block
            total = mxu(weight_ref[h, b, :, :seen], value_all[:seen, columns])
            out_all[b, :, columns] = (total * part_ref[h, b]).astype(jnp.bfloat16)
    for step, out in enumerate(outs):
        out[...] = out_all[here ^ step]


def join_kernel(*rest, steps, width):
    pieces, out_ref, sem = rest[: len(steps)], rest[-2], rest[-1]
    here = lax.axis_index("seq")
    copies = []
    for n, (step, piece) in enumerate(zip(steps, pieces)):
        columns = pl.ds(pl.multiple_of((here ^ step) * width, width), width)
        copies.append(pltpu.make_async_copy(piece, out_ref.at[:, columns], sem.at[n]))
    for copy in copies:
        copy.start()
    for copy in copies:
        copy.wait()


WHOLE = pl.BlockSpec(memory_space=pltpu.VMEM)


def head_shards(
    gate_input, value_input, short_filter, long_filter, query_weight, key_matrix, value_matrix
):
    count = lax.axis_size("seq")
    block, local_width = gate_input.shape
    width = local_width // count
    heads = width // HEAD_DIM
    here = lax.axis_index("seq")
    groups = lax.axis_size("groups") if heads % lax.axis_size("groups") == 0 else 1

    def swap(value, step):
        return lax.ppermute(value, "seq", [(i, i ^ step) for i in range(count)])

    def packed(arrays, parts, after=()):
        return pl.pallas_call(
            functools.partial(pack_kernel, parts=parts, width=width),
            out_shape=[
                pltpu.VMEM((len(chosen) * block, columns), jnp.bfloat16)
                for _, columns, _, chosen in parts
            ],
            in_specs=[pl.BlockSpec(memory_space=pl.ANY)] * (len(arrays) + len(after)),
            out_specs=[WHOLE] * len(parts),
            scratch_shapes=[
                pltpu.SemaphoreType.DMA((sum(len(chosen) for *_, chosen in parts),))
            ],
            compiler_params=params,
        )(*[pltpu.with_memory_space_constraint(a, pltpu.HBM) for a in arrays], *after)

    ahead, back = block_tables(block)
    scratch = lambda n: pltpu.VMEM((n, block, width), jnp.bfloat16)
    params = pltpu.CompilerParams(vmem_limit_bytes=32 * 1024 * 1024)
    far = range(2, count)
    share = width // groups
    every = (0, 1, 2, 3, 4)
    pieces = packed(
        [gate_input, value_input, long_filter, key_matrix, value_matrix],
        [(step, share, True, (2,)) for step in far]
        + [(step, width, False, (0, 1)) for step in far]
        + [(1, width, False, every)]
        + [(step, width, False, (3, 4)) for step in far[:-1]]
        + [(far[-1], width, False, (n,)) for n in (3, 4)],
    )
    filters, streams, near, later = (
        pieces[: len(far)],
        pieces[len(far) : 2 * len(far)],
        pieces[2 * len(far)],
        pieces[2 * len(far) + 1 :],
    )
    near = swap(near, 1)
    filters = [swap(piece, step) for step, piece in zip(far, filters)]
    arrived = [swap(piece, step) for step, piece in zip(far, streams)]
    near, *rest = lax.optimization_barrier((near, *filters, *later))
    filters, later = rest[: len(far)], rest[len(far) :]
    shares = [jnp.concatenate(filters)]
    for shift in range(1, groups):
        shares.append(
            lax.ppermute(
                shares[0], "groups", [(i, (i + shift) % groups) for i in range(groups)]
            )
        )
    later = [swap(piece, step) for step, piece in zip([*far, far[-1]], later)]
    arrived_keys, arrived_values = later[:-1], [*later[:-2], later[-1]]
    tables = jnp.asarray(ahead), jnp.asarray(back)
    streamed = jax.ShapeDtypeStruct((count, block, width), jnp.bfloat16)
    mixed = pl.pallas_call(
        functools.partial(smooth_kernel, count=count, block=block),
        out_shape=streamed,
        in_specs=[WHOLE] * (count + 4),
        out_specs=WHOLE,
        scratch_shapes=[scratch(count + 1), scratch(count)],
        compiler_params=params,
    )(gate_input, value_input, near, *arrived, short_filter, *tables)
    queries = pl.pallas_call(
        functools.partial(
            conv_kernel, count=count, groups=groups, block=block, head_dim=HEAD_DIM
        ),
        out_shape=streamed,
        in_specs=[WHOLE] * (groups + 6),
        out_specs=WHOLE,
        scratch_shapes=[scratch(count + 1)],
        compiler_params=params,
    )(mixed, long_filter, near, *shares, query_weight, *tables)
    weights, parts = pl.pallas_call(
        functools.partial(weigh_kernel, count=count, block=block, head_dim=HEAD_DIM),
        out_shape=[
            jax.ShapeDtypeStruct((heads, count, block, count * block), jnp.bfloat16),
            jax.ShapeDtypeStruct((heads, count, block, HEAD_DIM), jnp.float32),
        ],
        in_specs=[WHOLE] * (count + 1),
        out_specs=[WHOLE] * 2,
        scratch_shapes=[scratch(count)],
        compiler_params=params,
    )(queries, key_matrix, near, *arrived_keys)
    pieces = pl.pallas_call(
        functools.partial(sum_kernel, count=count, block=block, head_dim=HEAD_DIM),
        out_shape=[jax.ShapeDtypeStruct((block, width), jnp.bfloat16)] * count,
        in_specs=[WHOLE] * (count + 2),
        out_specs=[WHOLE] * count,
        scratch_shapes=[
            pltpu.VMEM((count * block, width), jnp.bfloat16),
            scratch(count),
        ],
        compiler_params=params,
    )(weights, parts, value_matrix, near, *arrived_values)
    swapped = {step: swap(pieces[step], step) for step in [*far, 1]}
    pieces = [pieces[0]] + [swapped[step] for step in range(1, count)]

    def joined(steps, *before):
        return pl.pallas_call(
            functools.partial(join_kernel, steps=steps, width=width),
            out_shape=pltpu.HBM((block, local_width), jnp.bfloat16),
            in_specs=[WHOLE] * len(steps) + [pl.BlockSpec(memory_space=pl.ANY)] * len(before),
            out_specs=pl.BlockSpec(memory_space=pl.ANY),
            scratch_shapes=[pltpu.SemaphoreType.DMA((len(steps),))],
            input_output_aliases={len(steps): 0} if before else {},
            compiler_params=params,
        )(*[pieces[step] for step in steps], *before)

    return joined(tuple(far), joined((0, 1)))


def shards(*arrays):
    count = lax.axis_size("seq")
    block, local_width = arrays[0].shape
    even = local_width % (count * HEAD_DIM) == 0
    if even and count > 1 and count & (count - 1) == 0 and block == TAPS:
        return head_shards(*arrays)
    return general_shards(*arrays)


def solution(mesh):
    in_specs = (
        P(("groups", "seq"), "chan"),
        P(("groups", "seq"), "chan"),
        P("chan", None),
        P("seq", "chan"),
        P("chan", None, None),
        P(("groups", "seq"), "chan"),
        P(("groups", "seq"), "chan"),
    )
    out_specs = P(("groups", "seq"), "chan")
    return jax.shard_map(shards, mesh=mesh, in_specs=in_specs, out_specs=out_specs, check_vma=False)
```

```python
import functools
import math

import jax
import jax.numpy as jnp
import ml_dtypes
import numpy as np
from jax import lax
from jax.experimental import pallas as pl
from jax.experimental.pallas import tpu as pltpu
from jax.sharding import PartitionSpec as P

HEAD_DIM = 128
TAPS = 128
RADIX = 128


HIGHEST = lax.Precision.HIGHEST


def shifted(value, axis, steps):
    count = lax.axis_size(axis)
    initial, last = (max(0, -steps), min(count, count - steps))
    return lax.ppermute(value, axis, [(source, source + steps) for source in range(initial, last)])


def unit_table(height, breadth, modulus, orient):
    product = (
        lax.broadcasted_iota(jnp.int32, (height, breadth), 0)
        * lax.broadcasted_iota(jnp.int32, (height, breadth), 1)
        % modulus
    )
    angles = 2.0 * math.pi / modulus * product.astype(jnp.float32)
    return (jnp.cos(angles), orient * jnp.sin(angles))


def block_table(factor, orient):
    inner_re, inner_im = unit_table(factor, factor, factor, orient)
    upper = jnp.concatenate([inner_re, inner_im], axis=1)
    lower = jnp.concatenate([-inner_im, inner_re], axis=1)
    return jnp.concatenate([upper, lower], axis=0)


def spectrum(signal, factor):
    channels, length = signal.shape
    full_length = 2 * length
    column_count = full_length // factor
    folded = signal.reshape(channels, column_count // 2, factor)
    outer_re, outer_im = unit_table(column_count, column_count // 2, column_count, -1.0)
    outer_both = jnp.concatenate([outer_re, outer_im], axis=0)
    first = jnp.einsum("kn,cnm->ckm", outer_both, folded, precision=HIGHEST)
    first_re = first[:, :column_count]
    first_im = first[:, column_count:]
    twist_re, twist_im = unit_table(column_count, factor, full_length, -1.0)
    mid_re = first_re * twist_re - first_im * twist_im
    mid_im = first_re * twist_im + first_im * twist_re
    joined = jnp.concatenate([mid_re, mid_im], axis=2)
    return jnp.einsum("ckn,nm->ckm", joined, block_table(factor, -1.0), precision=HIGHEST)


def inverse(spec_both, factor, length):
    channels = spec_both.shape[0]
    full_length = 2 * length
    column_count = full_length // factor
    mid = jnp.einsum("ckm,mn->ckn", spec_both, block_table(factor, 1.0), precision=HIGHEST)
    mid_re = mid[:, :, :factor]
    mid_im = mid[:, :, factor:]
    twist_re, twist_im = unit_table(column_count, factor, full_length, 1.0)
    turn_re = mid_re * twist_re - mid_im * twist_im
    turn_im = mid_re * twist_im + mid_im * twist_re
    outer_re, outer_im = unit_table(column_count // 2, column_count, column_count, 1.0)
    outer_both = jnp.concatenate([outer_re, -outer_im], axis=1)
    turned = jnp.concatenate([turn_re, turn_im], axis=1)
    result = jnp.einsum("nk,ckm->cnm", outer_both, turned, precision=HIGHEST)
    return result.reshape(channels, length) / full_length


def general_shards(
    gate_input, value_input, short_filter, long_filter, query_weight, key_matrix, value_matrix
):
    seq_rows, local_width = gate_input.shape
    last_rows = gate_input[seq_rows - (TAPS - 1) :]
    earlier = shifted(last_rows, "seq", 1)
    padded = jnp.concatenate([earlier, gate_input], axis=0).astype(jnp.float32)
    kernel = short_filter[:, ::-1].T[:, None, :]
    smoothed = lax.conv_general_dilated(
        padded[None],
        kernel,
        (1,),
        "VALID",
        dimension_numbers=("NHC", "HIO", "NHC"),
        feature_group_count=local_width,
        precision=HIGHEST,
    )[0]
    mixed_input = (smoothed * value_input.astype(jnp.float32)).astype(jnp.bfloat16)
    signal, kernel_line = (
        lax.all_to_all(mixed_input.T, "seq", split_axis=0, concat_axis=1, tiled=True),
        lax.all_to_all(long_filter.T, "seq", split_axis=0, concat_axis=1, tiled=True),
    )
    length = signal.shape[1]
    signal_both = spectrum(signal.astype(jnp.float32), RADIX)
    kernel_both = spectrum(kernel_line.astype(jnp.float32), RADIX)
    signal_re = signal_both[:, :, :RADIX]
    signal_im = signal_both[:, :, RADIX:]
    kernel_re = kernel_both[:, :, :RADIX]
    kernel_im = kernel_both[:, :, RADIX:]
    joint = jnp.concatenate(
        [
            signal_re * kernel_re - signal_im * kernel_im,
            signal_re * kernel_im + signal_im * kernel_re,
        ],
        axis=2,
    )
    conv_line = inverse(joint, RADIX, length).astype(jnp.bfloat16)
    my_index = lax.axis_index("seq")
    group_firsts = [my_index * seq_rows]
    conv_columns = lax.all_to_all(conv_line, "seq", split_axis=1, concat_axis=0, tiled=True)
    heads_here = local_width // HEAD_DIM
    conv_heads = conv_columns.reshape(heads_here, HEAD_DIM, seq_rows)
    query_heads = jnp.einsum(
        "hds,hde->hse", conv_heads, query_weight, preferred_element_type=jnp.float32
    ).astype(jnp.bfloat16)
    group_count = len(group_firsts)
    query_groups = [query_heads]
    key_heads = key_matrix.reshape(seq_rows, heads_here, HEAD_DIM).transpose(1, 0, 2)
    value_heads = value_matrix.reshape(seq_rows, heads_here, HEAD_DIM).transpose(1, 0, 2)
    score_scale = 1.0 / math.sqrt(HEAD_DIM)

    def attend_group(running, group_query, group_first, key_block, value_block, first_row):
        block_rows = key_block.shape[1]

        def compute(current):
            peak_value, weight_sum, weighted = current
            scores = (
                jnp.einsum(
                    "hqd,hkd->hqk", group_query, key_block, preferred_element_type=jnp.float32
                )
                * score_scale
            )
            key_pos = first_row + lax.iota(jnp.int32, block_rows)
            query_pos = group_first + lax.iota(jnp.int32, seq_rows)
            allowed = (key_pos[None, :] <= query_pos[:, None])[None]
            scores = jnp.where(allowed, scores, -1e30)
            new_peak = jnp.maximum(peak_value, jnp.max(scores, axis=2))
            weights = jnp.where(allowed, jnp.exp(scores - new_peak[:, :, None]), 0.0)
            rescale = jnp.exp(peak_value - new_peak)
            weight_sum = weight_sum * rescale + jnp.sum(weights, axis=2)
            weighted = weighted * rescale[:, :, None] + jnp.einsum(
                "hqk,hkd->hqd",
                weights.astype(jnp.bfloat16),
                value_block,
                preferred_element_type=jnp.float32,
            )
            return (new_peak, weight_sum, weighted)

        live = first_row <= group_first + seq_rows - 1
        return lax.cond(live, compute, lambda current: current, running)

    def attend(states, key_block, value_block, first_row):
        return tuple(
            (
                attend_group(
                    states[g], query_groups[g], group_firsts[g], key_block, value_block, first_row
                )
                for g in range(group_count)
            )
        )

    one_state = (
        jnp.full((heads_here, seq_rows), -1e30, jnp.float32),
        jnp.zeros((heads_here, seq_rows), jnp.float32),
        jnp.zeros((heads_here, seq_rows, HEAD_DIM), jnp.float32),
    )
    initial = tuple((one_state for g in range(group_count)))
    running = initial
    key_piece = lax.all_gather(key_heads, "seq", axis=1, tiled=True)
    value_piece = lax.all_gather(value_heads, "seq", axis=1, tiled=True)
    piece_rows = key_piece.shape[1]
    block_rows = 512
    block_count = piece_rows // block_rows
    key_blocks = key_piece.reshape(heads_here, block_count, block_rows, HEAD_DIM).transpose(
        1, 0, 2, 3
    )
    value_blocks = value_piece.reshape(heads_here, block_count, block_rows, HEAD_DIM).transpose(
        1, 0, 2, 3
    )

    def advance(current, element):
        key_block, value_block, position = element
        return (attend(current, key_block, value_block, position * block_rows), None)

    running, _ = lax.scan(
        advance, running, (key_blocks, value_blocks, lax.iota(jnp.int32, block_count))
    )
    outputs = [state[2] / state[1][:, :, None] for state in running]
    result = outputs[0]
    attended_rows = result.transpose(1, 0, 2).reshape(seq_rows, local_width).astype(jnp.bfloat16)
    return attended_rows


def block_tables(block):
    angle = np.pi / block * (np.arange(block) + 0.5)
    turns = angle[:, None] * np.arange(block)[None]
    ahead = np.concatenate([np.cos(turns), -np.sin(turns)], axis=0)
    back = np.concatenate([np.cos(turns.T), -np.sin(turns.T)], axis=1) / block

    def pair(table):
        high = table.astype(ml_dtypes.bfloat16)
        rest = (table - high.astype(np.float64)).astype(ml_dtypes.bfloat16)
        return np.concatenate([high, rest], axis=0)

    return pair(ahead), pair(back)


def two_parts(value):
    high = value.astype(jnp.bfloat16)
    return high, (value - high.astype(jnp.float32)).astype(jnp.bfloat16)


def mxu(left, right):
    return jnp.dot(left, right, preferred_element_type=jnp.float32)


def folded_sum(stacked):
    half = stacked.shape[0] // 2
    return stacked[:half] + stacked[half:]


def wide_mxu(table, value):
    half = table.shape[0] // 2
    wide = jnp.concatenate([table[:half], table[half:]], axis=1)
    return mxu(wide, jnp.concatenate([value, value], axis=0))


def to_blocks(back, spectra, block):
    parts = [two_parts(jnp.concatenate(spec, axis=0)) for spec in spectra]
    main = [mxu(back, high) for high, _ in parts]
    small = [mxu(back[:block], rest) for _, rest in parts]
    return [folded_sum(large) + rest for large, rest in zip(main, small)]


def pack_kernel(*rest, parts, width):
    outs, sem = rest[-len(parts) - 1 : -1], rest[-1]
    here, group = lax.axis_index("seq"), lax.axis_index("groups")
    copies = []
    for (step, columns, blocks), out in zip(parts, outs):
        for n, (i, slot) in enumerate(blocks):
            start = (here ^ step) * width + (group if slot is None else slot) * columns
            source = rest[i].at[:, pl.ds(pl.multiple_of(start, HEAD_DIM), columns)]
            rows = source.shape[0]
            copies.append(
                pltpu.make_async_copy(
                    source, out.at[n * rows : (n + 1) * rows], sem.at[len(copies)]
                )
            )
    for copy in copies:
        copy.start()
    for copy in copies:
        copy.wait()


def own_columns(ref, here, width):
    return ref[:, pl.ds(pl.multiple_of(here * width, width), width)]


def with_block_before(spec, before, block):
    odd = lax.broadcasted_iota(jnp.int32, (block, spec.shape[1]), 0) % 2
    sign = 1.0 - 2.0 * odd.astype(jnp.float32)
    return spec[:block] - sign * before[block:], spec[block:] + sign * before[:block]


def local_kernel(gate_ref, filter_ref, near_ref, taps_ref, ahead_ref, *outs, block):
    gate_spec_ref, filter_spec_ref, taps_spec_ref = outs
    here = lax.axis_index("seq")
    width = near_ref.shape[1]
    ahead = ahead_ref[...]
    gate_spec_ref[0] = wide_mxu(ahead, own_columns(gate_ref, here, width))
    gate_spec_ref[1] = wide_mxu(ahead, near_ref[:block])
    filter_spec_ref[0] = wide_mxu(ahead, own_columns(filter_ref, here, width))
    filter_spec_ref[1] = wide_mxu(ahead, near_ref[2 * block : 3 * block])
    turned = (((1,), (1,)), ((), ()))
    taps = taps_ref[pl.ds(pl.multiple_of(here * width, width), width)]
    taps_high, taps_rest = two_parts(taps)
    taps_spec_ref[...] = folded_sum(
        lax.dot_general(ahead, taps_high, turned, preferred_element_type=jnp.float32)
    ) + lax.dot_general(
        ahead[: 2 * block], taps_rest, turned, preferred_element_type=jnp.float32
    )


def smooth_kernel(gate_spec_ref, taps_spec_ref, value_ref, near_ref, *rest, count, block):
    arrived = rest[: count - 2]
    ahead_ref, back_ref, line_ref, gate_all, value_all = rest[count - 2 :]
    here = lax.axis_index("seq")
    width = near_ref.shape[1]
    ahead = ahead_ref[...]
    back = back_ref[...]
    value_all[here] = own_columns(value_ref, here, width)
    value_all[here ^ 1] = near_ref[block : 2 * block]
    gate_all[here] = gate_spec_ref[0]
    gate_all[here ^ 1] = gate_spec_ref[1]
    for step, piece in enumerate(arrived, 2):
        columns = piece.shape[1]
        slots = width // columns

        def joined(first):
            return jnp.concatenate(
                [piece[n * block : (n + 1) * block] for n in range(first, first + slots)], axis=1
            )

        gate_all[here ^ step] = wide_mxu(ahead, joined(0))
        value_all[here ^ step] = joined(slots)
    taps_re, taps_im = taps_spec_ref[:block], taps_spec_ref[block:]
    spectra = []
    for b in range(count):
        gate_spec = gate_all[b]
        if b > 0:
            gate_re, gate_im = with_block_before(gate_spec, gate_all[b - 1], block)
        else:
            gate_re, gate_im = gate_spec[:block], gate_spec[block:]
        spectra.append(
            (gate_re * taps_re - gate_im * taps_im, gate_re * taps_im + gate_im * taps_re)
        )
    mixed = [
        (smoothed * value_all[b].astype(jnp.float32)).astype(jnp.bfloat16)
        for b, smoothed in enumerate(to_blocks(back, spectra, block))
    ]
    for b in range(count):
        line_ref[b] = wide_mxu(ahead, mixed[b])


def conv_kernel(line_ref, filter_spec_ref, *rest, count, groups, block, head_dim):
    far = count - 2
    shares = [rest[n * far : (n + 1) * far] for n in range(groups)]
    weight_ref, ahead_ref, back_ref, query_ref, filter_all, spec_all = rest[groups * far :]
    here = lax.axis_index("seq")
    group = lax.axis_index("groups") if groups > 1 else 0
    for shift, pieces in enumerate(shares):
        for n, piece in enumerate(pieces):
            columns = piece.shape[1]
            start = lax.rem(group + groups - shift, groups) * columns
            chosen = pl.ds(pl.multiple_of(start, head_dim), columns)
            filter_all[n, :, chosen] = piece[piece.shape[0] - block :]
    ahead = ahead_ref[...]
    back = back_ref[...]
    heads = line_ref.shape[2] // head_dim
    spec_all[here] = filter_spec_ref[0]
    spec_all[here ^ 1] = filter_spec_ref[1]
    for n in range(far):
        spec_all[here ^ (n + 2)] = wide_mxu(ahead, filter_all[n])
    lines = [(line_ref[b, :block], line_ref[b, block:]) for b in range(count)]
    kernels = [(spec_all[0, :block], spec_all[0, block:])] + [
        with_block_before(spec_all[b], spec_all[b - 1], block) for b in range(1, count)
    ]
    totals = []
    for b in range(count):
        total_re, total_im = 0.0, 0.0
        for j in range(b + 1):
            line_re, line_im = lines[j]
            kernel_re, kernel_im = kernels[b - j]
            total_re = total_re + (line_re * kernel_re - line_im * kernel_im)
            total_im = total_im + (line_re * kernel_im + line_im * kernel_re)
        totals.append((total_re, total_im))
    for b, conv_out in enumerate(to_blocks(back, totals, block)):
        conv_out = conv_out.astype(jnp.bfloat16)
        for h in range(heads):
            columns = slice(h * head_dim, (h + 1) * head_dim)
            query_ref[b, :, columns] = mxu(
                conv_out[:, columns], weight_ref[here * heads + h]
            ).astype(jnp.bfloat16)


def weigh_kernel(query_ref, own_ref, near_ref, *rest, count, block, head_dim):
    arrived = rest[: count - 2]
    weight_ref, part_ref, key_all = rest[count - 2 :]
    here = lax.axis_index("seq")
    key_all[here] = own_columns(own_ref, here, near_ref.shape[1])
    for step, piece in enumerate((near_ref, *arrived), 1):
        first = max(piece.shape[0] - 2 * block, 0)
        key_all[here ^ step] = piece[first : first + block]
    width = query_ref.shape[2]
    turned = (((1,), (1,)), ((), ()))
    scale = 1.0 / math.sqrt(head_dim)
    row = lax.broadcasted_iota(jnp.int32, (block, block), 0)
    column = lax.broadcasted_iota(jnp.int32, (block, block), 1)
    allowed = column <= row
    places = [(h, b) for h in range(width // head_dim) for b in range(count)]
    scores = []
    for h, b in places:
        columns = slice(h * head_dim, (h + 1) * head_dim)
        query = query_ref[b, :, columns]
        parts = []
        for j in range(b + 1):
            part = lax.dot_general(
                query, key_all[j, :, columns], turned, preferred_element_type=jnp.float32
            )
            part = part * scale
            parts.append(jnp.where(allowed, part, -1e30) if j == b else part)
        scores.append(parts)
    peaks = [
        jnp.max(functools.reduce(jnp.maximum, parts), axis=1, keepdims=True) for parts in scores
    ]
    sums = []
    for (h, b), parts, peak in zip(places, scores, peaks):
        weights = [jnp.exp(part - peak) for part in parts]
        weights[b] = jnp.where(allowed, weights[b], 0.0)
        sums.append(jnp.sum(functools.reduce(jnp.add, weights), axis=1, keepdims=True))
        for j in range(b + 1):
            weight_ref[h, b, :, j * block : (j + 1) * block] = weights[j].astype(jnp.bfloat16)
    for (h, b), weight_sum in zip(places, sums):
        part_ref[h, b] = jnp.broadcast_to(1.0 / weight_sum, (block, head_dim))


def sum_kernel(
    weight_ref, part_ref, own_ref, near_ref, *rest, count, block, head_dim
):
    arrived = rest[: count - 2]
    outs = rest[count - 2 : 2 * count - 2]
    value_all, out_all = rest[2 * count - 2 :]
    here = lax.axis_index("seq")

    def rows_of(b):
        return pl.ds(pl.multiple_of(b * block, block), block)

    value_all[rows_of(here)] = own_columns(own_ref, here, near_ref.shape[1])
    for step, piece in enumerate((near_ref, *arrived), 1):
        value_all[rows_of(here ^ step)] = piece[-block:]
    for h in range(value_all.shape[1] // head_dim):
        columns = slice(h * head_dim, (h + 1) * head_dim)
        for b in range(count):
            seen = (b + 1) * block
            total = mxu(weight_ref[h, b, :, :seen], value_all[:seen, columns])
            out_all[b, :, columns] = (total * part_ref[h, b]).astype(jnp.bfloat16)
    for step, out in enumerate(outs):
        out[...] = out_all[here ^ step]


def join_kernel(*rest, steps, width):
    pieces, out_ref, sem = rest[: len(steps)], rest[-2], rest[-1]
    here = lax.axis_index("seq")
    copies = []
    for n, (step, piece) in enumerate(zip(steps, pieces)):
        columns = pl.ds(pl.multiple_of((here ^ step) * width, width), width)
        copies.append(pltpu.make_async_copy(piece, out_ref.at[:, columns], sem.at[n]))
    for copy in copies:
        copy.start()
    for copy in copies:
        copy.wait()


WHOLE = pl.BlockSpec(memory_space=pltpu.VMEM)


def head_shards(
    gate_input, value_input, short_filter, long_filter, query_weight, key_matrix, value_matrix
):
    count = lax.axis_size("seq")
    block, local_width = gate_input.shape
    width = local_width // count
    heads = width // HEAD_DIM
    here = lax.axis_index("seq")
    groups = lax.axis_size("groups") if heads % lax.axis_size("groups") == 0 else 1

    def swap(value, step):
        return lax.ppermute(value, "seq", [(i, i ^ step) for i in range(count)])

    def packed(arrays, parts, after=()):
        return pl.pallas_call(
            functools.partial(pack_kernel, parts=parts, width=width),
            out_shape=[
                pltpu.VMEM((len(chosen) * block, columns), jnp.bfloat16)
                for _, columns, chosen in parts
            ],
            in_specs=[pl.BlockSpec(memory_space=pl.ANY)] * (len(arrays) + len(after)),
            out_specs=[WHOLE] * len(parts),
            scratch_shapes=[
                pltpu.SemaphoreType.DMA((sum(len(chosen) for *_, chosen in parts),))
            ],
            compiler_params=params,
        )(*[pltpu.with_memory_space_constraint(a, pltpu.HBM) for a in arrays], *after)

    ahead, back = block_tables(block)
    scratch = lambda n: pltpu.VMEM((n, block, width), jnp.bfloat16)
    params = pltpu.CompilerParams(vmem_limit_bytes=32 * 1024 * 1024)
    far = range(2, count)
    share = width // groups
    slots = range(groups)
    streams = [(i, slot) for i in (0, 1) for slot in slots] + [(2, None)]
    arrays = [gate_input, value_input, long_filter, key_matrix, value_matrix]
    first, near = packed(
        arrays, [(far[0], share, streams), (1, width, [(n, 0) for n in range(5)])]
    )
    near = swap(near, 1)
    pieces = packed(
        arrays,
        [(step, share, streams) for step in far[1:]]
        + [(step, width, [(3, 0), (4, 0)]) for step in far[:-1]]
        + [(far[-1], width, [(n, 0)]) for n in (3, 4)],
        after=[near],
    )
    arrived = [swap(piece, step) for step, piece in zip(far, [first, *pieces])]
    later = pieces[len(far) - 1 :]
    filters = [piece[-block:] for piece in arrived]
    shares = arrived + [
        lax.ppermute(piece, "groups", [(i, (i + shift) % groups) for i in range(groups)])
        for shift in range(1, groups)
        for piece in filters
    ]
    later = [swap(piece, step) for step, piece in zip([*far, far[-1]], later)]
    arrived_keys, arrived_values = later[:-1], [*later[:-2], later[-1]]
    tables = jnp.asarray(ahead), jnp.asarray(back)
    spectra = lambda n: (n, 2 * block, width)
    gate_spec, filter_spec, taps_spec = pl.pallas_call(
        functools.partial(local_kernel, block=block),
        out_shape=[
            jax.ShapeDtypeStruct(spectra(2), jnp.float32),
            jax.ShapeDtypeStruct(spectra(2), jnp.float32),
            jax.ShapeDtypeStruct((2 * block, width), jnp.float32),
        ],
        in_specs=[WHOLE] * 5,
        out_specs=[WHOLE] * 3,
        compiler_params=params,
    )(gate_input, long_filter, near, short_filter, tables[0])
    lines = pl.pallas_call(
        functools.partial(smooth_kernel, count=count, block=block),
        out_shape=jax.ShapeDtypeStruct(spectra(count), jnp.float32),
        in_specs=[WHOLE] * (count + 4),
        out_specs=WHOLE,
        scratch_shapes=[pltpu.VMEM(spectra(count), jnp.float32), scratch(count)],
        compiler_params=params,
    )(gate_spec, taps_spec, value_input, near, *arrived, *tables)
    queries = pl.pallas_call(
        functools.partial(
            conv_kernel, count=count, groups=groups, block=block, head_dim=HEAD_DIM
        ),
        out_shape=jax.ShapeDtypeStruct((count, block, width), jnp.bfloat16),
        in_specs=[WHOLE] * (groups * len(far) + 5),
        out_specs=WHOLE,
        scratch_shapes=[scratch(len(far)), pltpu.VMEM(spectra(count), jnp.float32)],
        compiler_params=params,
    )(lines, filter_spec, *shares, query_weight, *tables)
    weights, parts = pl.pallas_call(
        functools.partial(weigh_kernel, count=count, block=block, head_dim=HEAD_DIM),
        out_shape=[
            jax.ShapeDtypeStruct((heads, count, block, count * block), jnp.bfloat16),
            jax.ShapeDtypeStruct((heads, count, block, HEAD_DIM), jnp.float32),
        ],
        in_specs=[WHOLE] * (count + 1),
        out_specs=[WHOLE] * 2,
        scratch_shapes=[scratch(count)],
        compiler_params=params,
    )(queries, key_matrix, near, *arrived_keys)
    pieces = pl.pallas_call(
        functools.partial(sum_kernel, count=count, block=block, head_dim=HEAD_DIM),
        out_shape=[jax.ShapeDtypeStruct((block, width), jnp.bfloat16)] * count,
        in_specs=[WHOLE] * (count + 2),
        out_specs=[WHOLE] * count,
        scratch_shapes=[
            pltpu.VMEM((count * block, width), jnp.bfloat16),
            scratch(count),
        ],
        compiler_params=params,
    )(weights, parts, value_matrix, near, *arrived_values)
    swapped = {step: swap(pieces[step], step) for step in [*far, 1]}
    pieces = [pieces[0]] + [swapped[step] for step in range(1, count)]

    def joined(steps, *before):
        return pl.pallas_call(
            functools.partial(join_kernel, steps=steps, width=width),
            out_shape=pltpu.HBM((block, local_width), jnp.bfloat16),
            in_specs=[WHOLE] * len(steps) + [pl.BlockSpec(memory_space=pl.ANY)] * len(before),
            out_specs=pl.BlockSpec(memory_space=pl.ANY),
            scratch_shapes=[pltpu.SemaphoreType.DMA((len(steps),))],
            input_output_aliases={len(steps): 0} if before else {},
            compiler_params=params,
        )(*[pieces[step] for step in steps], *before)

    return joined(tuple(far), joined((0, 1)))


def shards(*arrays):
    count = lax.axis_size("seq")
    block, local_width = arrays[0].shape
    even = local_width % (count * HEAD_DIM) == 0
    if even and count > 1 and count & (count - 1) == 0 and block == TAPS:
        return head_shards(*arrays)
    return general_shards(*arrays)


def solution(mesh):
    in_specs = (
        P(("groups", "seq"), "chan"),
        P(("groups", "seq"), "chan"),
        P("chan", None),
        P("seq", "chan"),
        P("chan", None, None),
        P(("groups", "seq"), "chan"),
        P(("groups", "seq"), "chan"),
    )
    out_specs = P(("groups", "seq"), "chan")
    return jax.shard_map(shards, mesh=mesh, in_specs=in_specs, out_specs=out_specs, check_vma=False)
```

```python
import functools
import math

import jax
import jax.numpy as jnp
import ml_dtypes
import numpy as np
from jax import lax
from jax.experimental import pallas as pl
from jax.experimental.pallas import tpu as pltpu
from jax.sharding import PartitionSpec as P

HEAD_DIM = 128
TAPS = 128
RADIX = 128


HIGHEST = lax.Precision.HIGHEST


def shifted(value, axis, steps):
    count = lax.axis_size(axis)
    initial, last = (max(0, -steps), min(count, count - steps))
    return lax.ppermute(value, axis, [(source, source + steps) for source in range(initial, last)])


def unit_table(height, breadth, modulus, orient):
    product = (
        lax.broadcasted_iota(jnp.int32, (height, breadth), 0)
        * lax.broadcasted_iota(jnp.int32, (height, breadth), 1)
        % modulus
    )
    angles = 2.0 * math.pi / modulus * product.astype(jnp.float32)
    return (jnp.cos(angles), orient * jnp.sin(angles))


def block_table(factor, orient):
    inner_re, inner_im = unit_table(factor, factor, factor, orient)
    upper = jnp.concatenate([inner_re, inner_im], axis=1)
    lower = jnp.concatenate([-inner_im, inner_re], axis=1)
    return jnp.concatenate([upper, lower], axis=0)


def spectrum(signal, factor):
    channels, length = signal.shape
    full_length = 2 * length
    column_count = full_length // factor
    folded = signal.reshape(channels, column_count // 2, factor)
    outer_re, outer_im = unit_table(column_count, column_count // 2, column_count, -1.0)
    outer_both = jnp.concatenate([outer_re, outer_im], axis=0)
    first = jnp.einsum("kn,cnm->ckm", outer_both, folded, precision=HIGHEST)
    first_re = first[:, :column_count]
    first_im = first[:, column_count:]
    twist_re, twist_im = unit_table(column_count, factor, full_length, -1.0)
    mid_re = first_re * twist_re - first_im * twist_im
    mid_im = first_re * twist_im + first_im * twist_re
    joined = jnp.concatenate([mid_re, mid_im], axis=2)
    return jnp.einsum("ckn,nm->ckm", joined, block_table(factor, -1.0), precision=HIGHEST)


def inverse(spec_both, factor, length):
    channels = spec_both.shape[0]
    full_length = 2 * length
    column_count = full_length // factor
    mid = jnp.einsum("ckm,mn->ckn", spec_both, block_table(factor, 1.0), precision=HIGHEST)
    mid_re = mid[:, :, :factor]
    mid_im = mid[:, :, factor:]
    twist_re, twist_im = unit_table(column_count, factor, full_length, 1.0)
    turn_re = mid_re * twist_re - mid_im * twist_im
    turn_im = mid_re * twist_im + mid_im * twist_re
    outer_re, outer_im = unit_table(column_count // 2, column_count, column_count, 1.0)
    outer_both = jnp.concatenate([outer_re, -outer_im], axis=1)
    turned = jnp.concatenate([turn_re, turn_im], axis=1)
    result = jnp.einsum("nk,ckm->cnm", outer_both, turned, precision=HIGHEST)
    return result.reshape(channels, length) / full_length


def general_shards(
    gate_input, value_input, short_filter, long_filter, query_weight, key_matrix, value_matrix
):
    seq_rows, local_width = gate_input.shape
    last_rows = gate_input[seq_rows - (TAPS - 1) :]
    earlier = shifted(last_rows, "seq", 1)
    padded = jnp.concatenate([earlier, gate_input], axis=0).astype(jnp.float32)
    kernel = short_filter[:, ::-1].T[:, None, :]
    smoothed = lax.conv_general_dilated(
        padded[None],
        kernel,
        (1,),
        "VALID",
        dimension_numbers=("NHC", "HIO", "NHC"),
        feature_group_count=local_width,
        precision=HIGHEST,
    )[0]
    mixed_input = (smoothed * value_input.astype(jnp.float32)).astype(jnp.bfloat16)
    signal, kernel_line = (
        lax.all_to_all(mixed_input.T, "seq", split_axis=0, concat_axis=1, tiled=True),
        lax.all_to_all(long_filter.T, "seq", split_axis=0, concat_axis=1, tiled=True),
    )
    length = signal.shape[1]
    signal_both = spectrum(signal.astype(jnp.float32), RADIX)
    kernel_both = spectrum(kernel_line.astype(jnp.float32), RADIX)
    signal_re = signal_both[:, :, :RADIX]
    signal_im = signal_both[:, :, RADIX:]
    kernel_re = kernel_both[:, :, :RADIX]
    kernel_im = kernel_both[:, :, RADIX:]
    joint = jnp.concatenate(
        [
            signal_re * kernel_re - signal_im * kernel_im,
            signal_re * kernel_im + signal_im * kernel_re,
        ],
        axis=2,
    )
    conv_line = inverse(joint, RADIX, length).astype(jnp.bfloat16)
    my_index = lax.axis_index("seq")
    group_firsts = [my_index * seq_rows]
    conv_columns = lax.all_to_all(conv_line, "seq", split_axis=1, concat_axis=0, tiled=True)
    heads_here = local_width // HEAD_DIM
    conv_heads = conv_columns.reshape(heads_here, HEAD_DIM, seq_rows)
    query_heads = jnp.einsum(
        "hds,hde->hse", conv_heads, query_weight, preferred_element_type=jnp.float32
    ).astype(jnp.bfloat16)
    group_count = len(group_firsts)
    query_groups = [query_heads]
    key_heads = key_matrix.reshape(seq_rows, heads_here, HEAD_DIM).transpose(1, 0, 2)
    value_heads = value_matrix.reshape(seq_rows, heads_here, HEAD_DIM).transpose(1, 0, 2)
    score_scale = 1.0 / math.sqrt(HEAD_DIM)

    def attend_group(running, group_query, group_first, key_block, value_block, first_row):
        block_rows = key_block.shape[1]

        def compute(current):
            peak_value, weight_sum, weighted = current
            scores = (
                jnp.einsum(
                    "hqd,hkd->hqk", group_query, key_block, preferred_element_type=jnp.float32
                )
                * score_scale
            )
            key_pos = first_row + lax.iota(jnp.int32, block_rows)
            query_pos = group_first + lax.iota(jnp.int32, seq_rows)
            allowed = (key_pos[None, :] <= query_pos[:, None])[None]
            scores = jnp.where(allowed, scores, -1e30)
            new_peak = jnp.maximum(peak_value, jnp.max(scores, axis=2))
            weights = jnp.where(allowed, jnp.exp(scores - new_peak[:, :, None]), 0.0)
            rescale = jnp.exp(peak_value - new_peak)
            weight_sum = weight_sum * rescale + jnp.sum(weights, axis=2)
            weighted = weighted * rescale[:, :, None] + jnp.einsum(
                "hqk,hkd->hqd",
                weights.astype(jnp.bfloat16),
                value_block,
                preferred_element_type=jnp.float32,
            )
            return (new_peak, weight_sum, weighted)

        live = first_row <= group_first + seq_rows - 1
        return lax.cond(live, compute, lambda current: current, running)

    def attend(states, key_block, value_block, first_row):
        return tuple(
            (
                attend_group(
                    states[g], query_groups[g], group_firsts[g], key_block, value_block, first_row
                )
                for g in range(group_count)
            )
        )

    one_state = (
        jnp.full((heads_here, seq_rows), -1e30, jnp.float32),
        jnp.zeros((heads_here, seq_rows), jnp.float32),
        jnp.zeros((heads_here, seq_rows, HEAD_DIM), jnp.float32),
    )
    initial = tuple((one_state for g in range(group_count)))
    running = initial
    key_piece = lax.all_gather(key_heads, "seq", axis=1, tiled=True)
    value_piece = lax.all_gather(value_heads, "seq", axis=1, tiled=True)
    piece_rows = key_piece.shape[1]
    block_rows = 512
    block_count = piece_rows // block_rows
    key_blocks = key_piece.reshape(heads_here, block_count, block_rows, HEAD_DIM).transpose(
        1, 0, 2, 3
    )
    value_blocks = value_piece.reshape(heads_here, block_count, block_rows, HEAD_DIM).transpose(
        1, 0, 2, 3
    )

    def advance(current, element):
        key_block, value_block, position = element
        return (attend(current, key_block, value_block, position * block_rows), None)

    running, _ = lax.scan(
        advance, running, (key_blocks, value_blocks, lax.iota(jnp.int32, block_count))
    )
    outputs = [state[2] / state[1][:, :, None] for state in running]
    result = outputs[0]
    attended_rows = result.transpose(1, 0, 2).reshape(seq_rows, local_width).astype(jnp.bfloat16)
    return attended_rows


def block_tables(block):
    angle = np.pi / block * (np.arange(block) + 0.5)
    turns = angle[:, None] * np.arange(block)[None]
    ahead = np.concatenate([np.cos(turns), -np.sin(turns)], axis=0)
    back = np.concatenate([np.cos(turns.T), -np.sin(turns.T)], axis=1) / block

    def pair(table):
        high = table.astype(ml_dtypes.bfloat16)
        rest = (table - high.astype(np.float64)).astype(ml_dtypes.bfloat16)
        return np.concatenate([high, rest], axis=0)

    return pair(ahead), pair(back)


def two_parts(value):
    high = value.astype(jnp.bfloat16)
    return high, (value - high.astype(jnp.float32)).astype(jnp.bfloat16)


def mxu(left, right):
    return jnp.dot(left, right, preferred_element_type=jnp.float32)


def folded_sum(stacked):
    half = stacked.shape[0] // 2
    return stacked[:half] + stacked[half:]


def wide_mxu(table, value):
    half = table.shape[0] // 2
    wide = jnp.concatenate([table[:half], table[half:]], axis=1)
    return mxu(wide, jnp.concatenate([value, value], axis=0))


def to_blocks(back, spectra, block):
    parts = [two_parts(jnp.concatenate(spec, axis=0)) for spec in spectra]
    main = [mxu(back, high) for high, _ in parts]
    small = [mxu(back[:block], rest) for _, rest in parts]
    return [folded_sum(large) + rest for large, rest in zip(main, small)]


def pack_kernel(*rest, parts, width):
    outs, sem = rest[-len(parts) - 1 : -1], rest[-1]
    here, group = lax.axis_index("seq"), lax.axis_index("groups")
    copies = []
    for (step, columns, blocks), out in zip(parts, outs):
        for n, (i, slot) in enumerate(blocks):
            start = (here ^ step) * width + (group if slot is None else slot) * columns
            source = rest[i].at[:, pl.ds(pl.multiple_of(start, HEAD_DIM), columns)]
            rows = source.shape[0]
            copies.append(
                pltpu.make_async_copy(
                    source, out.at[n * rows : (n + 1) * rows], sem.at[len(copies)]
                )
            )
    for copy in copies:
        copy.start()
    for copy in copies:
        copy.wait()


def own_columns(ref, here, width):
    return ref[:, pl.ds(pl.multiple_of(here * width, width), width)]


def with_block_before(spec, before, block):
    odd = lax.broadcasted_iota(jnp.int32, (block, spec.shape[1]), 0) % 2
    sign = 1.0 - 2.0 * odd.astype(jnp.float32)
    return spec[:block] - sign * before[block:], spec[block:] + sign * before[:block]


def local_kernel(gate_ref, filter_ref, near_ref, taps_ref, ahead_ref, *outs, block):
    gate_spec_ref, filter_spec_ref, taps_spec_ref = outs
    here = lax.axis_index("seq")
    width = near_ref.shape[1]
    ahead = ahead_ref[...]
    gate_spec_ref[0] = wide_mxu(ahead, own_columns(gate_ref, here, width))
    gate_spec_ref[1] = wide_mxu(ahead, near_ref[:block])
    filter_spec_ref[0] = wide_mxu(ahead, own_columns(filter_ref, here, width))
    filter_spec_ref[1] = wide_mxu(ahead, near_ref[2 * block : 3 * block])
    turned = (((1,), (1,)), ((), ()))
    taps = taps_ref[pl.ds(pl.multiple_of(here * width, width), width)]
    taps_high, taps_rest = two_parts(taps)
    taps_spec_ref[...] = folded_sum(
        lax.dot_general(ahead, taps_high, turned, preferred_element_type=jnp.float32)
    ) + lax.dot_general(
        ahead[: 2 * block], taps_rest, turned, preferred_element_type=jnp.float32
    )


def smooth_kernel(gate_spec_ref, taps_spec_ref, value_ref, near_ref, *rest, count, block):
    arrived = rest[: count - 2]
    ahead_ref, back_ref, line_ref, gate_all, value_all = rest[count - 2 :]
    here = lax.axis_index("seq")
    width = near_ref.shape[1]
    ahead = ahead_ref[...]
    back = back_ref[...]
    value_all[here] = own_columns(value_ref, here, width)
    value_all[here ^ 1] = near_ref[block : 2 * block]
    gate_all[here] = gate_spec_ref[0]
    gate_all[here ^ 1] = gate_spec_ref[1]
    for step, piece in enumerate(arrived, 2):
        columns = piece.shape[1]
        slots = width // columns

        def joined(first):
            return jnp.concatenate(
                [piece[n * block : (n + 1) * block] for n in range(first, first + slots)], axis=1
            )

        gate_all[here ^ step] = wide_mxu(ahead, joined(0))
        value_all[here ^ step] = joined(slots)
    taps_re, taps_im = taps_spec_ref[:block], taps_spec_ref[block:]
    spectra = []
    for b in range(count):
        gate_spec = gate_all[b]
        if b > 0:
            gate_re, gate_im = with_block_before(gate_spec, gate_all[b - 1], block)
        else:
            gate_re, gate_im = gate_spec[:block], gate_spec[block:]
        spectra.append(
            (gate_re * taps_re - gate_im * taps_im, gate_re * taps_im + gate_im * taps_re)
        )
    mixed = [
        (smoothed * value_all[b].astype(jnp.float32)).astype(jnp.bfloat16)
        for b, smoothed in enumerate(to_blocks(back, spectra, block))
    ]
    for b in range(count):
        line_ref[b] = wide_mxu(ahead, mixed[b])


def share_start(shift, columns, groups):
    group = lax.axis_index("groups") if groups > 1 else 0
    return pl.multiple_of(lax.rem(group + groups - shift, groups) * columns, HEAD_DIM)


def conv_kernel(line_ref, filter_spec_ref, *rest, count, groups, shift, block, head_dim):
    far = count - 2
    arrived = rest[:far]
    weight_ref, ahead_ref, back_ref, query_ref, spec_all = rest[far:]
    here = lax.axis_index("seq")
    width = line_ref.shape[2]
    columns = width // groups
    start = share_start(shift, columns, groups)
    chosen = pl.ds(start, columns)
    ahead = ahead_ref[...]
    back = back_ref[...]
    first_head = here * (width // head_dim) + start // head_dim
    spec_all[here] = filter_spec_ref[0, :, chosen]
    spec_all[here ^ 1] = filter_spec_ref[1, :, chosen]
    for step, piece in enumerate(arrived, 2):
        spec_all[here ^ step] = wide_mxu(ahead, piece[piece.shape[0] - block :])
    lines = [(line_ref[b, :block, chosen], line_ref[b, block:, chosen]) for b in range(count)]
    kernels = [(spec_all[0, :block], spec_all[0, block:])] + [
        with_block_before(spec_all[b], spec_all[b - 1], block) for b in range(1, count)
    ]
    totals = []
    for b in range(count):
        total_re, total_im = 0.0, 0.0
        for j in range(b + 1):
            line_re, line_im = lines[j]
            kernel_re, kernel_im = kernels[b - j]
            total_re = total_re + (line_re * kernel_re - line_im * kernel_im)
            total_im = total_im + (line_re * kernel_im + line_im * kernel_re)
        totals.append((total_re, total_im))
    for b, conv_out in enumerate(to_blocks(back, totals, block)):
        conv_out = conv_out.astype(jnp.bfloat16)
        for h in range(columns // head_dim):
            part = slice(h * head_dim, (h + 1) * head_dim)
            query_ref[b, :, part] = mxu(conv_out[:, part], weight_ref[first_head + h]).astype(
                jnp.bfloat16
            )


def weigh_kernel(own_ref, near_ref, *rest, count, groups, block, head_dim):
    arrived, queries = rest[: count - 2], rest[count - 2 : count - 2 + groups]
    weight_ref, part_ref, key_all = rest[count - 2 + groups :]
    here = lax.axis_index("seq")
    key_all[here] = own_columns(own_ref, here, near_ref.shape[1])
    for step, piece in enumerate((near_ref, *arrived), 1):
        first = max(piece.shape[0] - 2 * block, 0)
        key_all[here ^ step] = piece[first : first + block]
    turned = (((1,), (1,)), ((), ()))
    scale = math.log2(math.e) / math.sqrt(head_dim)
    row = lax.broadcasted_iota(jnp.int32, (block, block), 0)
    column = lax.broadcasted_iota(jnp.int32, (block, block), 1)
    allowed = column <= row
    share = queries[0].shape[2]
    heads = share // head_dim
    places = [(h, b) for h in range(groups * heads) for b in range(count)]
    scores = {place: [] for place in places}
    for h in range(groups * heads):
        shift, part = divmod(h, heads)
        query = jnp.concatenate(
            [queries[shift][b, :, part * head_dim : (part + 1) * head_dim] for b in range(count)],
            axis=0,
        )
        columns = pl.ds(share_start(shift, share, groups) + part * head_dim, head_dim)
        for j in range(count):
            later = lax.dot_general(
                query[j * block :],
                key_all[j, :, columns],
                turned,
                preferred_element_type=jnp.float32,
            )
            for b in range(j, count):
                score = later[(b - j) * block : (b - j + 1) * block]
                scores[h, b].append(jnp.where(allowed, score, -1e30) if j == b else score)
    peaks = {
        place: jnp.max(functools.reduce(jnp.maximum, parts), axis=1, keepdims=True)
        for place, parts in scores.items()
    }
    sums = {}
    for h, b in places:
        weights = [jnp.exp2((score - peaks[h, b]) * scale) for score in scores[h, b]]
        weights[b] = jnp.where(allowed, weights[b], 0.0)
        sums[h, b] = jnp.sum(functools.reduce(jnp.add, weights), axis=1, keepdims=True)
        for j in range(b + 1):
            weight_ref[h, b, :, j * block : (j + 1) * block] = weights[j].astype(jnp.bfloat16)
    for h, b in places:
        part_ref[h, b] = jnp.broadcast_to(1.0 / sums[h, b], (block, head_dim))


def sum_kernel(weight_ref, part_ref, own_ref, near_ref, *rest, count, groups, block, head_dim):
    arrived = rest[: count - 2]
    outs = rest[count - 2 : 2 * count - 2]
    value_all, out_all = rest[2 * count - 2 :]
    here = lax.axis_index("seq")

    def rows_of(b):
        return pl.ds(pl.multiple_of(b * block, block), block)

    value_all[rows_of(here)] = own_columns(own_ref, here, near_ref.shape[1])
    for step, piece in enumerate((near_ref, *arrived), 1):
        value_all[rows_of(here ^ step)] = piece[-block:]
    share = value_all.shape[1] // groups
    for h in range(weight_ref.shape[0]):
        shift, part = divmod(h, share // head_dim)
        columns = pl.ds(share_start(shift, share, groups) + part * head_dim, head_dim)
        for b in range(count):
            seen = (b + 1) * block
            total = mxu(weight_ref[h, b, :, :seen], value_all[:seen, columns])
            out_all[b, :, columns] = (total * part_ref[h, b]).astype(jnp.bfloat16)
    for step, out in enumerate(outs):
        out[...] = out_all[here ^ step]


def join_kernel(*rest, steps, width):
    pieces, out_ref, sem = rest[: len(steps)], rest[-2], rest[-1]
    here = lax.axis_index("seq")
    copies = []
    for n, (step, piece) in enumerate(zip(steps, pieces)):
        columns = pl.ds(pl.multiple_of((here ^ step) * width, width), width)
        copies.append(pltpu.make_async_copy(piece, out_ref.at[:, columns], sem.at[n]))
    for copy in copies:
        copy.start()
    for copy in copies:
        copy.wait()


WHOLE = pl.BlockSpec(memory_space=pltpu.VMEM)


def head_shards(
    gate_input, value_input, short_filter, long_filter, query_weight, key_matrix, value_matrix
):
    count = lax.axis_size("seq")
    block, local_width = gate_input.shape
    width = local_width // count
    heads = width // HEAD_DIM
    here = lax.axis_index("seq")
    groups = lax.axis_size("groups") if heads % lax.axis_size("groups") == 0 else 1

    def swap(value, step):
        return lax.ppermute(value, "seq", [(i, i ^ step) for i in range(count)])

    def packed(arrays, parts, after=()):
        return pl.pallas_call(
            functools.partial(pack_kernel, parts=parts, width=width),
            out_shape=[
                pltpu.VMEM((len(chosen) * block, columns), jnp.bfloat16)
                for _, columns, chosen in parts
            ],
            in_specs=[pl.BlockSpec(memory_space=pl.ANY)] * (len(arrays) + len(after)),
            out_specs=[WHOLE] * len(parts),
            scratch_shapes=[
                pltpu.SemaphoreType.DMA((sum(len(chosen) for *_, chosen in parts),))
            ],
            compiler_params=params,
        )(*[pltpu.with_memory_space_constraint(a, pltpu.HBM) for a in arrays], *after)

    ahead, back = block_tables(block)
    scratch = lambda n: pltpu.VMEM((n, block, width), jnp.bfloat16)
    params = pltpu.CompilerParams(vmem_limit_bytes=32 * 1024 * 1024)
    far = range(2, count)
    share = width // groups
    slots = range(groups)
    streams = [(i, slot) for i in (0, 1) for slot in slots] + [(2, None)]
    arrays = [gate_input, value_input, long_filter, key_matrix, value_matrix]
    first, near = packed(
        arrays, [(far[0], share, streams), (1, width, [(n, 0) for n in range(5)])]
    )
    near = swap(near, 1)
    pieces = packed(
        arrays,
        [(step, share, streams) for step in far[1:]]
        + [(step, width, [(3, 0), (4, 0)]) for step in far[:-1]]
        + [(far[-1], width, [(n, 0)]) for n in (3, 4)],
        after=[near],
    )
    arrived = [swap(piece, step) for step, piece in zip(far, [first, *pieces])]
    later = pieces[len(far) - 1 :]
    tables = jnp.asarray(ahead), jnp.asarray(back)
    spectra = lambda n: (n, 2 * block, width)
    gate_spec, filter_spec, taps_spec = pl.pallas_call(
        functools.partial(local_kernel, block=block),
        out_shape=[
            jax.ShapeDtypeStruct(spectra(2), jnp.float32),
            jax.ShapeDtypeStruct(spectra(2), jnp.float32),
            jax.ShapeDtypeStruct((2 * block, width), jnp.float32),
        ],
        in_specs=[WHOLE] * 5,
        out_specs=[WHOLE] * 3,
        compiler_params=params,
    )(gate_input, long_filter, near, short_filter, tables[0])
    filters = [piece[-block:] for piece in arrived]
    filters[0], taps_spec = lax.optimization_barrier((filters[0], taps_spec))
    shares = [arrived] + [
        [
            lax.ppermute(piece, "groups", [(i, (i + shift) % groups) for i in range(groups)])
            for piece in filters
        ]
        for shift in range(1, groups)
    ]
    later = [swap(piece, step) for step, piece in zip([*far, far[-1]], later)]
    arrived_keys, arrived_values = later[:-1], [*later[:-2], later[-1]]
    lines = pl.pallas_call(
        functools.partial(smooth_kernel, count=count, block=block),
        out_shape=jax.ShapeDtypeStruct(spectra(count), jnp.float32),
        in_specs=[WHOLE] * (count + 4),
        out_specs=WHOLE,
        scratch_shapes=[pltpu.VMEM(spectra(count), jnp.float32), scratch(count)],
        compiler_params=params,
    )(gate_spec, taps_spec, value_input, near, *arrived, *tables)
    queries = [
        pl.pallas_call(
            functools.partial(
                conv_kernel,
                count=count,
                groups=groups,
                shift=shift,
                block=block,
                head_dim=HEAD_DIM,
            ),
            out_shape=jax.ShapeDtypeStruct((count, block, share), jnp.bfloat16),
            in_specs=[WHOLE] * (len(far) + 5),
            out_specs=WHOLE,
            scratch_shapes=[pltpu.VMEM((count, 2 * block, share), jnp.float32)],
            compiler_params=params,
        )(lines, filter_spec, *pieces, query_weight, *tables)
        for shift, pieces in enumerate(shares)
    ]
    weights, parts = pl.pallas_call(
        functools.partial(
            weigh_kernel, count=count, groups=groups, block=block, head_dim=HEAD_DIM
        ),
        out_shape=[
            jax.ShapeDtypeStruct((heads, count, block, count * block), jnp.bfloat16),
            jax.ShapeDtypeStruct((heads, count, block, HEAD_DIM), jnp.float32),
        ],
        in_specs=[WHOLE] * (count + groups),
        out_specs=[WHOLE] * 2,
        scratch_shapes=[scratch(count)],
        compiler_params=params,
    )(key_matrix, near, *arrived_keys, *queries)
    pieces = pl.pallas_call(
        functools.partial(
            sum_kernel, count=count, groups=groups, block=block, head_dim=HEAD_DIM
        ),
        out_shape=[jax.ShapeDtypeStruct((block, width), jnp.bfloat16)] * count,
        in_specs=[WHOLE] * (count + 2),
        out_specs=[WHOLE] * count,
        scratch_shapes=[
            pltpu.VMEM((count * block, width), jnp.bfloat16),
            scratch(count),
        ],
        compiler_params=params,
    )(weights, parts, value_matrix, near, *arrived_values)
    swapped = {step: swap(pieces[step], step) for step in [*far, 1]}
    pieces = [pieces[0]] + [swapped[step] for step in range(1, count)]

    def joined(steps, *before):
        return pl.pallas_call(
            functools.partial(join_kernel, steps=steps, width=width),
            out_shape=pltpu.HBM((block, local_width), jnp.bfloat16),
            in_specs=[WHOLE] * len(steps) + [pl.BlockSpec(memory_space=pl.ANY)] * len(before),
            out_specs=pl.BlockSpec(memory_space=pl.ANY),
            scratch_shapes=[pltpu.SemaphoreType.DMA((len(steps),))],
            input_output_aliases={len(steps): 0} if before else {},
            compiler_params=params,
        )(*[pieces[step] for step in steps], *before)

    return joined(tuple(far), joined((0, 1)))


def shards(*arrays):
    count = lax.axis_size("seq")
    block, local_width = arrays[0].shape
    even = local_width % (count * HEAD_DIM) == 0
    if even and count > 1 and count & (count - 1) == 0 and block == TAPS:
        return head_shards(*arrays)
    return general_shards(*arrays)


def solution(mesh):
    in_specs = (
        P(("groups", "seq"), "chan"),
        P(("groups", "seq"), "chan"),
        P("chan", None),
        P("seq", "chan"),
        P("chan", None, None),
        P(("groups", "seq"), "chan"),
        P(("groups", "seq"), "chan"),
    )
    out_specs = P(("groups", "seq"), "chan")
    return jax.shard_map(shards, mesh=mesh, in_specs=in_specs, out_specs=out_specs, check_vma=False)
```

```python
import functools
import math

import jax
import jax.numpy as jnp
import ml_dtypes
import numpy as np
from jax import lax
from jax.experimental import pallas as pl
from jax.experimental.pallas import tpu as pltpu
from jax.sharding import PartitionSpec as P

HEAD_DIM = 128
TAPS = 128
RADIX = 128


HIGHEST = lax.Precision.HIGHEST


def shifted(value, axis, steps):
    count = lax.axis_size(axis)
    initial, last = (max(0, -steps), min(count, count - steps))
    return lax.ppermute(value, axis, [(source, source + steps) for source in range(initial, last)])


def unit_table(height, breadth, modulus, orient):
    product = (
        lax.broadcasted_iota(jnp.int32, (height, breadth), 0)
        * lax.broadcasted_iota(jnp.int32, (height, breadth), 1)
        % modulus
    )
    angles = 2.0 * math.pi / modulus * product.astype(jnp.float32)
    return (jnp.cos(angles), orient * jnp.sin(angles))


def block_table(factor, orient):
    inner_re, inner_im = unit_table(factor, factor, factor, orient)
    upper = jnp.concatenate([inner_re, inner_im], axis=1)
    lower = jnp.concatenate([-inner_im, inner_re], axis=1)
    return jnp.concatenate([upper, lower], axis=0)


def spectrum(signal, factor):
    channels, length = signal.shape
    full_length = 2 * length
    column_count = full_length // factor
    folded = signal.reshape(channels, column_count // 2, factor)
    outer_re, outer_im = unit_table(column_count, column_count // 2, column_count, -1.0)
    outer_both = jnp.concatenate([outer_re, outer_im], axis=0)
    first = jnp.einsum("kn,cnm->ckm", outer_both, folded, precision=HIGHEST)
    first_re = first[:, :column_count]
    first_im = first[:, column_count:]
    twist_re, twist_im = unit_table(column_count, factor, full_length, -1.0)
    mid_re = first_re * twist_re - first_im * twist_im
    mid_im = first_re * twist_im + first_im * twist_re
    joined = jnp.concatenate([mid_re, mid_im], axis=2)
    return jnp.einsum("ckn,nm->ckm", joined, block_table(factor, -1.0), precision=HIGHEST)


def inverse(spec_both, factor, length):
    channels = spec_both.shape[0]
    full_length = 2 * length
    column_count = full_length // factor
    mid = jnp.einsum("ckm,mn->ckn", spec_both, block_table(factor, 1.0), precision=HIGHEST)
    mid_re = mid[:, :, :factor]
    mid_im = mid[:, :, factor:]
    twist_re, twist_im = unit_table(column_count, factor, full_length, 1.0)
    turn_re = mid_re * twist_re - mid_im * twist_im
    turn_im = mid_re * twist_im + mid_im * twist_re
    outer_re, outer_im = unit_table(column_count // 2, column_count, column_count, 1.0)
    outer_both = jnp.concatenate([outer_re, -outer_im], axis=1)
    turned = jnp.concatenate([turn_re, turn_im], axis=1)
    result = jnp.einsum("nk,ckm->cnm", outer_both, turned, precision=HIGHEST)
    return result.reshape(channels, length) / full_length


def general_shards(
    gate_input, value_input, short_filter, long_filter, query_weight, key_matrix, value_matrix
):
    seq_rows, local_width = gate_input.shape
    last_rows = gate_input[seq_rows - (TAPS - 1) :]
    earlier = shifted(last_rows, "seq", 1)
    padded = jnp.concatenate([earlier, gate_input], axis=0).astype(jnp.float32)
    kernel = short_filter[:, ::-1].T[:, None, :]
    smoothed = lax.conv_general_dilated(
        padded[None],
        kernel,
        (1,),
        "VALID",
        dimension_numbers=("NHC", "HIO", "NHC"),
        feature_group_count=local_width,
        precision=HIGHEST,
    )[0]
    mixed_input = (smoothed * value_input.astype(jnp.float32)).astype(jnp.bfloat16)
    signal, kernel_line = (
        lax.all_to_all(mixed_input.T, "seq", split_axis=0, concat_axis=1, tiled=True),
        lax.all_to_all(long_filter.T, "seq", split_axis=0, concat_axis=1, tiled=True),
    )
    length = signal.shape[1]
    signal_both = spectrum(signal.astype(jnp.float32), RADIX)
    kernel_both = spectrum(kernel_line.astype(jnp.float32), RADIX)
    signal_re = signal_both[:, :, :RADIX]
    signal_im = signal_both[:, :, RADIX:]
    kernel_re = kernel_both[:, :, :RADIX]
    kernel_im = kernel_both[:, :, RADIX:]
    joint = jnp.concatenate(
        [
            signal_re * kernel_re - signal_im * kernel_im,
            signal_re * kernel_im + signal_im * kernel_re,
        ],
        axis=2,
    )
    conv_line = inverse(joint, RADIX, length).astype(jnp.bfloat16)
    my_index = lax.axis_index("seq")
    group_firsts = [my_index * seq_rows]
    conv_columns = lax.all_to_all(conv_line, "seq", split_axis=1, concat_axis=0, tiled=True)
    heads_here = local_width // HEAD_DIM
    conv_heads = conv_columns.reshape(heads_here, HEAD_DIM, seq_rows)
    query_heads = jnp.einsum(
        "hds,hde->hse", conv_heads, query_weight, preferred_element_type=jnp.float32
    ).astype(jnp.bfloat16)
    group_count = len(group_firsts)
    query_groups = [query_heads]
    key_heads = key_matrix.reshape(seq_rows, heads_here, HEAD_DIM).transpose(1, 0, 2)
    value_heads = value_matrix.reshape(seq_rows, heads_here, HEAD_DIM).transpose(1, 0, 2)
    score_scale = 1.0 / math.sqrt(HEAD_DIM)

    def attend_group(running, group_query, group_first, key_block, value_block, first_row):
        block_rows = key_block.shape[1]

        def compute(current):
            peak_value, weight_sum, weighted = current
            scores = (
                jnp.einsum(
                    "hqd,hkd->hqk", group_query, key_block, preferred_element_type=jnp.float32
                )
                * score_scale
            )
            key_pos = first_row + lax.iota(jnp.int32, block_rows)
            query_pos = group_first + lax.iota(jnp.int32, seq_rows)
            allowed = (key_pos[None, :] <= query_pos[:, None])[None]
            scores = jnp.where(allowed, scores, -1e30)
            new_peak = jnp.maximum(peak_value, jnp.max(scores, axis=2))
            weights = jnp.where(allowed, jnp.exp(scores - new_peak[:, :, None]), 0.0)
            rescale = jnp.exp(peak_value - new_peak)
            weight_sum = weight_sum * rescale + jnp.sum(weights, axis=2)
            weighted = weighted * rescale[:, :, None] + jnp.einsum(
                "hqk,hkd->hqd",
                weights.astype(jnp.bfloat16),
                value_block,
                preferred_element_type=jnp.float32,
            )
            return (new_peak, weight_sum, weighted)

        live = first_row <= group_first + seq_rows - 1
        return lax.cond(live, compute, lambda current: current, running)

    def attend(states, key_block, value_block, first_row):
        return tuple(
            (
                attend_group(
                    states[g], query_groups[g], group_firsts[g], key_block, value_block, first_row
                )
                for g in range(group_count)
            )
        )

    one_state = (
        jnp.full((heads_here, seq_rows), -1e30, jnp.float32),
        jnp.zeros((heads_here, seq_rows), jnp.float32),
        jnp.zeros((heads_here, seq_rows, HEAD_DIM), jnp.float32),
    )
    initial = tuple((one_state for g in range(group_count)))
    running = initial
    key_piece = lax.all_gather(key_heads, "seq", axis=1, tiled=True)
    value_piece = lax.all_gather(value_heads, "seq", axis=1, tiled=True)
    piece_rows = key_piece.shape[1]
    block_rows = 512
    block_count = piece_rows // block_rows
    key_blocks = key_piece.reshape(heads_here, block_count, block_rows, HEAD_DIM).transpose(
        1, 0, 2, 3
    )
    value_blocks = value_piece.reshape(heads_here, block_count, block_rows, HEAD_DIM).transpose(
        1, 0, 2, 3
    )

    def advance(current, element):
        key_block, value_block, position = element
        return (attend(current, key_block, value_block, position * block_rows), None)

    running, _ = lax.scan(
        advance, running, (key_blocks, value_blocks, lax.iota(jnp.int32, block_count))
    )
    outputs = [state[2] / state[1][:, :, None] for state in running]
    result = outputs[0]
    attended_rows = result.transpose(1, 0, 2).reshape(seq_rows, local_width).astype(jnp.bfloat16)
    return attended_rows


def block_tables(block):
    angle = np.pi / block * (np.arange(block) + 0.5)
    turns = angle[:, None] * np.arange(block)[None]
    ahead = np.concatenate([np.cos(turns), -np.sin(turns)], axis=0)
    back = np.concatenate([np.cos(turns.T), -np.sin(turns.T)], axis=1) / block

    def pair(table):
        high = table.astype(ml_dtypes.bfloat16)
        rest = (table - high.astype(np.float64)).astype(ml_dtypes.bfloat16)
        return np.concatenate([high, rest], axis=0)

    return pair(ahead), pair(back)


def two_parts(value):
    high = value.astype(jnp.bfloat16)
    return high, (value - high.astype(jnp.float32)).astype(jnp.bfloat16)


def mxu(left, right):
    return jnp.dot(left, right, preferred_element_type=jnp.float32)


def folded_sum(stacked):
    half = stacked.shape[0] // 2
    return stacked[:half] + stacked[half:]


def wide_mxu(table, value):
    half = table.shape[0] // 2
    wide = jnp.concatenate([table[:half], table[half:]], axis=1)
    return mxu(wide, jnp.concatenate([value, value], axis=0))


def to_blocks(back, spectra, block):
    parts = [two_parts(jnp.concatenate(spec, axis=0)) for spec in spectra]
    main = [mxu(back, high) for high, _ in parts]
    small = [mxu(back[:block], rest) for _, rest in parts]
    return [folded_sum(large) + rest for large, rest in zip(main, small)]


def pack_kernel(*rest, parts, width):
    outs, sem = rest[-len(parts) - 1 : -1], rest[-1]
    here, group = lax.axis_index("seq"), lax.axis_index("groups")
    copies = []
    for (step, columns, blocks), out in zip(parts, outs):
        for n, (i, slot) in enumerate(blocks):
            start = (here ^ step) * width + (group if slot is None else slot) * columns
            source = rest[i].at[:, pl.ds(pl.multiple_of(start, HEAD_DIM), columns)]
            rows = source.shape[0]
            copies.append(
                pltpu.make_async_copy(
                    source, out.at[n * rows : (n + 1) * rows], sem.at[len(copies)]
                )
            )
    for copy in copies:
        copy.start()
    for copy in copies:
        copy.wait()


def own_columns(ref, here, width):
    return ref[:, pl.ds(pl.multiple_of(here * width, width), width)]


def with_block_before(spec, before, block):
    odd = lax.broadcasted_iota(jnp.int32, (block, spec.shape[1]), 0) % 2
    sign = 1.0 - 2.0 * odd.astype(jnp.float32)
    return spec[:block] - sign * before[block:], spec[block:] + sign * before[:block]


def local_kernel(gate_ref, filter_ref, near_ref, taps_ref, ahead_ref, *outs, block):
    gate_spec_ref, filter_spec_ref, taps_spec_ref = outs
    here = lax.axis_index("seq")
    width = near_ref.shape[1]
    ahead = ahead_ref[...]
    gate_spec_ref[0] = wide_mxu(ahead, own_columns(gate_ref, here, width))
    gate_spec_ref[1] = wide_mxu(ahead, near_ref[:block])
    filter_spec_ref[0] = wide_mxu(ahead, own_columns(filter_ref, here, width))
    filter_spec_ref[1] = wide_mxu(ahead, near_ref[2 * block : 3 * block])
    turned = (((1,), (1,)), ((), ()))
    taps = taps_ref[pl.ds(pl.multiple_of(here * width, width), width)]
    taps_high, taps_rest = two_parts(taps)
    taps_spec_ref[...] = folded_sum(
        lax.dot_general(ahead, taps_high, turned, preferred_element_type=jnp.float32)
    ) + lax.dot_general(
        ahead[: 2 * block], taps_rest, turned, preferred_element_type=jnp.float32
    )


def smooth_kernel(gate_spec_ref, taps_spec_ref, value_ref, near_ref, *rest, count, block):
    arrived = rest[: count - 2]
    ahead_ref, back_ref, line_ref, gate_all, value_all = rest[count - 2 :]
    here = lax.axis_index("seq")
    width = near_ref.shape[1]
    ahead = ahead_ref[...]
    back = back_ref[...]
    value_all[here] = own_columns(value_ref, here, width)
    value_all[here ^ 1] = near_ref[block : 2 * block]
    gate_all[here] = gate_spec_ref[0]
    gate_all[here ^ 1] = gate_spec_ref[1]
    for step, piece in enumerate(arrived, 2):
        columns = piece.shape[1]
        slots = width // columns

        def joined(first):
            return jnp.concatenate(
                [piece[n * block : (n + 1) * block] for n in range(first, first + slots)], axis=1
            )

        gate_all[here ^ step] = wide_mxu(ahead, joined(0))
        value_all[here ^ step] = joined(slots)
    taps_re, taps_im = taps_spec_ref[:block], taps_spec_ref[block:]
    spectra = []
    for b in range(count):
        gate_spec = gate_all[b]
        if b > 0:
            gate_re, gate_im = with_block_before(gate_spec, gate_all[b - 1], block)
        else:
            gate_re, gate_im = gate_spec[:block], gate_spec[block:]
        spectra.append(
            (gate_re * taps_re - gate_im * taps_im, gate_re * taps_im + gate_im * taps_re)
        )
    mixed = [
        (smoothed * value_all[b].astype(jnp.float32)).astype(jnp.bfloat16)
        for b, smoothed in enumerate(to_blocks(back, spectra, block))
    ]
    for b in range(count):
        line_ref[b] = wide_mxu(ahead, mixed[b])


def share_start(shift, columns, groups):
    group = lax.axis_index("groups") if groups > 1 else 0
    return pl.multiple_of(lax.rem(group + groups - shift, groups) * columns, HEAD_DIM)


def conv_kernel(line_ref, filter_spec_ref, *rest, count, groups, shift, block, head_dim):
    far = count - 2
    arrived = rest[:far]
    weight_ref, ahead_ref, back_ref, query_ref, spec_all = rest[far:]
    here = lax.axis_index("seq")
    width = line_ref.shape[2]
    columns = width // groups
    start = share_start(shift, columns, groups)
    chosen = pl.ds(start, columns)
    ahead = ahead_ref[...]
    back = back_ref[...]
    first_head = here * (width // head_dim) + start // head_dim
    spec_all[here] = filter_spec_ref[0, :, chosen]
    spec_all[here ^ 1] = filter_spec_ref[1, :, chosen]
    for step, piece in enumerate(arrived, 2):
        spec_all[here ^ step] = wide_mxu(ahead, piece[piece.shape[0] - block :])
    lines = [(line_ref[b, :block, chosen], line_ref[b, block:, chosen]) for b in range(count)]
    kernels = [(spec_all[0, :block], spec_all[0, block:])] + [
        with_block_before(spec_all[b], spec_all[b - 1], block) for b in range(1, count)
    ]
    totals = []
    for b in range(count):
        total_re, total_im = 0.0, 0.0
        for j in range(b + 1):
            line_re, line_im = lines[j]
            kernel_re, kernel_im = kernels[b - j]
            total_re = total_re + (line_re * kernel_re - line_im * kernel_im)
            total_im = total_im + (line_re * kernel_im + line_im * kernel_re)
        totals.append((total_re, total_im))
    for b, conv_out in enumerate(to_blocks(back, totals, block)):
        conv_out = conv_out.astype(jnp.bfloat16)
        for h in range(columns // head_dim):
            part = slice(h * head_dim, (h + 1) * head_dim)
            query_ref[b, :, part] = mxu(conv_out[:, part], weight_ref[first_head + h]).astype(
                jnp.bfloat16
            )


def weigh_kernel(own_ref, near_ref, *rest, count, groups, block, head_dim):
    arrived, queries = rest[: count - 2], rest[count - 2 : count - 2 + groups]
    weight_ref, part_ref, key_all = rest[count - 2 + groups :]
    here = lax.axis_index("seq")
    key_all[here] = own_columns(own_ref, here, near_ref.shape[1])
    for step, piece in enumerate((near_ref, *arrived), 1):
        first = max(piece.shape[0] - 2 * block, 0)
        key_all[here ^ step] = piece[first : first + block]
    turned = (((1,), (1,)), ((), ()))
    scale = math.log2(math.e) / math.sqrt(head_dim)
    row = lax.broadcasted_iota(jnp.int32, (block, block), 0)
    column = lax.broadcasted_iota(jnp.int32, (block, block), 1)
    allowed = column <= row
    share = queries[0].shape[2]
    heads = share // head_dim
    places = [(h, b) for h in range(groups * heads) for b in range(count)]
    scores = {place: [] for place in places}
    for h in range(groups * heads):
        shift, part = divmod(h, heads)
        query = jnp.concatenate(
            [queries[shift][b, :, part * head_dim : (part + 1) * head_dim] for b in range(count)],
            axis=0,
        )
        columns = pl.ds(share_start(shift, share, groups) + part * head_dim, head_dim)
        for j in range(count):
            later = lax.dot_general(
                query[j * block :],
                key_all[j, :, columns],
                turned,
                preferred_element_type=jnp.float32,
            )
            for b in range(j, count):
                score = later[(b - j) * block : (b - j + 1) * block]
                scores[h, b].append(jnp.where(allowed, score, -1e30) if j == b else score)
    peaks = {
        place: jnp.max(functools.reduce(jnp.maximum, parts), axis=1, keepdims=True)
        for place, parts in scores.items()
    }
    sums = {}
    for h, b in places:
        weights = [jnp.exp2((score - peaks[h, b]) * scale) for score in scores[h, b]]
        weights[b] = jnp.where(allowed, weights[b], 0.0)
        sums[h, b] = jnp.sum(functools.reduce(jnp.add, weights), axis=1, keepdims=True)
        for j in range(b + 1):
            weight_ref[h, b, :, j * block : (j + 1) * block] = weights[j].astype(jnp.bfloat16)
    for h, b in places:
        part_ref[h, b] = jnp.broadcast_to(1.0 / sums[h, b], (block, head_dim))


def sum_kernel(weight_ref, part_ref, own_ref, near_ref, *rest, count, groups, block, head_dim):
    arrived = rest[: count - 2]
    outs = rest[count - 2 : 2 * count - 2]
    value_all, out_all = rest[2 * count - 2 :]
    here = lax.axis_index("seq")

    def rows_of(b):
        return pl.ds(pl.multiple_of(b * block, block), block)

    value_all[rows_of(here)] = own_columns(own_ref, here, near_ref.shape[1])
    for step, piece in enumerate((near_ref, *arrived), 1):
        value_all[rows_of(here ^ step)] = piece[-block:]
    share = value_all.shape[1] // groups
    totals = []
    for h in range(weight_ref.shape[0]):
        shift, part = divmod(h, share // head_dim)
        columns = pl.ds(share_start(shift, share, groups) + part * head_dim, head_dim)
        for b in range(count):
            seen = (b + 1) * block
            total = mxu(weight_ref[h, b, :, :seen], value_all[:seen, columns])
            totals.append((h, b, columns, total))
    for h, b, columns, total in totals:
        out_all[b, :, columns] = (total * part_ref[h, b]).astype(jnp.bfloat16)
    for step, out in enumerate(outs):
        out[...] = out_all[here ^ step]


def join_kernel(*rest, steps, width):
    pieces, out_ref, sem = rest[: len(steps)], rest[-2], rest[-1]
    here = lax.axis_index("seq")
    copies = []
    for n, (step, piece) in enumerate(zip(steps, pieces)):
        columns = pl.ds(pl.multiple_of((here ^ step) * width, width), width)
        copies.append(pltpu.make_async_copy(piece, out_ref.at[:, columns], sem.at[n]))
    for copy in copies:
        copy.start()
    for copy in copies:
        copy.wait()


WHOLE = pl.BlockSpec(memory_space=pltpu.VMEM)


def head_shards(
    gate_input, value_input, short_filter, long_filter, query_weight, key_matrix, value_matrix
):
    count = lax.axis_size("seq")
    block, local_width = gate_input.shape
    width = local_width // count
    heads = width // HEAD_DIM
    here = lax.axis_index("seq")
    groups = lax.axis_size("groups") if heads % lax.axis_size("groups") == 0 else 1

    def swap(value, step):
        return lax.ppermute(value, "seq", [(i, i ^ step) for i in range(count)])

    def packed(arrays, parts, after=()):
        return pl.pallas_call(
            functools.partial(pack_kernel, parts=parts, width=width),
            out_shape=[
                pltpu.VMEM((len(chosen) * block, columns), jnp.bfloat16)
                for _, columns, chosen in parts
            ],
            in_specs=[pl.BlockSpec(memory_space=pl.ANY)] * (len(arrays) + len(after)),
            out_specs=[WHOLE] * len(parts),
            scratch_shapes=[
                pltpu.SemaphoreType.DMA((sum(len(chosen) for *_, chosen in parts),))
            ],
            compiler_params=params,
        )(*[pltpu.with_memory_space_constraint(a, pltpu.HBM) for a in arrays], *after)

    ahead, back = block_tables(block)
    scratch = lambda n: pltpu.VMEM((n, block, width), jnp.bfloat16)
    params = pltpu.CompilerParams(vmem_limit_bytes=32 * 1024 * 1024)
    far = range(2, count)
    share = width // groups
    slots = range(groups)
    streams = [(i, slot) for i in (0, 1) for slot in slots] + [(2, None)]
    arrays = [gate_input, value_input, long_filter, key_matrix, value_matrix]
    first, near = packed(
        arrays, [(far[0], share, streams), (1, width, [(n, 0) for n in range(5)])]
    )
    near = swap(near, 1)
    pieces = packed(
        arrays,
        [(step, share, streams) for step in far[1:]]
        + [(step, width, [(3, 0), (4, 0)]) for step in far[:-1]]
        + [(far[-1], width, [(n, 0)]) for n in (3, 4)],
        after=[near],
    )
    arrived = [swap(piece, step) for step, piece in zip(far, [first, *pieces])]
    later = pieces[len(far) - 1 :]
    tables = jnp.asarray(ahead), jnp.asarray(back)
    spectra = lambda n: (n, 2 * block, width)
    gate_spec, filter_spec, taps_spec = pl.pallas_call(
        functools.partial(local_kernel, block=block),
        out_shape=[
            jax.ShapeDtypeStruct(spectra(2), jnp.float32),
            jax.ShapeDtypeStruct(spectra(2), jnp.float32),
            jax.ShapeDtypeStruct((2 * block, width), jnp.float32),
        ],
        in_specs=[WHOLE] * 5,
        out_specs=[WHOLE] * 3,
        compiler_params=params,
    )(gate_input, long_filter, near, short_filter, tables[0])
    filters = [piece[-block:] for piece in arrived]
    filters[0], taps_spec = lax.optimization_barrier((filters[0], taps_spec))
    shares = [arrived] + [
        [
            lax.ppermute(piece, "groups", [(i, (i + shift) % groups) for i in range(groups)])
            for piece in filters
        ]
        for shift in range(1, groups)
    ]
    later = [swap(piece, step) for step, piece in zip([*far, far[-1]], later)]
    arrived_keys, arrived_values = later[:-1], [*later[:-2], later[-1]]
    lines = pl.pallas_call(
        functools.partial(smooth_kernel, count=count, block=block),
        out_shape=jax.ShapeDtypeStruct(spectra(count), jnp.float32),
        in_specs=[WHOLE] * (count + 4),
        out_specs=WHOLE,
        scratch_shapes=[pltpu.VMEM(spectra(count), jnp.float32), scratch(count)],
        compiler_params=params,
    )(gate_spec, taps_spec, value_input, near, *arrived, *tables)
    queries = [
        pl.pallas_call(
            functools.partial(
                conv_kernel,
                count=count,
                groups=groups,
                shift=shift,
                block=block,
                head_dim=HEAD_DIM,
            ),
            out_shape=jax.ShapeDtypeStruct((count, block, share), jnp.bfloat16),
            in_specs=[WHOLE] * (len(far) + 5),
            out_specs=WHOLE,
            scratch_shapes=[pltpu.VMEM((count, 2 * block, share), jnp.float32)],
            compiler_params=params,
        )(lines, filter_spec, *pieces, query_weight, *tables)
        for shift, pieces in enumerate(shares)
    ]
    weights, parts = pl.pallas_call(
        functools.partial(
            weigh_kernel, count=count, groups=groups, block=block, head_dim=HEAD_DIM
        ),
        out_shape=[
            jax.ShapeDtypeStruct((heads, count, block, count * block), jnp.bfloat16),
            jax.ShapeDtypeStruct((heads, count, block, HEAD_DIM), jnp.float32),
        ],
        in_specs=[WHOLE] * (count + groups),
        out_specs=[WHOLE] * 2,
        scratch_shapes=[scratch(count)],
        compiler_params=params,
    )(key_matrix, near, *arrived_keys, *queries)
    pieces = pl.pallas_call(
        functools.partial(
            sum_kernel, count=count, groups=groups, block=block, head_dim=HEAD_DIM
        ),
        out_shape=[jax.ShapeDtypeStruct((block, width), jnp.bfloat16)] * count,
        in_specs=[WHOLE] * (count + 2),
        out_specs=[WHOLE] * count,
        scratch_shapes=[
            pltpu.VMEM((count * block, width), jnp.bfloat16),
            scratch(count),
        ],
        compiler_params=params,
    )(weights, parts, value_matrix, near, *arrived_values)
    swapped = {step: swap(pieces[step], step) for step in [*far, 1]}
    pieces = [pieces[0]] + [swapped[step] for step in range(1, count)]

    def joined(steps, *before):
        return pl.pallas_call(
            functools.partial(join_kernel, steps=steps, width=width),
            out_shape=pltpu.HBM((block, local_width), jnp.bfloat16),
            in_specs=[WHOLE] * len(steps) + [pl.BlockSpec(memory_space=pl.ANY)] * len(before),
            out_specs=pl.BlockSpec(memory_space=pl.ANY),
            scratch_shapes=[pltpu.SemaphoreType.DMA((len(steps),))],
            input_output_aliases={len(steps): 0} if before else {},
            compiler_params=params,
        )(*[pieces[step] for step in steps], *before)

    result = joined((0, 1))
    for step in far:
        result = joined((step,), result)
    return result


def shards(*arrays):
    count = lax.axis_size("seq")
    block, local_width = arrays[0].shape
    even = local_width % (count * HEAD_DIM) == 0
    if even and count > 1 and count & (count - 1) == 0 and block == TAPS:
        return head_shards(*arrays)
    return general_shards(*arrays)


def solution(mesh):
    in_specs = (
        P(("groups", "seq"), "chan"),
        P(("groups", "seq"), "chan"),
        P("chan", None),
        P("seq", "chan"),
        P("chan", None, None),
        P(("groups", "seq"), "chan"),
        P(("groups", "seq"), "chan"),
    )
    out_specs = P(("groups", "seq"), "chan")
    return jax.shard_map(shards, mesh=mesh, in_specs=in_specs, out_specs=out_specs, check_vma=False)
```

```python
import functools
import math

import jax
import jax.numpy as jnp
import ml_dtypes
import numpy as np
from jax import lax
from jax.experimental import pallas as pl
from jax.experimental.pallas import tpu as pltpu
from jax.sharding import PartitionSpec as P

HEAD_DIM = 128
TAPS = 128
RADIX = 128


HIGHEST = lax.Precision.HIGHEST


def shifted(value, axis, steps):
    count = lax.axis_size(axis)
    initial, last = (max(0, -steps), min(count, count - steps))
    return lax.ppermute(value, axis, [(source, source + steps) for source in range(initial, last)])


def unit_table(height, breadth, modulus, orient):
    product = (
        lax.broadcasted_iota(jnp.int32, (height, breadth), 0)
        * lax.broadcasted_iota(jnp.int32, (height, breadth), 1)
        % modulus
    )
    angles = 2.0 * math.pi / modulus * product.astype(jnp.float32)
    return (jnp.cos(angles), orient * jnp.sin(angles))


def block_table(factor, orient):
    inner_re, inner_im = unit_table(factor, factor, factor, orient)
    upper = jnp.concatenate([inner_re, inner_im], axis=1)
    lower = jnp.concatenate([-inner_im, inner_re], axis=1)
    return jnp.concatenate([upper, lower], axis=0)


def spectrum(signal, factor):
    channels, length = signal.shape
    full_length = 2 * length
    column_count = full_length // factor
    folded = signal.reshape(channels, column_count // 2, factor)
    outer_re, outer_im = unit_table(column_count, column_count // 2, column_count, -1.0)
    outer_both = jnp.concatenate([outer_re, outer_im], axis=0)
    first = jnp.einsum("kn,cnm->ckm", outer_both, folded, precision=HIGHEST)
    first_re = first[:, :column_count]
    first_im = first[:, column_count:]
    twist_re, twist_im = unit_table(column_count, factor, full_length, -1.0)
    mid_re = first_re * twist_re - first_im * twist_im
    mid_im = first_re * twist_im + first_im * twist_re
    joined = jnp.concatenate([mid_re, mid_im], axis=2)
    return jnp.einsum("ckn,nm->ckm", joined, block_table(factor, -1.0), precision=HIGHEST)


def inverse(spec_both, factor, length):
    channels = spec_both.shape[0]
    full_length = 2 * length
    column_count = full_length // factor
    mid = jnp.einsum("ckm,mn->ckn", spec_both, block_table(factor, 1.0), precision=HIGHEST)
    mid_re = mid[:, :, :factor]
    mid_im = mid[:, :, factor:]
    twist_re, twist_im = unit_table(column_count, factor, full_length, 1.0)
    turn_re = mid_re * twist_re - mid_im * twist_im
    turn_im = mid_re * twist_im + mid_im * twist_re
    outer_re, outer_im = unit_table(column_count // 2, column_count, column_count, 1.0)
    outer_both = jnp.concatenate([outer_re, -outer_im], axis=1)
    turned = jnp.concatenate([turn_re, turn_im], axis=1)
    result = jnp.einsum("nk,ckm->cnm", outer_both, turned, precision=HIGHEST)
    return result.reshape(channels, length) / full_length


def general_shards(
    gate_input, value_input, short_filter, long_filter, query_weight, key_matrix, value_matrix
):
    seq_rows, local_width = gate_input.shape
    last_rows = gate_input[seq_rows - (TAPS - 1) :]
    earlier = shifted(last_rows, "seq", 1)
    padded = jnp.concatenate([earlier, gate_input], axis=0).astype(jnp.float32)
    kernel = short_filter[:, ::-1].T[:, None, :]
    smoothed = lax.conv_general_dilated(
        padded[None],
        kernel,
        (1,),
        "VALID",
        dimension_numbers=("NHC", "HIO", "NHC"),
        feature_group_count=local_width,
        precision=HIGHEST,
    )[0]
    mixed_input = (smoothed * value_input.astype(jnp.float32)).astype(jnp.bfloat16)
    signal, kernel_line = (
        lax.all_to_all(mixed_input.T, "seq", split_axis=0, concat_axis=1, tiled=True),
        lax.all_to_all(long_filter.T, "seq", split_axis=0, concat_axis=1, tiled=True),
    )
    length = signal.shape[1]
    signal_both = spectrum(signal.astype(jnp.float32), RADIX)
    kernel_both = spectrum(kernel_line.astype(jnp.float32), RADIX)
    signal_re = signal_both[:, :, :RADIX]
    signal_im = signal_both[:, :, RADIX:]
    kernel_re = kernel_both[:, :, :RADIX]
    kernel_im = kernel_both[:, :, RADIX:]
    joint = jnp.concatenate(
        [
            signal_re * kernel_re - signal_im * kernel_im,
            signal_re * kernel_im + signal_im * kernel_re,
        ],
        axis=2,
    )
    conv_line = inverse(joint, RADIX, length).astype(jnp.bfloat16)
    my_index = lax.axis_index("seq")
    group_firsts = [my_index * seq_rows]
    conv_columns = lax.all_to_all(conv_line, "seq", split_axis=1, concat_axis=0, tiled=True)
    heads_here = local_width // HEAD_DIM
    conv_heads = conv_columns.reshape(heads_here, HEAD_DIM, seq_rows)
    query_heads = jnp.einsum(
        "hds,hde->hse", conv_heads, query_weight, preferred_element_type=jnp.float32
    ).astype(jnp.bfloat16)
    group_count = len(group_firsts)
    query_groups = [query_heads]
    key_heads = key_matrix.reshape(seq_rows, heads_here, HEAD_DIM).transpose(1, 0, 2)
    value_heads = value_matrix.reshape(seq_rows, heads_here, HEAD_DIM).transpose(1, 0, 2)
    score_scale = 1.0 / math.sqrt(HEAD_DIM)

    def attend_group(running, group_query, group_first, key_block, value_block, first_row):
        block_rows = key_block.shape[1]

        def compute(current):
            peak_value, weight_sum, weighted = current
            scores = (
                jnp.einsum(
                    "hqd,hkd->hqk", group_query, key_block, preferred_element_type=jnp.float32
                )
                * score_scale
            )
            key_pos = first_row + lax.iota(jnp.int32, block_rows)
            query_pos = group_first + lax.iota(jnp.int32, seq_rows)
            allowed = (key_pos[None, :] <= query_pos[:, None])[None]
            scores = jnp.where(allowed, scores, -1e30)
            new_peak = jnp.maximum(peak_value, jnp.max(scores, axis=2))
            weights = jnp.where(allowed, jnp.exp(scores - new_peak[:, :, None]), 0.0)
            rescale = jnp.exp(peak_value - new_peak)
            weight_sum = weight_sum * rescale + jnp.sum(weights, axis=2)
            weighted = weighted * rescale[:, :, None] + jnp.einsum(
                "hqk,hkd->hqd",
                weights.astype(jnp.bfloat16),
                value_block,
                preferred_element_type=jnp.float32,
            )
            return (new_peak, weight_sum, weighted)

        live = first_row <= group_first + seq_rows - 1
        return lax.cond(live, compute, lambda current: current, running)

    def attend(states, key_block, value_block, first_row):
        return tuple(
            (
                attend_group(
                    states[g], query_groups[g], group_firsts[g], key_block, value_block, first_row
                )
                for g in range(group_count)
            )
        )

    one_state = (
        jnp.full((heads_here, seq_rows), -1e30, jnp.float32),
        jnp.zeros((heads_here, seq_rows), jnp.float32),
        jnp.zeros((heads_here, seq_rows, HEAD_DIM), jnp.float32),
    )
    initial = tuple((one_state for g in range(group_count)))
    running = initial
    key_piece = lax.all_gather(key_heads, "seq", axis=1, tiled=True)
    value_piece = lax.all_gather(value_heads, "seq", axis=1, tiled=True)
    piece_rows = key_piece.shape[1]
    block_rows = 512
    block_count = piece_rows // block_rows
    key_blocks = key_piece.reshape(heads_here, block_count, block_rows, HEAD_DIM).transpose(
        1, 0, 2, 3
    )
    value_blocks = value_piece.reshape(heads_here, block_count, block_rows, HEAD_DIM).transpose(
        1, 0, 2, 3
    )

    def advance(current, element):
        key_block, value_block, position = element
        return (attend(current, key_block, value_block, position * block_rows), None)

    running, _ = lax.scan(
        advance, running, (key_blocks, value_blocks, lax.iota(jnp.int32, block_count))
    )
    outputs = [state[2] / state[1][:, :, None] for state in running]
    result = outputs[0]
    attended_rows = result.transpose(1, 0, 2).reshape(seq_rows, local_width).astype(jnp.bfloat16)
    return attended_rows


def block_tables(block):
    angle = np.pi / block * (np.arange(block) + 0.5)
    turns = angle[:, None] * np.arange(block)[None]
    ahead = np.concatenate([np.cos(turns), -np.sin(turns)], axis=0)
    back = np.concatenate([np.cos(turns.T), -np.sin(turns.T)], axis=1) / block

    def pair(table):
        high = table.astype(ml_dtypes.bfloat16)
        rest = (table - high.astype(np.float64)).astype(ml_dtypes.bfloat16)
        return np.concatenate([high, rest], axis=0)

    return pair(ahead), pair(back)


def two_parts(value):
    high = value.astype(jnp.bfloat16)
    return high, (value - high.astype(jnp.float32)).astype(jnp.bfloat16)


def mxu(left, right):
    return jnp.dot(left, right, preferred_element_type=jnp.float32)


def folded_sum(stacked):
    half = stacked.shape[0] // 2
    return stacked[:half] + stacked[half:]


def wide_mxu(table, value):
    half = table.shape[0] // 2
    wide = jnp.concatenate([table[:half], table[half:]], axis=1)
    return mxu(wide, jnp.concatenate([value, value], axis=0))


def to_blocks(back, spectra, block):
    parts = [two_parts(jnp.concatenate(spec, axis=0)) for spec in spectra]
    main = [mxu(back, high) for high, _ in parts]
    small = [mxu(back[:block], rest) for _, rest in parts]
    return [folded_sum(large) + rest for large, rest in zip(main, small)]


def pack_kernel(*rest, parts, width):
    outs, sem = rest[-len(parts) - 1 : -1], rest[-1]
    here, group = lax.axis_index("seq"), lax.axis_index("groups")
    copies = []
    for (step, columns, blocks), out in zip(parts, outs):
        for n, (i, slot) in enumerate(blocks):
            start = (here ^ step) * width + (group if slot is None else slot) * columns
            source = rest[i].at[:, pl.ds(pl.multiple_of(start, HEAD_DIM), columns)]
            rows = source.shape[0]
            copies.append(
                pltpu.make_async_copy(
                    source, out.at[n * rows : (n + 1) * rows], sem.at[len(copies)]
                )
            )
    for copy in copies:
        copy.start()
    for copy in copies:
        copy.wait()


def own_columns(ref, here, width):
    return ref[:, pl.ds(pl.multiple_of(here * width, width), width)]


def with_block_before(spec, before, block):
    odd = lax.broadcasted_iota(jnp.int32, (block, spec.shape[1]), 0) % 2
    sign = 1.0 - 2.0 * odd.astype(jnp.float32)
    return spec[:block] - sign * before[block:], spec[block:] + sign * before[:block]


def local_kernel(gate_ref, filter_ref, near_ref, taps_ref, ahead_ref, *outs, block):
    gate_spec_ref, filter_spec_ref, taps_spec_ref = outs
    here = lax.axis_index("seq")
    width = near_ref.shape[1]
    ahead = ahead_ref[...]
    gate_spec_ref[0] = wide_mxu(ahead, own_columns(gate_ref, here, width))
    gate_spec_ref[1] = wide_mxu(ahead, near_ref[:block])
    filter_spec_ref[0] = wide_mxu(ahead, own_columns(filter_ref, here, width))
    filter_spec_ref[1] = wide_mxu(ahead, near_ref[2 * block : 3 * block])
    turned = (((1,), (1,)), ((), ()))
    taps = taps_ref[pl.ds(pl.multiple_of(here * width, width), width)]
    taps_high, taps_rest = two_parts(taps)
    taps_spec_ref[...] = folded_sum(
        lax.dot_general(ahead, taps_high, turned, preferred_element_type=jnp.float32)
    ) + lax.dot_general(
        ahead[: 2 * block], taps_rest, turned, preferred_element_type=jnp.float32
    )


def smooth_kernel(gate_spec_ref, taps_spec_ref, value_ref, near_ref, *rest, count, block):
    arrived = rest[: count - 2]
    ahead_ref, back_ref, line_ref, gate_all, value_all = rest[count - 2 :]
    here = lax.axis_index("seq")
    width = near_ref.shape[1]
    ahead = ahead_ref[...]
    back = back_ref[...]
    value_all[here] = own_columns(value_ref, here, width)
    value_all[here ^ 1] = near_ref[block : 2 * block]
    gate_all[here] = gate_spec_ref[0]
    gate_all[here ^ 1] = gate_spec_ref[1]
    for step, piece in enumerate(arrived, 2):
        columns = piece.shape[1]
        slots = width // columns

        def joined(first):
            return jnp.concatenate(
                [piece[n * block : (n + 1) * block] for n in range(first, first + slots)], axis=1
            )

        gate_all[here ^ step] = wide_mxu(ahead, joined(0))
        value_all[here ^ step] = joined(slots)
    taps_re, taps_im = taps_spec_ref[:block], taps_spec_ref[block:]
    spectra = []
    for b in range(count):
        gate_spec = gate_all[b]
        if b > 0:
            gate_re, gate_im = with_block_before(gate_spec, gate_all[b - 1], block)
        else:
            gate_re, gate_im = gate_spec[:block], gate_spec[block:]
        spectra.append(
            (gate_re * taps_re - gate_im * taps_im, gate_re * taps_im + gate_im * taps_re)
        )
    mixed = [
        (smoothed * value_all[b].astype(jnp.float32)).astype(jnp.bfloat16)
        for b, smoothed in enumerate(to_blocks(back, spectra, block))
    ]
    for b in range(count):
        line_ref[b] = wide_mxu(ahead, mixed[b])


def share_start(shift, columns, groups):
    group = lax.axis_index("groups") if groups > 1 else 0
    return pl.multiple_of(lax.rem(group + groups - shift, groups) * columns, HEAD_DIM)


def conv_kernel(line_ref, filter_spec_ref, *rest, count, groups, shift, block, head_dim):
    far = count - 2
    arrived = rest[:far]
    weight_ref, ahead_ref, back_ref, query_ref, spec_all = rest[far:]
    here = lax.axis_index("seq")
    width = line_ref.shape[2]
    columns = width // groups
    start = share_start(shift, columns, groups)
    chosen = pl.ds(start, columns)
    ahead = ahead_ref[...]
    back = back_ref[...]
    first_head = here * (width // head_dim) + start // head_dim
    spec_all[here] = filter_spec_ref[0, :, chosen]
    spec_all[here ^ 1] = filter_spec_ref[1, :, chosen]
    for step, piece in enumerate(arrived, 2):
        spec_all[here ^ step] = wide_mxu(ahead, piece[piece.shape[0] - block :])
    lines = [(line_ref[b, :block, chosen], line_ref[b, block:, chosen]) for b in range(count)]
    kernels = [(spec_all[0, :block], spec_all[0, block:])] + [
        with_block_before(spec_all[b], spec_all[b - 1], block) for b in range(1, count)
    ]
    totals = []
    for b in range(count):
        total_re, total_im = 0.0, 0.0
        for j in range(b + 1):
            line_re, line_im = lines[j]
            kernel_re, kernel_im = kernels[b - j]
            total_re = total_re + (line_re * kernel_re - line_im * kernel_im)
            total_im = total_im + (line_re * kernel_im + line_im * kernel_re)
        totals.append((total_re, total_im))
    for b, conv_out in enumerate(to_blocks(back, totals, block)):
        conv_out = conv_out.astype(jnp.bfloat16)
        for h in range(columns // head_dim):
            part = slice(h * head_dim, (h + 1) * head_dim)
            query_ref[b, :, part] = mxu(conv_out[:, part], weight_ref[first_head + h]).astype(
                jnp.bfloat16
            )


def weigh_kernel(own_ref, near_ref, *rest, count, groups, block, head_dim):
    arrived, queries = rest[: count - 2], rest[count - 2 : count - 2 + groups]
    weight_ref, part_ref, key_all = rest[count - 2 + groups :]
    here = lax.axis_index("seq")
    key_all[here] = own_columns(own_ref, here, near_ref.shape[1])
    for step, piece in enumerate((near_ref, *arrived), 1):
        first = max(piece.shape[0] - 2 * block, 0)
        key_all[here ^ step] = piece[first : first + block]
    turned = (((1,), (1,)), ((), ()))
    scale = math.log2(math.e) / math.sqrt(head_dim)
    row = lax.broadcasted_iota(jnp.int32, (block, block), 0)
    column = lax.broadcasted_iota(jnp.int32, (block, block), 1)
    allowed = column <= row
    share = queries[0].shape[2]
    heads = share // head_dim
    places = [(h, b) for h in range(groups * heads) for b in range(count)]
    scores = {place: [] for place in places}
    for h in range(groups * heads):
        shift, part = divmod(h, heads)
        query = jnp.concatenate(
            [queries[shift][b, :, part * head_dim : (part + 1) * head_dim] for b in range(count)],
            axis=0,
        )
        columns = pl.ds(share_start(shift, share, groups) + part * head_dim, head_dim)
        for j in range(count):
            later = lax.dot_general(
                query[j * block :],
                key_all[j, :, columns],
                turned,
                preferred_element_type=jnp.float32,
            )
            for b in range(j, count):
                score = later[(b - j) * block : (b - j + 1) * block]
                scores[h, b].append(jnp.where(allowed, score, -1e30) if j == b else score)
    peaks = {
        place: jnp.max(functools.reduce(jnp.maximum, parts), axis=1, keepdims=True)
        for place, parts in scores.items()
    }
    sums = {}
    for h, b in places:
        weights = [jnp.exp2((score - peaks[h, b]) * scale) for score in scores[h, b]]
        weights[b] = jnp.where(allowed, weights[b], 0.0)
        sums[h, b] = jnp.sum(functools.reduce(jnp.add, weights), axis=1, keepdims=True)
        for j in range(b + 1):
            weight_ref[h, b, :, j * block : (j + 1) * block] = weights[j].astype(jnp.bfloat16)
    for h, b in places:
        part_ref[h, b] = jnp.broadcast_to(1.0 / sums[h, b], (block, head_dim))


def sum_kernel(weight_ref, part_ref, own_ref, near_ref, *rest, count, groups, block, head_dim):
    arrived = rest[: count - 2]
    outs = rest[count - 2 : 2 * count - 2]
    value_all, out_all = rest[2 * count - 2 :]
    here = lax.axis_index("seq")

    def rows_of(b):
        return pl.ds(pl.multiple_of(b * block, block), block)

    value_all[rows_of(here)] = own_columns(own_ref, here, near_ref.shape[1])
    for step, piece in enumerate((near_ref, *arrived), 1):
        value_all[rows_of(here ^ step)] = piece[-block:]
    share = value_all.shape[1] // groups
    totals = []
    for h in range(weight_ref.shape[0]):
        shift, part = divmod(h, share // head_dim)
        columns = pl.ds(share_start(shift, share, groups) + part * head_dim, head_dim)
        for b in range(count):
            seen = (b + 1) * block
            total = mxu(weight_ref[h, b, :, :seen], value_all[:seen, columns])
            totals.append((h, b, columns, total))
    for h, b, columns, total in totals:
        out_all[b, :, columns] = (total * part_ref[h, b]).astype(jnp.bfloat16)
    for step, out in enumerate(outs):
        out[...] = out_all[here ^ step]


def join_kernel(*rest, steps, width):
    pieces, out_ref, sem = rest[: len(steps)], rest[-2], rest[-1]
    here = lax.axis_index("seq")
    copies = []
    for n, (step, piece) in enumerate(zip(steps, pieces)):
        columns = pl.ds(pl.multiple_of((here ^ step) * width, width), width)
        copies.append(pltpu.make_async_copy(piece, out_ref.at[:, columns], sem.at[n]))
    for copy in copies:
        copy.start()
    for copy in copies:
        copy.wait()


WHOLE = pl.BlockSpec(memory_space=pltpu.VMEM)


def head_shards(
    gate_input, value_input, short_filter, long_filter, query_weight, key_matrix, value_matrix
):
    count = lax.axis_size("seq")
    block, local_width = gate_input.shape
    width = local_width // count
    heads = width // HEAD_DIM
    here = lax.axis_index("seq")
    groups = lax.axis_size("groups") if heads % lax.axis_size("groups") == 0 else 1

    def swap(value, step):
        return lax.ppermute(value, "seq", [(i, i ^ step) for i in range(count)])

    def packed(arrays, parts, after=()):
        return pl.pallas_call(
            functools.partial(pack_kernel, parts=parts, width=width),
            out_shape=[
                pltpu.VMEM((len(chosen) * block, columns), jnp.bfloat16)
                for _, columns, chosen in parts
            ],
            in_specs=[pl.BlockSpec(memory_space=pl.ANY)] * (len(arrays) + len(after)),
            out_specs=[WHOLE] * len(parts),
            scratch_shapes=[
                pltpu.SemaphoreType.DMA((sum(len(chosen) for *_, chosen in parts),))
            ],
            compiler_params=params,
        )(*[pltpu.with_memory_space_constraint(a, pltpu.HBM) for a in arrays], *after)

    ahead, back = block_tables(block)
    scratch = lambda n: pltpu.VMEM((n, block, width), jnp.bfloat16)
    params = pltpu.CompilerParams(vmem_limit_bytes=32 * 1024 * 1024)
    far = range(2, count)
    share = width // groups
    slots = range(groups)
    streams = [(i, slot) for i in (0, 1) for slot in slots] + [(2, None if groups > 1 else 0)]
    arrays = [gate_input, value_input, long_filter, key_matrix, value_matrix]
    first, near = packed(
        arrays, [(far[0], share, streams), (1, width, [(n, 0) for n in range(5)])]
    )
    near = swap(near, 1)
    pieces = packed(
        arrays,
        [(step, share, streams) for step in far[1:]]
        + [(step, width, [(3, 0), (4, 0)]) for step in far[:-1]]
        + [(far[-1], width, [(n, 0)]) for n in (3, 4)],
        after=[near],
    )
    arrived = [swap(piece, step) for step, piece in zip(far, [first, *pieces])]
    later = pieces[len(far) - 1 :]
    tables = jnp.asarray(ahead), jnp.asarray(back)
    spectra = lambda n: (n, 2 * block, width)
    gate_spec, filter_spec, taps_spec = pl.pallas_call(
        functools.partial(local_kernel, block=block),
        out_shape=[
            jax.ShapeDtypeStruct(spectra(2), jnp.float32),
            jax.ShapeDtypeStruct(spectra(2), jnp.float32),
            jax.ShapeDtypeStruct((2 * block, width), jnp.float32),
        ],
        in_specs=[WHOLE] * 5,
        out_specs=[WHOLE] * 3,
        compiler_params=params,
    )(gate_input, long_filter, near, short_filter, tables[0])
    filters = [piece[-block:] for piece in arrived]
    filters[0], taps_spec = lax.optimization_barrier((filters[0], taps_spec))
    shares = [arrived] + [
        [
            lax.ppermute(piece, "groups", [(i, (i + shift) % groups) for i in range(groups)])
            for piece in filters
        ]
        for shift in range(1, groups)
    ]
    later = [swap(piece, step) for step, piece in zip([*far, far[-1]], later)]
    arrived_keys, arrived_values = later[:-1], [*later[:-2], later[-1]]
    lines = pl.pallas_call(
        functools.partial(smooth_kernel, count=count, block=block),
        out_shape=jax.ShapeDtypeStruct(spectra(count), jnp.float32),
        in_specs=[WHOLE] * (count + 4),
        out_specs=WHOLE,
        scratch_shapes=[pltpu.VMEM(spectra(count), jnp.float32), scratch(count)],
        compiler_params=params,
    )(gate_spec, taps_spec, value_input, near, *arrived, *tables)
    queries = [
        pl.pallas_call(
            functools.partial(
                conv_kernel,
                count=count,
                groups=groups,
                shift=shift,
                block=block,
                head_dim=HEAD_DIM,
            ),
            out_shape=jax.ShapeDtypeStruct((count, block, share), jnp.bfloat16),
            in_specs=[WHOLE] * (len(far) + 5),
            out_specs=WHOLE,
            scratch_shapes=[pltpu.VMEM((count, 2 * block, share), jnp.float32)],
            compiler_params=params,
        )(lines, filter_spec, *pieces, query_weight, *tables)
        for shift, pieces in enumerate(shares)
    ]
    weights, parts = pl.pallas_call(
        functools.partial(
            weigh_kernel, count=count, groups=groups, block=block, head_dim=HEAD_DIM
        ),
        out_shape=[
            jax.ShapeDtypeStruct((heads, count, block, count * block), jnp.bfloat16),
            jax.ShapeDtypeStruct((heads, count, block, HEAD_DIM), jnp.float32),
        ],
        in_specs=[WHOLE] * (count + groups),
        out_specs=[WHOLE] * 2,
        scratch_shapes=[scratch(count)],
        compiler_params=params,
    )(key_matrix, near, *arrived_keys, *queries)
    pieces = pl.pallas_call(
        functools.partial(
            sum_kernel, count=count, groups=groups, block=block, head_dim=HEAD_DIM
        ),
        out_shape=[jax.ShapeDtypeStruct((block, width), jnp.bfloat16)] * count,
        in_specs=[WHOLE] * (count + 2),
        out_specs=[WHOLE] * count,
        scratch_shapes=[
            pltpu.VMEM((count * block, width), jnp.bfloat16),
            scratch(count),
        ],
        compiler_params=params,
    )(weights, parts, value_matrix, near, *arrived_values)
    swapped = {step: swap(pieces[step], step) for step in [*far, 1]}
    pieces = [pieces[0]] + [swapped[step] for step in range(1, count)]

    def joined(steps, *before):
        return pl.pallas_call(
            functools.partial(join_kernel, steps=steps, width=width),
            out_shape=pltpu.HBM((block, local_width), jnp.bfloat16),
            in_specs=[WHOLE] * len(steps) + [pl.BlockSpec(memory_space=pl.ANY)] * len(before),
            out_specs=pl.BlockSpec(memory_space=pl.ANY),
            scratch_shapes=[pltpu.SemaphoreType.DMA((len(steps),))],
            input_output_aliases={len(steps): 0} if before else {},
            compiler_params=params,
        )(*[pieces[step] for step in steps], *before)

    result = joined((0, 1))
    for step in far:
        result = joined((step,), result)
    return result


def shards(*arrays):
    count = lax.axis_size("seq")
    block, local_width = arrays[0].shape
    even = local_width % (count * HEAD_DIM) == 0
    if even and count > 3 and count & (count - 1) == 0 and block == TAPS:
        return head_shards(*arrays)
    return general_shards(*arrays)


def solution(mesh):
    in_specs = (
        P(("groups", "seq"), "chan"),
        P(("groups", "seq"), "chan"),
        P("chan", None),
        P("seq", "chan"),
        P("chan", None, None),
        P(("groups", "seq"), "chan"),
        P(("groups", "seq"), "chan"),
    )
    out_specs = P(("groups", "seq"), "chan")
    return jax.shard_map(shards, mesh=mesh, in_specs=in_specs, out_specs=out_specs, check_vma=False)
```

```python
import functools
import math

import jax
import jax.numpy as jnp
import ml_dtypes
import numpy as np
from jax import lax
from jax.experimental import pallas as pl
from jax.experimental.pallas import tpu as pltpu
from jax.sharding import PartitionSpec as P

HEAD_DIM = 128
TAPS = 128
RADIX = 128


HIGHEST = lax.Precision.HIGHEST


def shifted(value, axis, steps):
    count = lax.axis_size(axis)
    initial, last = (max(0, -steps), min(count, count - steps))
    return lax.ppermute(value, axis, [(source, source + steps) for source in range(initial, last)])


def unit_table(height, breadth, modulus, orient):
    product = (
        lax.broadcasted_iota(jnp.int32, (height, breadth), 0)
        * lax.broadcasted_iota(jnp.int32, (height, breadth), 1)
        % modulus
    )
    angles = 2.0 * math.pi / modulus * product.astype(jnp.float32)
    return (jnp.cos(angles), orient * jnp.sin(angles))


def block_table(factor, orient):
    inner_re, inner_im = unit_table(factor, factor, factor, orient)
    upper = jnp.concatenate([inner_re, inner_im], axis=1)
    lower = jnp.concatenate([-inner_im, inner_re], axis=1)
    return jnp.concatenate([upper, lower], axis=0)


def spectrum(signal, factor):
    channels, length = signal.shape
    full_length = 2 * length
    column_count = full_length // factor
    folded = signal.reshape(channels, column_count // 2, factor)
    outer_re, outer_im = unit_table(column_count, column_count // 2, column_count, -1.0)
    outer_both = jnp.concatenate([outer_re, outer_im], axis=0)
    first = jnp.einsum("kn,cnm->ckm", outer_both, folded, precision=HIGHEST)
    first_re = first[:, :column_count]
    first_im = first[:, column_count:]
    twist_re, twist_im = unit_table(column_count, factor, full_length, -1.0)
    mid_re = first_re * twist_re - first_im * twist_im
    mid_im = first_re * twist_im + first_im * twist_re
    joined = jnp.concatenate([mid_re, mid_im], axis=2)
    return jnp.einsum("ckn,nm->ckm", joined, block_table(factor, -1.0), precision=HIGHEST)


def inverse(spec_both, factor, length):
    channels = spec_both.shape[0]
    full_length = 2 * length
    column_count = full_length // factor
    mid = jnp.einsum("ckm,mn->ckn", spec_both, block_table(factor, 1.0), precision=HIGHEST)
    mid_re = mid[:, :, :factor]
    mid_im = mid[:, :, factor:]
    twist_re, twist_im = unit_table(column_count, factor, full_length, 1.0)
    turn_re = mid_re * twist_re - mid_im * twist_im
    turn_im = mid_re * twist_im + mid_im * twist_re
    outer_re, outer_im = unit_table(column_count // 2, column_count, column_count, 1.0)
    outer_both = jnp.concatenate([outer_re, -outer_im], axis=1)
    turned = jnp.concatenate([turn_re, turn_im], axis=1)
    result = jnp.einsum("nk,ckm->cnm", outer_both, turned, precision=HIGHEST)
    return result.reshape(channels, length) / full_length


def general_shards(
    gate_input, value_input, short_filter, long_filter, query_weight, key_matrix, value_matrix
):
    seq_rows, local_width = gate_input.shape
    last_rows = gate_input[seq_rows - (TAPS - 1) :]
    earlier = shifted(last_rows, "seq", 1)
    padded = jnp.concatenate([earlier, gate_input], axis=0).astype(jnp.float32)
    kernel = short_filter[:, ::-1].T[:, None, :]
    smoothed = lax.conv_general_dilated(
        padded[None],
        kernel,
        (1,),
        "VALID",
        dimension_numbers=("NHC", "HIO", "NHC"),
        feature_group_count=local_width,
        precision=HIGHEST,
    )[0]
    mixed_input = (smoothed * value_input.astype(jnp.float32)).astype(jnp.bfloat16)
    signal, kernel_line = (
        lax.all_to_all(mixed_input.T, "seq", split_axis=0, concat_axis=1, tiled=True),
        lax.all_to_all(long_filter.T, "seq", split_axis=0, concat_axis=1, tiled=True),
    )
    length = signal.shape[1]
    signal_both = spectrum(signal.astype(jnp.float32), RADIX)
    kernel_both = spectrum(kernel_line.astype(jnp.float32), RADIX)
    signal_re = signal_both[:, :, :RADIX]
    signal_im = signal_both[:, :, RADIX:]
    kernel_re = kernel_both[:, :, :RADIX]
    kernel_im = kernel_both[:, :, RADIX:]
    joint = jnp.concatenate(
        [
            signal_re * kernel_re - signal_im * kernel_im,
            signal_re * kernel_im + signal_im * kernel_re,
        ],
        axis=2,
    )
    conv_line = inverse(joint, RADIX, length).astype(jnp.bfloat16)
    my_index = lax.axis_index("seq")
    group_firsts = [my_index * seq_rows]
    conv_columns = lax.all_to_all(conv_line, "seq", split_axis=1, concat_axis=0, tiled=True)
    heads_here = local_width // HEAD_DIM
    conv_heads = conv_columns.reshape(heads_here, HEAD_DIM, seq_rows)
    query_heads = jnp.einsum(
        "hds,hde->hse", conv_heads, query_weight, preferred_element_type=jnp.float32
    ).astype(jnp.bfloat16)
    group_count = len(group_firsts)
    query_groups = [query_heads]
    key_heads = key_matrix.reshape(seq_rows, heads_here, HEAD_DIM).transpose(1, 0, 2)
    value_heads = value_matrix.reshape(seq_rows, heads_here, HEAD_DIM).transpose(1, 0, 2)
    score_scale = 1.0 / math.sqrt(HEAD_DIM)

    def attend_group(running, group_query, group_first, key_block, value_block, first_row):
        block_rows = key_block.shape[1]

        def compute(current):
            peak_value, weight_sum, weighted = current
            scores = (
                jnp.einsum(
                    "hqd,hkd->hqk", group_query, key_block, preferred_element_type=jnp.float32
                )
                * score_scale
            )
            key_pos = first_row + lax.iota(jnp.int32, block_rows)
            query_pos = group_first + lax.iota(jnp.int32, seq_rows)
            allowed = (key_pos[None, :] <= query_pos[:, None])[None]
            scores = jnp.where(allowed, scores, -1e30)
            new_peak = jnp.maximum(peak_value, jnp.max(scores, axis=2))
            weights = jnp.where(allowed, jnp.exp(scores - new_peak[:, :, None]), 0.0)
            rescale = jnp.exp(peak_value - new_peak)
            weight_sum = weight_sum * rescale + jnp.sum(weights, axis=2)
            weighted = weighted * rescale[:, :, None] + jnp.einsum(
                "hqk,hkd->hqd",
                weights.astype(jnp.bfloat16),
                value_block,
                preferred_element_type=jnp.float32,
            )
            return (new_peak, weight_sum, weighted)

        live = first_row <= group_first + seq_rows - 1
        return lax.cond(live, compute, lambda current: current, running)

    def attend(states, key_block, value_block, first_row):
        return tuple(
            (
                attend_group(
                    states[g], query_groups[g], group_firsts[g], key_block, value_block, first_row
                )
                for g in range(group_count)
            )
        )

    one_state = (
        jnp.full((heads_here, seq_rows), -1e30, jnp.float32),
        jnp.zeros((heads_here, seq_rows), jnp.float32),
        jnp.zeros((heads_here, seq_rows, HEAD_DIM), jnp.float32),
    )
    initial = tuple((one_state for g in range(group_count)))
    running = initial
    key_piece = lax.all_gather(key_heads, "seq", axis=1, tiled=True)
    value_piece = lax.all_gather(value_heads, "seq", axis=1, tiled=True)
    piece_rows = key_piece.shape[1]
    block_rows = 512
    block_count = piece_rows // block_rows
    key_blocks = key_piece.reshape(heads_here, block_count, block_rows, HEAD_DIM).transpose(
        1, 0, 2, 3
    )
    value_blocks = value_piece.reshape(heads_here, block_count, block_rows, HEAD_DIM).transpose(
        1, 0, 2, 3
    )

    def advance(current, element):
        key_block, value_block, position = element
        return (attend(current, key_block, value_block, position * block_rows), None)

    running, _ = lax.scan(
        advance, running, (key_blocks, value_blocks, lax.iota(jnp.int32, block_count))
    )
    outputs = [state[2] / state[1][:, :, None] for state in running]
    result = outputs[0]
    attended_rows = result.transpose(1, 0, 2).reshape(seq_rows, local_width).astype(jnp.bfloat16)
    return attended_rows


def block_tables(block):
    angle = np.pi / block * (np.arange(block) + 0.5)
    turns = angle[:, None] * np.arange(block)[None]
    ahead = np.concatenate([np.cos(turns), -np.sin(turns)], axis=0)
    back = np.concatenate([np.cos(turns.T), -np.sin(turns.T)], axis=1) / block

    def pair(table):
        high = table.astype(ml_dtypes.bfloat16)
        rest = (table - high.astype(np.float64)).astype(ml_dtypes.bfloat16)
        return np.concatenate([high, rest], axis=0)

    return pair(ahead), pair(back)


def two_parts(value):
    high = value.astype(jnp.bfloat16)
    return high, (value - high.astype(jnp.float32)).astype(jnp.bfloat16)


def mxu(left, right):
    return jnp.dot(left, right, preferred_element_type=jnp.float32)


def folded_sum(stacked):
    half = stacked.shape[0] // 2
    return stacked[:half] + stacked[half:]


def wide_mxu(table, value):
    half = table.shape[0] // 2
    wide = jnp.concatenate([table[:half], table[half:]], axis=1)
    return mxu(wide, jnp.concatenate([value, value], axis=0))


def to_blocks(back, spectra, block):
    parts = [two_parts(jnp.concatenate(spec, axis=0)) for spec in spectra]
    main = [mxu(back, high) for high, _ in parts]
    small = [mxu(back[:block], rest) for _, rest in parts]
    return [folded_sum(large) + rest for large, rest in zip(main, small)]


def pack_kernel(*rest, parts, width):
    outs, sem = rest[-len(parts) - 1 : -1], rest[-1]
    here, group = lax.axis_index("seq"), lax.axis_index("groups")
    copies = []
    for (step, columns, blocks), out in zip(parts, outs):
        for n, (i, slot) in enumerate(blocks):
            start = (here ^ step) * width + (group if slot is None else slot) * columns
            source = rest[i].at[:, pl.ds(pl.multiple_of(start, HEAD_DIM), columns)]
            rows = source.shape[0]
            copies.append(
                pltpu.make_async_copy(
                    source, out.at[n * rows : (n + 1) * rows], sem.at[len(copies)]
                )
            )
    for copy in copies:
        copy.start()
    for copy in copies:
        copy.wait()


def own_columns(ref, here, width):
    return ref[:, pl.ds(pl.multiple_of(here * width, width), width)]


def with_block_before(spec, before, block):
    odd = lax.broadcasted_iota(jnp.int32, (block, spec.shape[1]), 0) % 2
    sign = 1.0 - 2.0 * odd.astype(jnp.float32)
    return spec[:block] - sign * before[block:], spec[block:] + sign * before[:block]


def local_kernel(gate_ref, filter_ref, near_ref, taps_ref, ahead_ref, *outs, block):
    gate_spec_ref, filter_spec_ref, taps_spec_ref = outs
    here = lax.axis_index("seq")
    width = near_ref.shape[1]
    ahead = ahead_ref[...]
    gate_spec_ref[0] = wide_mxu(ahead, own_columns(gate_ref, here, width))
    gate_spec_ref[1] = wide_mxu(ahead, near_ref[:block])
    filter_spec_ref[0] = wide_mxu(ahead, own_columns(filter_ref, here, width))
    filter_spec_ref[1] = wide_mxu(ahead, near_ref[2 * block : 3 * block])
    turned = (((1,), (1,)), ((), ()))
    taps = taps_ref[pl.ds(pl.multiple_of(here * width, width), width)]
    taps_high, taps_rest = two_parts(taps)
    taps_spec_ref[...] = folded_sum(
        lax.dot_general(ahead, taps_high, turned, preferred_element_type=jnp.float32)
    ) + lax.dot_general(
        ahead[: 2 * block], taps_rest, turned, preferred_element_type=jnp.float32
    )


def smooth_kernel(gate_spec_ref, taps_spec_ref, value_ref, near_ref, *rest, count, block):
    arrived = rest[: count - 2]
    ahead_ref, back_ref, line_ref, gate_all, value_all = rest[count - 2 :]
    here = lax.axis_index("seq")
    width = near_ref.shape[1]
    ahead = ahead_ref[...]
    back = back_ref[...]
    value_all[here] = own_columns(value_ref, here, width)
    value_all[here ^ 1] = near_ref[block : 2 * block]
    gate_all[here] = gate_spec_ref[0]
    gate_all[here ^ 1] = gate_spec_ref[1]
    for step, piece in enumerate(arrived, 2):
        columns = piece.shape[1]
        slots = width // columns

        def joined(first):
            return jnp.concatenate(
                [piece[n * block : (n + 1) * block] for n in range(first, first + slots)], axis=1
            )

        gate_all[here ^ step] = wide_mxu(ahead, joined(0))
        value_all[here ^ step] = joined(slots)
    taps_re, taps_im = taps_spec_ref[:block], taps_spec_ref[block:]
    spectra = []
    for b in range(count):
        gate_spec = gate_all[b]
        if b > 0:
            gate_re, gate_im = with_block_before(gate_spec, gate_all[b - 1], block)
        else:
            gate_re, gate_im = gate_spec[:block], gate_spec[block:]
        spectra.append(
            (gate_re * taps_re - gate_im * taps_im, gate_re * taps_im + gate_im * taps_re)
        )
    mixed = [
        (smoothed * value_all[b].astype(jnp.float32)).astype(jnp.bfloat16)
        for b, smoothed in enumerate(to_blocks(back, spectra, block))
    ]
    for b in range(count):
        line_ref[b] = wide_mxu(ahead, mixed[b])


def share_start(shift, columns, groups):
    group = lax.axis_index("groups") if groups > 1 else 0
    return pl.multiple_of(lax.rem(group + groups - shift, groups) * columns, HEAD_DIM)


def conv_kernel(line_ref, filter_spec_ref, *rest, count, groups, shift, block, head_dim):
    far = count - 2
    arrived = rest[:far]
    weight_ref, ahead_ref, back_ref, query_ref, spec_all = rest[far:]
    here = lax.axis_index("seq")
    width = line_ref.shape[2]
    columns = width // groups
    start = share_start(shift, columns, groups)
    chosen = pl.ds(start, columns)
    ahead = ahead_ref[...]
    back = back_ref[...]
    first_head = here * (width // head_dim) + start // head_dim
    spec_all[here] = filter_spec_ref[0, :, chosen]
    spec_all[here ^ 1] = filter_spec_ref[1, :, chosen]
    for step, piece in enumerate(arrived, 2):
        spec_all[here ^ step] = wide_mxu(ahead, piece[piece.shape[0] - block :])
    lines = [(line_ref[b, :block, chosen], line_ref[b, block:, chosen]) for b in range(count)]
    kernels = [(spec_all[0, :block], spec_all[0, block:])] + [
        with_block_before(spec_all[b], spec_all[b - 1], block) for b in range(1, count)
    ]
    totals = []
    for b in range(count):
        total_re, total_im = 0.0, 0.0
        for j in range(b + 1):
            line_re, line_im = lines[j]
            kernel_re, kernel_im = kernels[b - j]
            total_re = total_re + (line_re * kernel_re - line_im * kernel_im)
            total_im = total_im + (line_re * kernel_im + line_im * kernel_re)
        totals.append((total_re, total_im))
    for b, conv_out in enumerate(to_blocks(back, totals, block)):
        conv_out = conv_out.astype(jnp.bfloat16)
        for h in range(columns // head_dim):
            part = slice(h * head_dim, (h + 1) * head_dim)
            query_ref[b, :, part] = mxu(conv_out[:, part], weight_ref[first_head + h]).astype(
                jnp.bfloat16
            )


def weigh_kernel(own_ref, near_ref, *rest, count, groups, block, head_dim):
    arrived, queries = rest[: count - 2], rest[count - 2 : count - 2 + groups]
    weight_ref, part_ref, key_all = rest[count - 2 + groups :]
    here = lax.axis_index("seq")
    key_all[here] = own_columns(own_ref, here, near_ref.shape[1])
    for step, piece in enumerate((near_ref, *arrived), 1):
        first = max(piece.shape[0] - 2 * block, 0)
        key_all[here ^ step] = piece[first : first + block]
    turned = (((1,), (1,)), ((), ()))
    scale = math.log2(math.e) / math.sqrt(head_dim)
    row = lax.broadcasted_iota(jnp.int32, (block, block), 0)
    column = lax.broadcasted_iota(jnp.int32, (block, block), 1)
    allowed = column <= row
    share = queries[0].shape[2]
    heads = share // head_dim
    places = [(h, b) for h in range(groups * heads) for b in range(count)]
    scores = {place: [] for place in places}
    for h in range(groups * heads):
        shift, part = divmod(h, heads)
        query = jnp.concatenate(
            [queries[shift][b, :, part * head_dim : (part + 1) * head_dim] for b in range(count)],
            axis=0,
        )
        columns = pl.ds(share_start(shift, share, groups) + part * head_dim, head_dim)
        for j in range(count):
            later = lax.dot_general(
                query[j * block :],
                key_all[j, :, columns],
                turned,
                preferred_element_type=jnp.float32,
            )
            for b in range(j, count):
                score = later[(b - j) * block : (b - j + 1) * block]
                scores[h, b].append(jnp.where(allowed, score, -1e30) if j == b else score)
    peaks = {
        place: jnp.max(functools.reduce(jnp.maximum, parts), axis=1, keepdims=True)
        for place, parts in scores.items()
    }
    sums = {}
    for h, b in places:
        weights = [jnp.exp2((score - peaks[h, b]) * scale) for score in scores[h, b]]
        weights[b] = jnp.where(allowed, weights[b], 0.0)
        sums[h, b] = jnp.sum(functools.reduce(jnp.add, weights), axis=1, keepdims=True)
        for j in range(b + 1):
            weight_ref[h, b, :, j * block : (j + 1) * block] = weights[j].astype(jnp.bfloat16)
    for h, b in places:
        part_ref[h, b] = jnp.broadcast_to(1.0 / sums[h, b], (block, head_dim))


def sum_kernel(weight_ref, part_ref, own_ref, near_ref, *rest, count, groups, block, head_dim):
    arrived = rest[: count - 2]
    outs = rest[count - 2 : 2 * count - 2]
    value_all, out_all = rest[2 * count - 2 :]
    here = lax.axis_index("seq")

    def rows_of(b):
        return pl.ds(pl.multiple_of(b * block, block), block)

    value_all[rows_of(here)] = own_columns(own_ref, here, near_ref.shape[1])
    for step, piece in enumerate((near_ref, *arrived), 1):
        value_all[rows_of(here ^ step)] = piece[-block:]
    share = value_all.shape[1] // groups
    totals = []
    for h in range(weight_ref.shape[0]):
        shift, part = divmod(h, share // head_dim)
        columns = pl.ds(share_start(shift, share, groups) + part * head_dim, head_dim)
        for b in range(count):
            seen = (b + 1) * block
            total = mxu(weight_ref[h, b, :, :seen], value_all[:seen, columns])
            totals.append((h, b, columns, total))
    for h, b, columns, total in totals:
        out_all[b, :, columns] = (total * part_ref[h, b]).astype(jnp.bfloat16)
    for step, out in enumerate(outs):
        out[...] = out_all[here ^ step]


def join_kernel(*rest, steps, width):
    pieces, out_ref, sem = rest[: len(steps)], rest[-2], rest[-1]
    here = lax.axis_index("seq")
    copies = []
    for n, (step, piece) in enumerate(zip(steps, pieces)):
        columns = pl.ds(pl.multiple_of((here ^ step) * width, width), width)
        copies.append(pltpu.make_async_copy(piece, out_ref.at[:, columns], sem.at[n]))
    for copy in copies:
        copy.start()
    for copy in copies:
        copy.wait()


WHOLE = pl.BlockSpec(memory_space=pltpu.VMEM)


def head_shards(
    gate_input, value_input, short_filter, long_filter, query_weight, key_matrix, value_matrix
):
    count = lax.axis_size("seq")
    block, local_width = gate_input.shape
    width = local_width // count
    heads = width // HEAD_DIM
    here = lax.axis_index("seq")
    groups = lax.axis_size("groups") if heads % lax.axis_size("groups") == 0 else 1

    def swap(value, step):
        return lax.ppermute(value, "seq", [(i, i ^ step) for i in range(count)])

    def packed(arrays, parts, after=()):
        return pl.pallas_call(
            functools.partial(pack_kernel, parts=parts, width=width),
            out_shape=[
                pltpu.VMEM((len(chosen) * block, columns), jnp.bfloat16)
                for _, columns, chosen in parts
            ],
            in_specs=[pl.BlockSpec(memory_space=pl.ANY)] * (len(arrays) + len(after)),
            out_specs=[WHOLE] * len(parts),
            scratch_shapes=[
                pltpu.SemaphoreType.DMA((sum(len(chosen) for *_, chosen in parts),))
            ],
            compiler_params=params,
        )(*[pltpu.with_memory_space_constraint(a, pltpu.HBM) for a in arrays], *after)

    ahead, back = block_tables(block)
    scratch = lambda n: pltpu.VMEM((n, block, width), jnp.bfloat16)
    params = pltpu.CompilerParams(vmem_limit_bytes=32 * 1024 * 1024)
    far = range(2, count)
    share = width // groups
    slots = range(groups)
    streams = [(i, slot) for i in (0, 1) for slot in slots] + [(2, None if groups > 1 else 0)]
    arrays = [gate_input, value_input, long_filter, key_matrix, value_matrix]
    first, near = packed(
        arrays, [(far[0], share, streams), (1, width, [(n, 0) for n in range(3)])]
    )
    near = swap(near, 1)
    near_later, *pieces = packed(
        arrays,
        [(1, width, [(3, 0), (4, 0)])]
        + [(step, share, streams) for step in far[1:]]
        + [(step, width, [(3, 0), (4, 0)]) for step in far[:-1]]
        + [(far[-1], width, [(n, 0)]) for n in (3, 4)],
        after=[near],
    )
    near_later = swap(near_later, 1)
    arrived = [swap(piece, step) for step, piece in zip(far, [first, *pieces])]
    later = pieces[len(far) - 1 :]
    tables = jnp.asarray(ahead), jnp.asarray(back)
    spectra = lambda n: (n, 2 * block, width)
    gate_spec, filter_spec, taps_spec = pl.pallas_call(
        functools.partial(local_kernel, block=block),
        out_shape=[
            jax.ShapeDtypeStruct(spectra(2), jnp.float32),
            jax.ShapeDtypeStruct(spectra(2), jnp.float32),
            jax.ShapeDtypeStruct((2 * block, width), jnp.float32),
        ],
        in_specs=[WHOLE] * 5,
        out_specs=[WHOLE] * 3,
        compiler_params=params,
    )(gate_input, long_filter, near, short_filter, tables[0])
    filters = [piece[-block:] for piece in arrived]
    filters[0], taps_spec, near_later = lax.optimization_barrier(
        (filters[0], taps_spec, near_later)
    )
    shares = [arrived] + [
        [
            lax.ppermute(piece, "groups", [(i, (i + shift) % groups) for i in range(groups)])
            for piece in filters
        ]
        for shift in range(1, groups)
    ]
    later = [swap(piece, step) for step, piece in zip([*far, far[-1]], later)]
    arrived_keys, arrived_values = later[:-1], [*later[:-2], later[-1]]
    lines = pl.pallas_call(
        functools.partial(smooth_kernel, count=count, block=block),
        out_shape=jax.ShapeDtypeStruct(spectra(count), jnp.float32),
        in_specs=[WHOLE] * (count + 4),
        out_specs=WHOLE,
        scratch_shapes=[pltpu.VMEM(spectra(count), jnp.float32), scratch(count)],
        compiler_params=params,
    )(gate_spec, taps_spec, value_input, near, *arrived, *tables)
    queries = [
        pl.pallas_call(
            functools.partial(
                conv_kernel,
                count=count,
                groups=groups,
                shift=shift,
                block=block,
                head_dim=HEAD_DIM,
            ),
            out_shape=jax.ShapeDtypeStruct((count, block, share), jnp.bfloat16),
            in_specs=[WHOLE] * (len(far) + 5),
            out_specs=WHOLE,
            scratch_shapes=[pltpu.VMEM((count, 2 * block, share), jnp.float32)],
            compiler_params=params,
        )(lines, filter_spec, *pieces, query_weight, *tables)
        for shift, pieces in enumerate(shares)
    ]
    weights, parts = pl.pallas_call(
        functools.partial(
            weigh_kernel, count=count, groups=groups, block=block, head_dim=HEAD_DIM
        ),
        out_shape=[
            jax.ShapeDtypeStruct((heads, count, block, count * block), jnp.bfloat16),
            jax.ShapeDtypeStruct((heads, count, block, HEAD_DIM), jnp.float32),
        ],
        in_specs=[WHOLE] * (count + groups),
        out_specs=[WHOLE] * 2,
        scratch_shapes=[scratch(count)],
        compiler_params=params,
    )(key_matrix, near_later, *arrived_keys, *queries)
    pieces = pl.pallas_call(
        functools.partial(
            sum_kernel, count=count, groups=groups, block=block, head_dim=HEAD_DIM
        ),
        out_shape=[jax.ShapeDtypeStruct((block, width), jnp.bfloat16)] * count,
        in_specs=[WHOLE] * (count + 2),
        out_specs=[WHOLE] * count,
        scratch_shapes=[
            pltpu.VMEM((count * block, width), jnp.bfloat16),
            scratch(count),
        ],
        compiler_params=params,
    )(weights, parts, value_matrix, near_later, *arrived_values)
    swapped = {step: swap(pieces[step], step) for step in [*far, 1]}
    pieces = [pieces[0]] + [swapped[step] for step in range(1, count)]

    def joined(steps, *before):
        return pl.pallas_call(
            functools.partial(join_kernel, steps=steps, width=width),
            out_shape=pltpu.HBM((block, local_width), jnp.bfloat16),
            in_specs=[WHOLE] * len(steps) + [pl.BlockSpec(memory_space=pl.ANY)] * len(before),
            out_specs=pl.BlockSpec(memory_space=pl.ANY),
            scratch_shapes=[pltpu.SemaphoreType.DMA((len(steps),))],
            input_output_aliases={len(steps): 0} if before else {},
            compiler_params=params,
        )(*[pieces[step] for step in steps], *before)

    result = joined((0, 1))
    for step in far:
        result = joined((step,), result)
    return result


def shards(*arrays):
    count = lax.axis_size("seq")
    block, local_width = arrays[0].shape
    even = local_width % (count * HEAD_DIM) == 0
    if even and count > 3 and count & (count - 1) == 0 and block == TAPS:
        return head_shards(*arrays)
    return general_shards(*arrays)


def solution(mesh):
    in_specs = (
        P(("groups", "seq"), "chan"),
        P(("groups", "seq"), "chan"),
        P("chan", None),
        P("seq", "chan"),
        P("chan", None, None),
        P(("groups", "seq"), "chan"),
        P(("groups", "seq"), "chan"),
    )
    out_specs = P(("groups", "seq"), "chan")
    return jax.shard_map(shards, mesh=mesh, in_specs=in_specs, out_specs=out_specs, check_vma=False)
```

```python
import functools
import math

import jax
import jax.numpy as jnp
import ml_dtypes
import numpy as np
from jax import lax
from jax.experimental import pallas as pl
from jax.experimental.pallas import tpu as pltpu
from jax.sharding import PartitionSpec as P

HEAD_DIM = 128
TAPS = 128
RADIX = 128


HIGHEST = lax.Precision.HIGHEST


def shifted(value, axis, steps):
    count = lax.axis_size(axis)
    initial, last = (max(0, -steps), min(count, count - steps))
    return lax.ppermute(value, axis, [(source, source + steps) for source in range(initial, last)])


def unit_table(height, breadth, modulus, orient):
    product = (
        lax.broadcasted_iota(jnp.int32, (height, breadth), 0)
        * lax.broadcasted_iota(jnp.int32, (height, breadth), 1)
        % modulus
    )
    angles = 2.0 * math.pi / modulus * product.astype(jnp.float32)
    return (jnp.cos(angles), orient * jnp.sin(angles))


def block_table(factor, orient):
    inner_re, inner_im = unit_table(factor, factor, factor, orient)
    upper = jnp.concatenate([inner_re, inner_im], axis=1)
    lower = jnp.concatenate([-inner_im, inner_re], axis=1)
    return jnp.concatenate([upper, lower], axis=0)


def spectrum(signal, factor):
    channels, length = signal.shape
    full_length = 2 * length
    column_count = full_length // factor
    folded = signal.reshape(channels, column_count // 2, factor)
    outer_re, outer_im = unit_table(column_count, column_count // 2, column_count, -1.0)
    outer_both = jnp.concatenate([outer_re, outer_im], axis=0)
    first = jnp.einsum("kn,cnm->ckm", outer_both, folded, precision=HIGHEST)
    first_re = first[:, :column_count]
    first_im = first[:, column_count:]
    twist_re, twist_im = unit_table(column_count, factor, full_length, -1.0)
    mid_re = first_re * twist_re - first_im * twist_im
    mid_im = first_re * twist_im + first_im * twist_re
    joined = jnp.concatenate([mid_re, mid_im], axis=2)
    return jnp.einsum("ckn,nm->ckm", joined, block_table(factor, -1.0), precision=HIGHEST)


def inverse(spec_both, factor, length):
    channels = spec_both.shape[0]
    full_length = 2 * length
    column_count = full_length // factor
    mid = jnp.einsum("ckm,mn->ckn", spec_both, block_table(factor, 1.0), precision=HIGHEST)
    mid_re = mid[:, :, :factor]
    mid_im = mid[:, :, factor:]
    twist_re, twist_im = unit_table(column_count, factor, full_length, 1.0)
    turn_re = mid_re * twist_re - mid_im * twist_im
    turn_im = mid_re * twist_im + mid_im * twist_re
    outer_re, outer_im = unit_table(column_count // 2, column_count, column_count, 1.0)
    outer_both = jnp.concatenate([outer_re, -outer_im], axis=1)
    turned = jnp.concatenate([turn_re, turn_im], axis=1)
    result = jnp.einsum("nk,ckm->cnm", outer_both, turned, precision=HIGHEST)
    return result.reshape(channels, length) / full_length


def general_shards(
    gate_input, value_input, short_filter, long_filter, query_weight, key_matrix, value_matrix
):
    seq_rows, local_width = gate_input.shape
    last_rows = gate_input[seq_rows - (TAPS - 1) :]
    earlier = shifted(last_rows, "seq", 1)
    padded = jnp.concatenate([earlier, gate_input], axis=0).astype(jnp.float32)
    kernel = short_filter[:, ::-1].T[:, None, :]
    smoothed = lax.conv_general_dilated(
        padded[None],
        kernel,
        (1,),
        "VALID",
        dimension_numbers=("NHC", "HIO", "NHC"),
        feature_group_count=local_width,
        precision=HIGHEST,
    )[0]
    mixed_input = (smoothed * value_input.astype(jnp.float32)).astype(jnp.bfloat16)
    signal, kernel_line = (
        lax.all_to_all(mixed_input.T, "seq", split_axis=0, concat_axis=1, tiled=True),
        lax.all_to_all(long_filter.T, "seq", split_axis=0, concat_axis=1, tiled=True),
    )
    length = signal.shape[1]
    signal_both = spectrum(signal.astype(jnp.float32), RADIX)
    kernel_both = spectrum(kernel_line.astype(jnp.float32), RADIX)
    signal_re = signal_both[:, :, :RADIX]
    signal_im = signal_both[:, :, RADIX:]
    kernel_re = kernel_both[:, :, :RADIX]
    kernel_im = kernel_both[:, :, RADIX:]
    joint = jnp.concatenate(
        [
            signal_re * kernel_re - signal_im * kernel_im,
            signal_re * kernel_im + signal_im * kernel_re,
        ],
        axis=2,
    )
    conv_line = inverse(joint, RADIX, length).astype(jnp.bfloat16)
    my_index = lax.axis_index("seq")
    group_firsts = [my_index * seq_rows]
    conv_columns = lax.all_to_all(conv_line, "seq", split_axis=1, concat_axis=0, tiled=True)
    heads_here = local_width // HEAD_DIM
    conv_heads = conv_columns.reshape(heads_here, HEAD_DIM, seq_rows)
    query_heads = jnp.einsum(
        "hds,hde->hse", conv_heads, query_weight, preferred_element_type=jnp.float32
    ).astype(jnp.bfloat16)
    group_count = len(group_firsts)
    query_groups = [query_heads]
    key_heads = key_matrix.reshape(seq_rows, heads_here, HEAD_DIM).transpose(1, 0, 2)
    value_heads = value_matrix.reshape(seq_rows, heads_here, HEAD_DIM).transpose(1, 0, 2)
    score_scale = 1.0 / math.sqrt(HEAD_DIM)

    def attend_group(running, group_query, group_first, key_block, value_block, first_row):
        block_rows = key_block.shape[1]

        def compute(current):
            peak_value, weight_sum, weighted = current
            scores = (
                jnp.einsum(
                    "hqd,hkd->hqk", group_query, key_block, preferred_element_type=jnp.float32
                )
                * score_scale
            )
            key_pos = first_row + lax.iota(jnp.int32, block_rows)
            query_pos = group_first + lax.iota(jnp.int32, seq_rows)
            allowed = (key_pos[None, :] <= query_pos[:, None])[None]
            scores = jnp.where(allowed, scores, -1e30)
            new_peak = jnp.maximum(peak_value, jnp.max(scores, axis=2))
            weights = jnp.where(allowed, jnp.exp(scores - new_peak[:, :, None]), 0.0)
            rescale = jnp.exp(peak_value - new_peak)
            weight_sum = weight_sum * rescale + jnp.sum(weights, axis=2)
            weighted = weighted * rescale[:, :, None] + jnp.einsum(
                "hqk,hkd->hqd",
                weights.astype(jnp.bfloat16),
                value_block,
                preferred_element_type=jnp.float32,
            )
            return (new_peak, weight_sum, weighted)

        live = first_row <= group_first + seq_rows - 1
        return lax.cond(live, compute, lambda current: current, running)

    def attend(states, key_block, value_block, first_row):
        return tuple(
            (
                attend_group(
                    states[g], query_groups[g], group_firsts[g], key_block, value_block, first_row
                )
                for g in range(group_count)
            )
        )

    one_state = (
        jnp.full((heads_here, seq_rows), -1e30, jnp.float32),
        jnp.zeros((heads_here, seq_rows), jnp.float32),
        jnp.zeros((heads_here, seq_rows, HEAD_DIM), jnp.float32),
    )
    initial = tuple((one_state for g in range(group_count)))
    running = initial
    key_piece = lax.all_gather(key_heads, "seq", axis=1, tiled=True)
    value_piece = lax.all_gather(value_heads, "seq", axis=1, tiled=True)
    piece_rows = key_piece.shape[1]
    block_rows = 512
    block_count = piece_rows // block_rows
    key_blocks = key_piece.reshape(heads_here, block_count, block_rows, HEAD_DIM).transpose(
        1, 0, 2, 3
    )
    value_blocks = value_piece.reshape(heads_here, block_count, block_rows, HEAD_DIM).transpose(
        1, 0, 2, 3
    )

    def advance(current, element):
        key_block, value_block, position = element
        return (attend(current, key_block, value_block, position * block_rows), None)

    running, _ = lax.scan(
        advance, running, (key_blocks, value_blocks, lax.iota(jnp.int32, block_count))
    )
    outputs = [state[2] / state[1][:, :, None] for state in running]
    result = outputs[0]
    attended_rows = result.transpose(1, 0, 2).reshape(seq_rows, local_width).astype(jnp.bfloat16)
    return attended_rows


def block_tables(block):
    angle = np.pi / block * (np.arange(block) + 0.5)
    turns = angle[:, None] * np.arange(block)[None]
    ahead = np.concatenate([np.cos(turns), -np.sin(turns)], axis=0)
    back = np.concatenate([np.cos(turns.T), -np.sin(turns.T)], axis=1) / block

    def pair(table):
        high = table.astype(ml_dtypes.bfloat16)
        rest = (table - high.astype(np.float64)).astype(ml_dtypes.bfloat16)
        return np.concatenate([high, rest], axis=0)

    return pair(ahead), pair(back)


def two_parts(value):
    high = value.astype(jnp.bfloat16)
    return high, (value - high.astype(jnp.float32)).astype(jnp.bfloat16)


def mxu(left, right):
    return jnp.dot(left, right, preferred_element_type=jnp.float32)


def folded_sum(stacked):
    half = stacked.shape[0] // 2
    return stacked[:half] + stacked[half:]


def wide_mxu(table, value):
    half = table.shape[0] // 2
    wide = jnp.concatenate([table[:half], table[half:]], axis=1)
    return mxu(wide, jnp.concatenate([value, value], axis=0))


def to_blocks(back, spectra, block):
    parts = [two_parts(jnp.concatenate(spec, axis=0)) for spec in spectra]
    main = [mxu(back, high) for high, _ in parts]
    small = [mxu(back[:block], rest) for _, rest in parts]
    return [folded_sum(large) + rest for large, rest in zip(main, small)]


def pack_kernel(*rest, parts, width):
    outs, sem = rest[-len(parts) - 1 : -1], rest[-1]
    here, group = lax.axis_index("seq"), lax.axis_index("groups")
    copies = []
    for (step, columns, blocks), out in zip(parts, outs):
        for n, (i, slot) in enumerate(blocks):
            start = (here ^ step) * width + (group if slot is None else slot) * columns
            source = rest[i].at[:, pl.ds(pl.multiple_of(start, HEAD_DIM), columns)]
            rows = source.shape[0]
            copies.append(
                pltpu.make_async_copy(
                    source, out.at[n * rows : (n + 1) * rows], sem.at[len(copies)]
                )
            )
    for copy in copies:
        copy.start()
    for copy in copies:
        copy.wait()


def own_columns(ref, here, width):
    return ref[:, pl.ds(pl.multiple_of(here * width, width), width)]


def with_block_before(spec, before, block):
    odd = lax.broadcasted_iota(jnp.int32, (block, spec.shape[1]), 0) % 2
    sign = 1.0 - 2.0 * odd.astype(jnp.float32)
    return spec[:block] - sign * before[block:], spec[block:] + sign * before[:block]


def local_kernel(gate_ref, filter_ref, near_ref, taps_ref, ahead_ref, *outs, block):
    gate_spec_ref, filter_spec_ref, taps_spec_ref = outs
    here = lax.axis_index("seq")
    width = near_ref.shape[1]
    ahead = ahead_ref[...]
    gate_spec_ref[0] = wide_mxu(ahead, own_columns(gate_ref, here, width))
    gate_spec_ref[1] = wide_mxu(ahead, near_ref[:block])
    filter_spec_ref[0] = wide_mxu(ahead, own_columns(filter_ref, here, width))
    filter_spec_ref[1] = wide_mxu(ahead, near_ref[2 * block : 3 * block])
    turned = (((1,), (1,)), ((), ()))
    taps = taps_ref[pl.ds(pl.multiple_of(here * width, width), width)]
    taps_high, taps_rest = two_parts(taps)
    taps_spec_ref[...] = folded_sum(
        lax.dot_general(ahead, taps_high, turned, preferred_element_type=jnp.float32)
    ) + lax.dot_general(
        ahead[: 2 * block], taps_rest, turned, preferred_element_type=jnp.float32
    )


def smooth_kernel(gate_spec_ref, taps_spec_ref, value_ref, near_ref, *rest, count, block):
    arrived = rest[: count - 2]
    ahead_ref, back_ref, line_ref, gate_all, value_all = rest[count - 2 :]
    here = lax.axis_index("seq")
    width = near_ref.shape[1]
    ahead = ahead_ref[...]
    back = back_ref[...]
    value_all[here] = own_columns(value_ref, here, width)
    value_all[here ^ 1] = near_ref[block : 2 * block]
    gate_all[here] = gate_spec_ref[0]
    gate_all[here ^ 1] = gate_spec_ref[1]
    for step, piece in enumerate(arrived, 2):
        columns = piece.shape[1]
        slots = width // columns

        def joined(first):
            return jnp.concatenate(
                [piece[n * block : (n + 1) * block] for n in range(first, first + slots)], axis=1
            )

        gate_all[here ^ step] = wide_mxu(ahead, joined(0))
        value_all[here ^ step] = joined(slots)
    taps_re, taps_im = taps_spec_ref[:block], taps_spec_ref[block:]
    spectra = []
    for b in range(count):
        gate_spec = gate_all[b]
        if b > 0:
            gate_re, gate_im = with_block_before(gate_spec, gate_all[b - 1], block)
        else:
            gate_re, gate_im = gate_spec[:block], gate_spec[block:]
        spectra.append(
            (gate_re * taps_re - gate_im * taps_im, gate_re * taps_im + gate_im * taps_re)
        )
    mixed = [
        (smoothed * value_all[b].astype(jnp.float32)).astype(jnp.bfloat16)
        for b, smoothed in enumerate(to_blocks(back, spectra, block))
    ]
    lines = [wide_mxu(ahead, part) for part in mixed]
    line_ref[0] = lines[0]
    for b in range(1, count):
        window_re, window_im = with_block_before(lines[b], lines[b - 1], block)
        line_ref[b, :block] = window_re
        line_ref[b, block:] = window_im


def share_start(shift, columns, groups):
    group = lax.axis_index("groups") if groups > 1 else 0
    return pl.multiple_of(lax.rem(group + groups - shift, groups) * columns, HEAD_DIM)


def conv_kernel(line_ref, filter_spec_ref, *rest, count, groups, shift, block, head_dim):
    far = count - 2
    arrived = rest[:far]
    weight_ref, ahead_ref, back_ref, query_ref, spec_all = rest[far:]
    here = lax.axis_index("seq")
    width = line_ref.shape[2]
    columns = width // groups
    start = share_start(shift, columns, groups)
    chosen = pl.ds(start, columns)
    ahead = ahead_ref[...]
    back = back_ref[...]
    first_head = here * (width // head_dim) + start // head_dim
    spec_all[here] = filter_spec_ref[0, :, chosen]
    spec_all[here ^ 1] = filter_spec_ref[1, :, chosen]
    for step, piece in enumerate(arrived, 2):
        spec_all[here ^ step] = wide_mxu(ahead, piece[piece.shape[0] - block :])
    lines = [(line_ref[b, :block, chosen], line_ref[b, block:, chosen]) for b in range(count)]
    kernels = [(spec_all[b, :block], spec_all[b, block:]) for b in range(count)]
    totals = []
    for b in range(count):
        total_re, total_im = 0.0, 0.0
        for j in range(b + 1):
            line_re, line_im = lines[j]
            kernel_re, kernel_im = kernels[b - j]
            total_re = total_re + (line_re * kernel_re - line_im * kernel_im)
            total_im = total_im + (line_re * kernel_im + line_im * kernel_re)
        totals.append((total_re, total_im))
    for b, conv_out in enumerate(to_blocks(back, totals, block)):
        conv_out = conv_out.astype(jnp.bfloat16)
        for h in range(columns // head_dim):
            part = slice(h * head_dim, (h + 1) * head_dim)
            query_ref[b, :, part] = mxu(conv_out[:, part], weight_ref[first_head + h]).astype(
                jnp.bfloat16
            )


def weigh_kernel(own_ref, near_ref, *rest, count, groups, block, head_dim):
    arrived, queries = rest[: count - 2], rest[count - 2 : count - 2 + groups]
    weight_ref, part_ref, key_all = rest[count - 2 + groups :]
    here = lax.axis_index("seq")
    key_all[here] = own_columns(own_ref, here, near_ref.shape[1])
    for step, piece in enumerate((near_ref, *arrived), 1):
        first = max(piece.shape[0] - 2 * block, 0)
        key_all[here ^ step] = piece[first : first + block]
    turned = (((1,), (1,)), ((), ()))
    scale = math.log2(math.e) / math.sqrt(head_dim)
    row = lax.broadcasted_iota(jnp.int32, (block, block), 0)
    column = lax.broadcasted_iota(jnp.int32, (block, block), 1)
    allowed = column <= row
    share = queries[0].shape[2]
    heads = share // head_dim
    places = [(h, b) for h in range(groups * heads) for b in range(count)]
    scores = {place: [] for place in places}
    for h in range(groups * heads):
        shift, part = divmod(h, heads)
        query = jnp.concatenate(
            [queries[shift][b, :, part * head_dim : (part + 1) * head_dim] for b in range(count)],
            axis=0,
        )
        columns = pl.ds(share_start(shift, share, groups) + part * head_dim, head_dim)
        for j in range(count):
            later = lax.dot_general(
                query[j * block :],
                key_all[j, :, columns],
                turned,
                preferred_element_type=jnp.float32,
            )
            for b in range(j, count):
                score = later[(b - j) * block : (b - j + 1) * block]
                scores[h, b].append(jnp.where(allowed, score, -1e30) if j == b else score)
    peaks = {
        place: jnp.max(functools.reduce(jnp.maximum, parts), axis=1, keepdims=True)
        for place, parts in scores.items()
    }
    sums = {}
    for h, b in places:
        weights = [jnp.exp2((score - peaks[h, b]) * scale) for score in scores[h, b]]
        weights[b] = jnp.where(allowed, weights[b], 0.0)
        sums[h, b] = jnp.sum(functools.reduce(jnp.add, weights), axis=1, keepdims=True)
        for j in range(b + 1):
            weight_ref[h, b, :, j * block : (j + 1) * block] = weights[j].astype(jnp.bfloat16)
    for h, b in places:
        part_ref[h, b] = jnp.broadcast_to(1.0 / sums[h, b], (block, head_dim))


def sum_kernel(weight_ref, part_ref, own_ref, near_ref, *rest, count, groups, block, head_dim):
    arrived = rest[: count - 2]
    outs = rest[count - 2 : 2 * count - 2]
    value_all, out_all = rest[2 * count - 2 :]
    here = lax.axis_index("seq")

    def rows_of(b):
        return pl.ds(pl.multiple_of(b * block, block), block)

    value_all[rows_of(here)] = own_columns(own_ref, here, near_ref.shape[1])
    for step, piece in enumerate((near_ref, *arrived), 1):
        value_all[rows_of(here ^ step)] = piece[-block:]
    share = value_all.shape[1] // groups
    totals = []
    for h in range(weight_ref.shape[0]):
        shift, part = divmod(h, share // head_dim)
        columns = pl.ds(share_start(shift, share, groups) + part * head_dim, head_dim)
        for b in range(count):
            seen = (b + 1) * block
            total = mxu(weight_ref[h, b, :, :seen], value_all[:seen, columns])
            totals.append((h, b, columns, total))
    for h, b, columns, total in totals:
        out_all[b, :, columns] = (total * part_ref[h, b]).astype(jnp.bfloat16)
    for step, out in enumerate(outs):
        out[...] = out_all[here ^ step]


def join_kernel(*rest, steps, width):
    pieces, out_ref, sem = rest[: len(steps)], rest[-2], rest[-1]
    here = lax.axis_index("seq")
    copies = []
    for n, (step, piece) in enumerate(zip(steps, pieces)):
        columns = pl.ds(pl.multiple_of((here ^ step) * width, width), width)
        copies.append(pltpu.make_async_copy(piece, out_ref.at[:, columns], sem.at[n]))
    for copy in copies:
        copy.start()
    for copy in copies:
        copy.wait()


WHOLE = pl.BlockSpec(memory_space=pltpu.VMEM)


def head_shards(
    gate_input, value_input, short_filter, long_filter, query_weight, key_matrix, value_matrix
):
    count = lax.axis_size("seq")
    block, local_width = gate_input.shape
    width = local_width // count
    heads = width // HEAD_DIM
    here = lax.axis_index("seq")
    groups = lax.axis_size("groups") if heads % lax.axis_size("groups") == 0 else 1

    def swap(value, step):
        return lax.ppermute(value, "seq", [(i, i ^ step) for i in range(count)])

    def packed(arrays, parts, after=()):
        return pl.pallas_call(
            functools.partial(pack_kernel, parts=parts, width=width),
            out_shape=[
                pltpu.VMEM((len(chosen) * block, columns), jnp.bfloat16)
                for _, columns, chosen in parts
            ],
            in_specs=[pl.BlockSpec(memory_space=pl.ANY)] * (len(arrays) + len(after)),
            out_specs=[WHOLE] * len(parts),
            scratch_shapes=[
                pltpu.SemaphoreType.DMA((sum(len(chosen) for *_, chosen in parts),))
            ],
            compiler_params=params,
        )(*[pltpu.with_memory_space_constraint(a, pltpu.HBM) for a in arrays], *after)

    ahead, back = block_tables(block)
    scratch = lambda n: pltpu.VMEM((n, block, width), jnp.bfloat16)
    params = pltpu.CompilerParams(vmem_limit_bytes=32 * 1024 * 1024)
    far = range(2, count)
    share = width // groups
    slots = range(groups)
    streams = [(i, slot) for i in (0, 1) for slot in slots] + [(2, None if groups > 1 else 0)]
    arrays = [gate_input, value_input, long_filter, key_matrix, value_matrix]
    first, near = packed(
        arrays, [(far[0], share, streams), (1, width, [(n, 0) for n in range(3)])]
    )
    near = swap(near, 1)
    near_later, *pieces = packed(
        arrays,
        [(1, width, [(3, 0), (4, 0)])]
        + [(step, share, streams) for step in far[1:]]
        + [(step, width, [(3, 0), (4, 0)]) for step in far[:-1]]
        + [(far[-1], width, [(n, 0)]) for n in (3, 4)],
        after=[near],
    )
    near_later = swap(near_later, 1)
    arrived = [swap(piece, step) for step, piece in zip(far, [first, *pieces])]
    later = pieces[len(far) - 1 :]
    tables = jnp.asarray(ahead), jnp.asarray(back)
    spectra = lambda n: (n, 2 * block, width)
    gate_spec, filter_spec, taps_spec = pl.pallas_call(
        functools.partial(local_kernel, block=block),
        out_shape=[
            jax.ShapeDtypeStruct(spectra(2), jnp.float32),
            jax.ShapeDtypeStruct(spectra(2), jnp.float32),
            jax.ShapeDtypeStruct((2 * block, width), jnp.float32),
        ],
        in_specs=[WHOLE] * 5,
        out_specs=[WHOLE] * 3,
        compiler_params=params,
    )(gate_input, long_filter, near, short_filter, tables[0])
    filters = [piece[-block:] for piece in arrived]
    filters[0], taps_spec, near_later = lax.optimization_barrier(
        (filters[0], taps_spec, near_later)
    )
    shares = [arrived] + [
        [
            lax.ppermute(piece, "groups", [(i, (i + shift) % groups) for i in range(groups)])
            for piece in filters
        ]
        for shift in range(1, groups)
    ]
    later = [swap(piece, step) for step, piece in zip([*far, far[-1]], later)]
    arrived_keys, arrived_values = later[:-1], [*later[:-2], later[-1]]
    lines = pl.pallas_call(
        functools.partial(smooth_kernel, count=count, block=block),
        out_shape=jax.ShapeDtypeStruct(spectra(count), jnp.float32),
        in_specs=[WHOLE] * (count + 4),
        out_specs=WHOLE,
        scratch_shapes=[pltpu.VMEM(spectra(count), jnp.float32), scratch(count)],
        compiler_params=params,
    )(gate_spec, taps_spec, value_input, near, *arrived, *tables)
    queries = [
        pl.pallas_call(
            functools.partial(
                conv_kernel,
                count=count,
                groups=groups,
                shift=shift,
                block=block,
                head_dim=HEAD_DIM,
            ),
            out_shape=jax.ShapeDtypeStruct((count, block, share), jnp.bfloat16),
            in_specs=[WHOLE] * (len(far) + 5),
            out_specs=WHOLE,
            scratch_shapes=[pltpu.VMEM((count, 2 * block, share), jnp.float32)],
            compiler_params=params,
        )(lines, filter_spec, *pieces, query_weight, *tables)
        for shift, pieces in enumerate(shares)
    ]
    weights, parts = pl.pallas_call(
        functools.partial(
            weigh_kernel, count=count, groups=groups, block=block, head_dim=HEAD_DIM
        ),
        out_shape=[
            jax.ShapeDtypeStruct((heads, count, block, count * block), jnp.bfloat16),
            jax.ShapeDtypeStruct((heads, count, block, HEAD_DIM), jnp.float32),
        ],
        in_specs=[WHOLE] * (count + groups),
        out_specs=[WHOLE] * 2,
        scratch_shapes=[scratch(count)],
        compiler_params=params,
    )(key_matrix, near_later, *arrived_keys, *queries)
    pieces = pl.pallas_call(
        functools.partial(
            sum_kernel, count=count, groups=groups, block=block, head_dim=HEAD_DIM
        ),
        out_shape=[jax.ShapeDtypeStruct((block, width), jnp.bfloat16)] * count,
        in_specs=[WHOLE] * (count + 2),
        out_specs=[WHOLE] * count,
        scratch_shapes=[
            pltpu.VMEM((count * block, width), jnp.bfloat16),
            scratch(count),
        ],
        compiler_params=params,
    )(weights, parts, value_matrix, near_later, *arrived_values)
    swapped = {step: swap(pieces[step], step) for step in [*far, 1]}
    pieces = [pieces[0]] + [swapped[step] for step in range(1, count)]

    def joined(steps, *before):
        return pl.pallas_call(
            functools.partial(join_kernel, steps=steps, width=width),
            out_shape=pltpu.HBM((block, local_width), jnp.bfloat16),
            in_specs=[WHOLE] * len(steps) + [pl.BlockSpec(memory_space=pl.ANY)] * len(before),
            out_specs=pl.BlockSpec(memory_space=pl.ANY),
            scratch_shapes=[pltpu.SemaphoreType.DMA((len(steps),))],
            input_output_aliases={len(steps): 0} if before else {},
            compiler_params=params,
        )(*[pieces[step] for step in steps], *before)

    result = joined((0, 1))
    for step in far:
        result = joined((step,), result)
    return result


def shards(*arrays):
    count = lax.axis_size("seq")
    block, local_width = arrays[0].shape
    even = local_width % (count * HEAD_DIM) == 0
    if even and count > 3 and count & (count - 1) == 0 and block == TAPS:
        return head_shards(*arrays)
    return general_shards(*arrays)


def solution(mesh):
    in_specs = (
        P(("groups", "seq"), "chan"),
        P(("groups", "seq"), "chan"),
        P("chan", None),
        P("seq", "chan"),
        P("chan", None, None),
        P(("groups", "seq"), "chan"),
        P(("groups", "seq"), "chan"),
    )
    out_specs = P(("groups", "seq"), "chan")
    return jax.shard_map(shards, mesh=mesh, in_specs=in_specs, out_specs=out_specs, check_vma=False)
```
